32 devices in a mesh: seq: 8 (over z, y), batch: 4 (over x, core).
Axes of the slice: x: 2, y: 2, z: 4, core: 2. Of those that a mesh axis runs over, the one named last changes fastest.
Arguments:
- tokens: bfloat16 [4, 2048, 1024], P('batch', 'seq'), may hold values from -6 to 6
- w_qkv: bfloat16 [1024, 3072], replicated, may hold values from -0.25 to 0.25
- w_out: bfloat16 [1024, 1024], replicated, may hold values from -0.75 to 0.75
- w_in: bfloat16 [8, 1024, 4096], P('seq'), may hold values from -0.1875 to 0.1875
- w_exp_out: bfloat16 [8, 4096, 1024], P('seq'), may hold values from -0.125 to 0.125
- gains: float32 [2, 1024], replicated, may hold values from 0.5 to 1.5
- biases: float32 [2, 1024], replicated, may hold values from -1 to 1
- lengths: int32 [4, 8], P('batch'), may hold values from 1 to 1792, as said below
- hash_ids: int32 [4, 2048, 1], P('batch', 'seq'), may hold values from 0 to 7; in each aligned block of 256 rows (0 to 255, 256 to 511, ..., all dimensions but the last counted through in order) at most 48 rows name the same one
- cotangent: bfloat16 [4, 2048, 1024], P('batch', 'seq'), may hold values from -6 to 6
Outputs:
- output: bfloat16 [4, 2048, 1024], P('batch', 'seq')
- d_tokens: float32 [4, 2048, 1024], P('batch', 'seq')
- d_w_qkv: float32 [1024, 3072], P(None, 'batch')
- d_w_out: float32 [1024, 1024], P(None, 'batch')
- d_w_in: float32 [8, 1024, 4096], P('seq', None, 'batch')
- d_w_exp_out: float32 [8, 4096, 1024], P('seq', 'batch')
- d_gains: float32 [2, 1024], P(None, 'batch')
- d_biases: float32 [2, 1024], P(None, 'batch')
The draws below stay inside these ranges and needn't reach their ends.
Inputs may be any that keep to these rules, and one draw needn't show every extreme that they name: Each row holds the 8 document lengths of one packed row in order, summing to 2048; one document is 1792 long and begins within the first 256 positions. `hash_ids`: among the 256 tokens of one device no expert is named more than 48 times.
All inputs are finite; a program needn't handle non-finite values.
Results may differ from the reference program's by a relative error of at most 0.035.
Values may be sent and summed in bfloat16 or wider, within the bound.
No kernel may reach another device: no remote copies, remote signals or barrier semaphores. Data moves between devices by JAX's collectives and lax.ppermute only.
A program may use at most 256 MiB of HBM per device.

```python
import math
import jax
import jax.numpy as jnp
import numpy as np
from jax import lax

D = 1024
HEADS = 16
HEAD_DIM = 64
FF = 4096
TOK_DEV = 256
DOCS = 8
PACKS = 4
PACK_LEN = 2048
EXPERTS = 8
CAP = 48
N_SEQ = 8


def draw_lengths(key, part):
    key = jax.random.fold_in(key, 11)

    def one_row(row_key):
        cut_key, place_key = jax.random.split(row_key)
        cuts = jax.random.permutation(cut_key, TOK_DEV - 1)[:DOCS - 2].astype(jnp.int32) + 1
        cuts = jnp.sort(cuts)
        edges = jnp.concatenate([jnp.zeros((1,), jnp.int32), cuts, jnp.full((1,), TOK_DEV, jnp.int32)])
        short_docs = edges[1:] - edges[:-1]
        long_place = jax.random.randint(place_key, (), 0, DOCS - 1)
        places = jnp.arange(DOCS, dtype=jnp.int32)
        picked = jnp.clip(jnp.where(places < long_place, places, places - 1), 0, DOCS - 2)
        taken = short_docs[picked]
        return jnp.where(places == long_place, PACK_LEN - TOK_DEV, taken).astype(jnp.int32)
    row_keys = jax.random.split(key, PACKS)
    return jax.vmap(one_row)(row_keys)


def shard_levels(key, dims, cuts, smallest, top_value):
    def one(axis_at, shards_of):
        draws = jax.random.uniform(jax.random.fold_in(jax.random.fold_in(key, 6), axis_at), (shards_of,), jnp.float32, smallest / len(cuts), top_value / len(cuts))
        return jnp.repeat(jnp.exp(draws), dims[axis_at] // shards_of).reshape((-1,) + (1,) * (len(dims) - axis_at - 1))

    level = one(*cuts[0])
    for cut in cuts[1:]:
        level = level * one(*cut)
    return level


def assign_block(rng, own, number, rows, amount, top, reach, skew):
    ranking = jax.random.permutation(rng, amount)
    packed, common = portions_of(amount, rows * top, reach, skew, True), portions_of(amount, rows * top, reach, skew, False)
    places = jnp.arange(amount)

    def named(tallies, turn):
        used = int((tallies > 0).sum())
        fixed = max(1, used // 4)
        passed = fixed + (places - fixed + turn * (used - fixed)) % max(1, amount - fixed)
        return jnp.zeros((amount,), jnp.int32).at[ranking[jnp.where(places < fixed, places, passed)]].set(jnp.asarray(tallies, jnp.int32))

    tallies = jnp.where(number % 4 == 0, named(packed, number // 4), named(common, number - number // 4 - 1))
    mixed = jax.random.permutation(jax.random.fold_in(own, 3), amount)
    giver, sink = mixed[0:amount // 2 * 2:2], mixed[1:amount // 2 * 2:2]
    margin = jnp.minimum(tallies[giver] - 1, reach - tallies[sink]) // 2
    margin = jnp.where((giver == ranking[0]) | (sink == ranking[0]) | (tallies[sink] == 0), 0, jnp.maximum(margin, 0))
    passed = jax.random.randint(jax.random.fold_in(own, 4), (amount // 2,), 0, 1 << 20) % (margin + 1)
    tallies = tallies.at[giver].add(-passed).at[sink].add(passed)
    members = jnp.searchsorted(jnp.cumsum(tallies), jnp.arange(rows * top), side="right").astype(jnp.int32)
    table = members.reshape(top, rows).T
    table = table[jax.random.permutation(jax.random.fold_in(own, 1), rows)]
    turn = jax.random.randint(jax.random.fold_in(own, 2), (rows, 1), 0, top)
    return jnp.take_along_axis(table, (jnp.arange(top)[None, :] + turn) % top, axis=1)


def portions_of(number_of, total, limit, skew, full):
    weights = [(1 << 20) // math.isqrt(grade ** skew) + 1 for grade in range(1, number_of + 1)]
    largest = limit if full else min(limit, max(-(-total // number_of), total * weights[0] // sum(weights)))
    least = 1 if total - largest >= number_of - 1 else 0
    given, rest = [largest] + [least] * (number_of - 1), total - largest - least * (number_of - 1)
    while rest > 0:
        free = [i for i in range(1, number_of) if given[i] < largest] or [i for i in range(1, number_of) if given[i] < limit]
        whole, budget = sum([weights[i] for i in free]), rest
        for i in free:
            extra = min(limit - given[i], max(1, budget * weights[i] // whole), rest)
            given[i] = given[i] + extra
            rest = rest - extra
    return np.array(given)


def normal_values(rng, shape, scale, bound, shards=(), kind=jnp.bfloat16):
    drawn = jax.random.normal(rng, shape, jnp.float32) * scale
    if len(shards) > 0:
        drawn = shard_levels(rng, shape, shards, -0.22, 0.18) * drawn
    return jnp.clip(drawn, min=-bound, max=bound).astype(kind)


def setup_inputs(seed: int = 0) -> dict:
    splits = jax.random.split(jax.random.key(seed), 11)
    tokens = normal_values(splits[0], (PACKS, PACK_LEN, D), 1.0, 6.0, ((0, 4), (1, 8)))
    w_qkv = normal_values(splits[1], (D, 3 * D), (D // 2) ** -0.5, 0.25)
    w_out = normal_values(splits[2], (D, D), (D // 16) ** -0.5, 0.75)
    w_in = normal_values(splits[3], (EXPERTS, D, FF), D ** -0.5, 0.1875, ((0, 8),))
    w_exp_out = normal_values(splits[4], (EXPERTS, FF, D), (FF // 2) ** -0.5, 0.125, ((0, 8),))
    gains = jnp.clip(1.0 + 0.1 * jax.random.normal(splits[5], (2, D), jnp.float32), 0.5, 1.5)
    biases = normal_values(splits[6], (2, D), 0.2, 1.0, (), jnp.float32)
    lengths = draw_lengths(jax.random.fold_in(splits[10], 71), 0)
    hash_ids_keys = jax.random.split(jax.random.fold_in(splits[8], 1), PACKS * PACK_LEN // TOK_DEV)
    hash_ids_turns = jax.random.permutation(jax.random.fold_in(splits[8], 3), PACKS * PACK_LEN // TOK_DEV)
    hash_ids = jax.vmap(lambda own, number: assign_block(jax.random.fold_in(splits[8], 2), own, number, TOK_DEV, EXPERTS, 1, CAP, 1))(hash_ids_keys, hash_ids_turns).reshape((PACKS, PACK_LEN, 1))
    cotangent = normal_values(splits[9], (PACKS, PACK_LEN, D), 1.0, 6.0, ((0, 4), (1, 8)))
    return {"tokens": tokens, "w_qkv": w_qkv, "w_out": w_out, "w_in": w_in, "w_exp_out": w_exp_out, "gains": gains, "biases": biases, "lengths": lengths, "hash_ids": hash_ids, "cotangent": cotangent}


@jax.custom_vjp
def low(v):
    return lax.optimization_barrier(v.astype(jnp.bfloat16)).astype(jnp.float32)

@jax.custom_vjp
def low_back(v):
    return v

def low_keep(v):
    return (low(v), None)

def low_pass(kept, grad):
    return (grad,)

def back_keep(v):
    return (v, None)

def back_low(kept, grad):
    return (low(grad),)
low.defvjp(low_keep, low_pass)
low_back.defvjp(back_keep, back_low)
NORM_EPS = 1e-05
MASKED = -1e+30
HIGHEST = lax.Precision.HIGHEST

def layer_norm(rows, gain_row, bias_row):
    row_mean = lax.optimization_barrier(jnp.mean(rows, axis=-1, keepdims=True))
    centred = rows - row_mean
    row_var = lax.optimization_barrier(jnp.mean(centred * centred, axis=-1, keepdims=True))
    return centred * lax.rsqrt(row_var + NORM_EPS) * gain_row + bias_row

def doc_numbers(length_row, places):
    doc_ends = jnp.cumsum(length_row).astype(jnp.int32)
    return lax.optimization_barrier(jnp.sum((doc_ends[None, :] <= places[:, None]).astype(jnp.int32), axis=1)).astype(jnp.int32)

def pack_attention(query, keys, values, doc_row):
    length = query.shape[0]
    query_heads = query.reshape(length, HEADS, HEAD_DIM)
    key_heads = keys.reshape(length, HEADS, HEAD_DIM)
    value_heads = values.reshape(length, HEADS, HEAD_DIM)
    block_rows = min(512, length)
    key_pos = jnp.arange(length, dtype=jnp.int32)
    score_scale = 1.0 / math.sqrt(HEAD_DIM)

    def one_block(first_row):
        query_block = lax.dynamic_slice_in_dim(query_heads, first_row, block_rows, 0)
        query_doc = lax.dynamic_slice_in_dim(doc_row, first_row, block_rows, 0)
        query_pos = first_row + jnp.arange(block_rows, dtype=jnp.int32)
        raw_scores = low_back(jnp.einsum('qhd,khd->hqk', query_block, key_heads, precision=HIGHEST))
        visible = (query_doc[:, None] == doc_row[None, :]) & (key_pos[None, :] <= query_pos[:, None])
        scores = jnp.where(visible[None], raw_scores * score_scale, MASKED)
        row_top = lax.optimization_barrier(jnp.max(scores, axis=-1, keepdims=True))
        weights = jnp.where(visible[None], jnp.exp(scores - row_top), 0.0)
        prob_full = low(weights / lax.optimization_barrier(jnp.sum(weights, axis=-1, keepdims=True)))
        return jnp.einsum('hqk,khd->qhd', prob_full, value_heads, precision=HIGHEST)
    starts = jnp.arange(length // block_rows, dtype=jnp.int32) * block_rows
    outputs = lax.map(jax.checkpoint(one_block), starts)
    return outputs.reshape(length, D)

def forward(x_all, w_qkv, w_out, w_in, w_exp_out, gains, biases, docs_all, slot_index):

    def one_pack(item):
        x_rows, doc_row = item
        normed = low(layer_norm(x_rows, gains[0], biases[0]))
        mixed = low(low_back(jnp.dot(normed, w_qkv, precision=HIGHEST)))
        attended = low(low_back(pack_attention(mixed[:, :D], mixed[:, D:2 * D], mixed[:, 2 * D:], doc_row)))
        return x_rows + low_back(jnp.dot(attended, w_out, precision=HIGHEST))
    middle = lax.map(one_pack, (x_all, docs_all))
    flat = middle.reshape(-1, D)
    expert_in = low(low_back(layer_norm(flat, gains[1], biases[1])))
    room = PACKS * N_SEQ * CAP
    buffer = jnp.zeros((EXPERTS * room, D), jnp.float32).at[slot_index].set(expert_in)
    buffer = buffer.reshape(EXPERTS, room, D)
    pre_act = low_back(jnp.einsum('erd,edf->erf', buffer, w_in, precision=HIGHEST))
    active = low(jax.nn.gelu(pre_act, approximate=False))
    made_rows = low(low_back(jnp.einsum('erf,efd->erd', active, w_exp_out, precision=HIGHEST)))
    back_rows = made_rows.reshape(EXPERTS * room, D)[slot_index]
    return (flat + back_rows).reshape(middle.shape)

def reference(tokens, w_qkv, w_out, w_in, w_exp_out, gains, biases, lengths, hash_ids, cotangent):
    places = jnp.arange(PACK_LEN, dtype=jnp.int32)
    docs_all = jax.vmap(lambda length_row: doc_numbers(length_row, places))(lengths)
    expert_ids = hash_ids.reshape(-1).astype(jnp.int32)
    one_hot = (expert_ids[:, None] == jnp.arange(EXPERTS, dtype=jnp.int32)[None, :]).astype(jnp.int32)
    slot_rank = (lax.optimization_barrier(jnp.sum(jnp.cumsum(one_hot, axis=0).astype(jnp.int32) * one_hot, axis=1)) - 1).astype(jnp.int32)
    room = PACKS * N_SEQ * CAP
    slot_index = (expert_ids * room + slot_rank).astype(jnp.int32)
    primals = (tokens.astype(jnp.float32), w_qkv.astype(jnp.float32), w_out.astype(jnp.float32), w_in.astype(jnp.float32), w_exp_out.astype(jnp.float32), gains.astype(jnp.float32), biases.astype(jnp.float32))

    def wrapped(*params):
        return forward(*params, docs_all, slot_index)
    result, pull = jax.vjp(wrapped, *primals)
    grads = pull(cotangent.astype(jnp.float32))
    return (result.astype(jnp.bfloat16), grads[0], grads[1], grads[2], grads[3], grads[4], grads[5], grads[6])
```

```python
import functools
import math

import jax
import jax.numpy as jnp
from jax import lax
from jax.experimental import pallas as pl
from jax.experimental.pallas import tpu as pltpu
from jax.sharding import PartitionSpec as P

HEADS = 16
HEAD_DIM = 64
NORM_EPS = 1e-05
MASKED = -1e30
LOG2E = 1.4426950408889634
F32 = jnp.float32
BF16 = jnp.bfloat16
VMEM_BYTES = 56 * 1024 * 1024


def dot(a, b, ca=1, cb=0):
    return lax.dot_general(a, b, (((ca,), (cb,)), ((), ())), preferred_element_type=F32)


def params():
    return pltpu.CompilerParams(vmem_limit_bytes=VMEM_BYTES)


def shape(dims, kind):
    return jax.ShapeDtypeStruct(dims, kind)


def norm_parts(rows):
    row_mean = jnp.mean(rows, axis=-1, keepdims=True)
    centred = rows - row_mean
    row_var = jnp.mean(centred * centred, axis=-1, keepdims=True)
    inv_std = lax.rsqrt(row_var + NORM_EPS)
    return centred * inv_std, inv_std


def norm_back(scaled, unit_rows, inv_std):
    centred = scaled - jnp.mean(scaled, axis=-1, keepdims=True)
    centred = centred - unit_rows * jnp.mean(scaled * unit_rows, axis=-1, keepdims=True)
    return centred * inv_std


def gelu_both(pre):
    cdf = 0.5 + 0.5 * lax.erf(pre * 0.7071067811865476)
    density = jnp.exp(-0.5 * pre * pre) * 0.3989422804014327
    return pre * cdf, cdf + pre * density


def whole(array):
    rank = len(array.shape)
    return pl.BlockSpec(array.shape, lambda *unused: (0,) * rank)


def slots_of(ids_row, experts, cap):
    count = ids_row.shape[1]
    members = (lax.broadcasted_iota(jnp.int32, (experts, count), 0) == ids_row).astype(F32)
    order = lax.broadcasted_iota(jnp.int32, (count, count), 0) <= lax.broadcasted_iota(
        jnp.int32, (count, count), 1
    )
    ranks = dot(members.astype(BF16), order.astype(BF16))
    rank = jnp.sum(members * ranks, axis=0, keepdims=True).astype(jnp.int32) - 1
    return ids_row * cap + rank


def pick_rows(slot_row, count, first=0):
    rows = lax.broadcasted_iota(jnp.int32, (count, slot_row.shape[1]), 0) + first
    return (rows == slot_row).astype(BF16)


def place_rows(slot_row, count):
    tokens = slot_row.shape[1]
    column = jnp.broadcast_to(slot_row.astype(F32), (128, tokens)).T[:, :1]
    return (lax.broadcasted_iota(jnp.int32, (tokens, count), 1).astype(F32) == column).astype(BF16)


def qkv_kernel(experts, cap, tok, place, x_ref, w_ref, gain_ref, bias_ref, *refs):
    qkv_ref, unit_ref, xs_ref, slot_ref = refs[-4:]
    step = pl.program_id(0)
    own_expert = place[pl.num_programs(0)]
    x = x_ref[0, :tok]
    unit, unused = norm_parts(x.astype(F32))
    normed = (unit * gain_ref[0:1] + bias_ref[0:1]).astype(BF16)
    qkv_ref[0] = dot(normed, w_ref[...]).astype(BF16)
    unit_ref[0] = unit.T.astype(BF16)
    ids = x_ref[0, tok:][:1, :tok].astype(F32).astype(jnp.int32)
    slot = slots_of(ids, experts, cap)
    slot_ref[0] = jnp.broadcast_to(slot, (8, tok))
    xs_ref[0] = dot(pick_rows(slot, cap, own_expert * cap), x).astype(BF16)


def qkv_step(shards, places, expert, held, w_own, gains, biases, seq_count, experts, cap):
    count, rows, width = shards.shape
    tok = rows - 16
    wide = w_own.shape[1]
    index = jnp.concatenate([places, expert[None]]).astype(jnp.int32)
    outs = [
        shape((seq_count, tok, wide), BF16),
        shape((seq_count, width, tok), BF16),
        shape((seq_count, cap, width), BF16),
        shape((seq_count, 8, tok), jnp.int32),
    ]
    spec = pltpu.PrefetchScalarGridSpec(
        num_scalar_prefetch=1,
        grid=(count,),
        in_specs=[
            pl.BlockSpec((1, rows, width), lambda i, at: (i, 0, 0)),
            whole(w_own),
            whole(gains),
            whole(biases),
        ]
        + [pl.BlockSpec(memory_space=pl.ANY)] * len(held),
        out_specs=[
            pl.BlockSpec((1,) + out.shape[1:], lambda i, at: (at[i], 0, 0)) for out in outs
        ],
    )
    return pl.pallas_call(
        functools.partial(qkv_kernel, experts, cap, tok),
        out_shape=outs,
        grid_spec=spec,
        input_output_aliases={5 + n: n for n in range(len(held))},
        compiler_params=params(),
        name="qkv_step",
    )(index, shards, w_own, gains, biases, *held)


def send_kernel(experts, cap, ids_ref, rows_ref, out_ref, slot_ref):
    slot = slots_of(ids_ref[0:1], experts, cap)
    slot_ref[...] = jnp.broadcast_to(slot, slot_ref.shape)
    out_ref[...] = dot(pick_rows(slot, experts * cap), rows_ref[...]).astype(BF16)


def send_rows(ids_row, rows, experts, cap):
    tok, width = rows.shape
    return pl.pallas_call(
        functools.partial(send_kernel, experts, cap),
        out_shape=[shape((experts * cap, width), BF16), shape((8, tok), jnp.int32)],
        compiler_params=params(),
        name="send_rows",
    )(jnp.broadcast_to(ids_row, (8, tok)), rows)


def doc_start(ends_ref, positions, docs):
    start = jnp.zeros_like(positions)
    for k in range(docs):
        start = jnp.where(ends_ref[k] <= positions, ends_ref[k], start)
    return start


def head_lanes(array, head):
    lane = lax.broadcasted_iota(jnp.int32, (1, array.shape[1]), 1)
    return jnp.where(lane // HEAD_DIM == head, array, jnp.zeros_like(array))


def attend_kernel(docs, cap, ends_ref, qkv_ref, slot_ref, send_ref, out_ref, lse_ref):
    blocks, tok, wide = qkv_ref.shape
    width = wide // 3
    heads = width // HEAD_DIM
    experts = send_ref.shape[0]
    here = pl.program_id(0)
    scale = LOG2E / math.sqrt(HEAD_DIM)
    lane = lax.broadcasted_iota(jnp.int32, (tok, width), 1)

    def run(block):
        q = qkv_ref[block, :, :width]
        local = lax.broadcasted_iota(jnp.int32, (tok, 1), 0)
        start = doc_start(ends_ref, block * tok + local, docs)
        ones = jnp.ones((tok, width), BF16)
        merged = jnp.zeros((tok, width), F32)
        lse = jnp.zeros((tok, width), F32)
        for head in range(heads):
            q_head = head_lanes(q, head)
            parts = []
            for other in range(block + 1):
                s = dot(q_head, qkv_ref[other, :, width : 2 * width], 1, 1)
                column = lax.broadcasted_iota(jnp.int32, (tok, tok), 1)
                if other == block:
                    mask = (column <= local) & (column + other * tok >= start)
                    s = jnp.where(mask, s, MASKED)
                elif other == 0 or block == blocks - 1:
                    s = jnp.where(column + other * tok >= start, s, MASKED)
                parts.append(s)
            top = parts[0]
            for s in parts[1:]:
                top = jnp.maximum(top, s)
            top = jnp.max(top, axis=1, keepdims=True)
            shift = top * scale
            total = jnp.zeros((tok, 2 * width), F32)
            for other in range(block + 1):
                p = jnp.exp2(parts[other] * scale - shift).astype(BF16)
                v = jnp.concatenate([qkv_ref[other, :, 2 * width :], ones], axis=1)
                total = total + dot(p, v)
            weight = total[:, width:]
            mine = lane // HEAD_DIM == head
            merged = jnp.where(mine, total[:, :width] / weight, merged)
            lse = jnp.where(lane == head, shift + jnp.log2(weight), lse)
        out_ref[0] = merged
        lse_ref[0] = lse.T[:8]
        pick = pick_rows(slot_ref[0, 0:1], experts * cap)
        rows = dot(pick, merged.astype(BF16)).astype(BF16)
        for e in range(experts):
            send_ref[e, 0] = rows[e * cap : (e + 1) * cap]

    for block in range(blocks):
        pl.when(here == block)(functools.partial(run, block))


def attend(qkv, slots, ends, cap):
    blocks, tok, wide = qkv.shape
    width = wide // 3
    return pl.pallas_call(
        functools.partial(attend_kernel, ends.shape[0], cap),
        out_shape=[
            shape((blocks, blocks, cap, width), BF16),
            shape((blocks, tok, width), F32),
            shape((blocks, 8, tok), F32),
        ],
        grid=(blocks,),
        in_specs=[
            pl.BlockSpec(memory_space=pltpu.SMEM),
            whole(qkv),
            pl.BlockSpec((1, 8, tok), lambda i: (i, 0, 0)),
        ],
        out_specs=[
            pl.BlockSpec((blocks, 1, cap, width), lambda i: (0, i, 0, 0)),
            pl.BlockSpec((1, tok, width), lambda i: (i, 0, 0)),
            pl.BlockSpec((1, 8, tok), lambda i: (i, 0, 0)),
        ],
        compiler_params=params(),
        name="attend",
    )(ends, qkv, slots)


def attend_back_kernel(
    docs, cap, ends_ref, qkv_ref, slot_ref, back_ref, out_ref, lse_ref, grad_ref, do_ref, dq_ref, delta_ref
):
    blocks, tok, wide = qkv_ref.shape
    width = wide // 3
    heads = width // HEAD_DIM
    experts = back_ref.shape[0]
    here = pl.program_id(0)
    scale = LOG2E / math.sqrt(HEAD_DIM)

    @pl.when(here == 0)
    def prepare():
        for t in range(blocks):
            rows = jnp.concatenate([back_ref[e, t] for e in range(experts)], axis=0)
            do = dot(place_rows(slot_ref[t, 0:1], experts * cap), rows)
            do_ref[t] = do.astype(BF16)
            product = (do * out_ref[t]).T
            delta = jnp.zeros((8, tok), F32)
            row = lax.broadcasted_iota(jnp.int32, (8, tok), 0)
            for head in range(heads):
                part = product[head * HEAD_DIM : (head + 1) * HEAD_DIM]
                delta = jnp.where(row == head, jnp.sum(part, axis=0, keepdims=True), delta)
            delta_ref[t] = delta
            dq_ref[t] = jnp.zeros((tok, width), F32)

    def run(block):
        k = qkv_ref[block, :, width : 2 * width]
        v = qkv_ref[block, :, 2 * width :]
        k_pos = lax.broadcasted_iota(jnp.int32, (tok, tok), 0) + block * tok
        dk = jnp.zeros((tok, width), F32)
        dv = jnp.zeros((tok, width), F32)
        for other in range(block, blocks):
            q_pos = lax.broadcasted_iota(jnp.int32, (1, tok), 1) + other * tok
            start = doc_start(ends_ref, q_pos, docs)
            q = qkv_ref[other, :, :width]
            do = do_ref[other]
            dq = dq_ref[other]
            for head in range(heads):
                q_head = head_lanes(q, head)
                do_head = head_lanes(do, head)
                s = dot(k, q_head, 1, 1)
                p = jnp.exp2(s * scale - lse_ref[other, head : head + 1])
                if other == block:
                    p = jnp.where((k_pos <= q_pos) & (k_pos >= start), p, 0.0)
                elif block == 0 or other == blocks - 1:
                    p = jnp.where(k_pos >= start, p, 0.0)
                dp = dot(v, do_head, 1, 1)
                ds = (p * (dp - delta_ref[other, head : head + 1])).astype(BF16)
                dv = dv + dot(p.astype(BF16), do_head)
                dk = dk + dot(ds, q_head)
                dq = dq + dot(ds, head_lanes(k, head), 0, 0)
            dq_ref[other] = dq
        factor = 1.0 / math.sqrt(HEAD_DIM)
        grad_ref[block, :, :width] = (dq_ref[block] * factor).astype(BF16)
        grad_ref[block, :, width : 2 * width] = (dk * factor).astype(BF16)
        grad_ref[block, :, 2 * width :] = dv.astype(BF16)

    for block in range(blocks):
        pl.when(here == block)(functools.partial(run, block))


def attend_back(qkv, slots, back, out, lse, ends, cap):
    blocks, tok, wide = qkv.shape
    width = wide // 3
    return pl.pallas_call(
        functools.partial(attend_back_kernel, ends.shape[0], cap),
        out_shape=shape((blocks, tok, wide), BF16),
        grid=(blocks,),
        in_specs=[pl.BlockSpec(memory_space=pltpu.SMEM)]
        + [whole(a) for a in (qkv, slots, back, out, lse)],
        out_specs=whole(qkv),
        scratch_shapes=[
            pltpu.VMEM((blocks, tok, width), BF16),
            pltpu.VMEM((blocks, tok, width), F32),
            pltpu.VMEM((blocks, 8, tok), F32),
        ],
        compiler_params=params(),
        name="attend_back",
    )(ends, qkv, slots, back, out, lse)


def pick_all(slots, count):
    return (slots[:, :1, :] == jnp.arange(count, dtype=jnp.int32)[None, :, None]).astype(BF16)


def long_masks(ends, first, tok, length):
    q_pos = first + jnp.arange(tok, dtype=jnp.int32)
    k_pos = jnp.arange(length, dtype=jnp.int32)
    start = jnp.max(jnp.where(ends[None, :] <= q_pos[:, None], ends[None, :], 0), axis=1)
    return (k_pos[None, :] <= q_pos[:, None]) & (k_pos[None, :] >= start[:, None])


def long_heads(rows, width):
    return rows.reshape(rows.shape[0], width // HEAD_DIM, HEAD_DIM).transpose(1, 0, 2)


def attend_long(qkv, slots, ends, cap):
    blocks, tok, wide = qkv.shape
    width = wide // 3
    length = blocks * tok
    flat = qkv.reshape(length, wide)
    keys = long_heads(flat[:, width : 2 * width], width)
    values = long_heads(flat[:, 2 * width :], width)

    def one(block):
        query = long_heads(qkv[block, :, :width], width)
        mask = long_masks(ends, block * tok, tok, length)
        s = jnp.einsum("hqd,hkd->hqk", query, keys, preferred_element_type=F32)
        s = jnp.where(mask, s / math.sqrt(HEAD_DIM), MASKED)
        top = jnp.max(s, axis=-1, keepdims=True)
        weights = jnp.where(mask, jnp.exp(s - top), 0.0)
        total = jnp.sum(weights, axis=-1, keepdims=True)
        out = jnp.einsum("hqk,hkd->hqd", (weights / total).astype(BF16), values, preferred_element_type=F32)
        return out.transpose(1, 0, 2).reshape(tok, width), (top + jnp.log(total))[:, :, 0]

    out, lse = lax.map(one, jnp.arange(blocks, dtype=jnp.int32))
    pick = pick_all(slots, blocks * cap)
    rows = jnp.einsum("tsk,tkd->tsd", pick, out.astype(BF16), preferred_element_type=F32)
    send = rows.astype(BF16).reshape(blocks, blocks, cap, width).transpose(1, 0, 2, 3)
    return send, out, lse


def attend_back_long(qkv, slots, back, out, lse, ends, cap):
    blocks, tok, wide = qkv.shape
    width = wide // 3
    length = blocks * tok
    heads = width // HEAD_DIM
    flat = qkv.reshape(length, wide)
    keys = long_heads(flat[:, width : 2 * width], width)
    values = long_heads(flat[:, 2 * width :], width)
    pick = pick_all(slots, blocks * cap)
    rows = back.transpose(1, 0, 2, 3).reshape(blocks, blocks * cap, width)
    do_all = jnp.einsum("tsk,tsd->tkd", pick, rows, preferred_element_type=F32)

    def one(sums, block):
        query = long_heads(qkv[block, :, :width], width)
        mask = long_masks(ends, block * tok, tok, length)
        do = do_all[block]
        delta = jnp.sum((do * out[block]).reshape(tok, heads, HEAD_DIM), axis=-1).T
        do = long_heads(do.astype(BF16), width)
        s = jnp.einsum("hqd,hkd->hqk", query, keys, preferred_element_type=F32)
        p = jnp.where(mask, jnp.exp(s / math.sqrt(HEAD_DIM) - lse[block][:, :, None]), 0.0)
        dp = jnp.einsum("hqd,hkd->hqk", do, values, preferred_element_type=F32)
        ds = (p * (dp - delta[:, :, None]) / math.sqrt(HEAD_DIM)).astype(BF16)
        dq = jnp.einsum("hqk,hkd->qhd", ds, keys, preferred_element_type=F32)
        dk = jnp.einsum("hqk,hqd->khd", ds, query, preferred_element_type=F32)
        dv = jnp.einsum("hqk,hqd->khd", p.astype(BF16), do, preferred_element_type=F32)
        sums = (sums[0] + dk.reshape(length, width), sums[1] + dv.reshape(length, width))
        return sums, dq.reshape(tok, width)

    start = jnp.zeros((length, width), F32)
    (dk, dv), dq = lax.scan(one, (start, start), jnp.arange(blocks, dtype=jnp.int32))
    grad = jnp.concatenate([dq.reshape(length, width), dk, dv], axis=1).astype(BF16)
    return grad.reshape(blocks, tok, wide)


def expert_kernel(
    att_ref, xs_ref, g_ref, w_out_ref, gain_ref, bias_ref, w1_ref, w2_ref,
    back_ref, datt_ref, ein_ref, branch_ref, sums_ref, mid_ref, made_ref, down_ref,
):
    step = pl.program_id(0)
    groups, rows, width = att_ref.shape
    cap = back_ref.shape[1] // 2

    @pl.when(step == 0)
    def begin():
        att = jnp.concatenate([att_ref[n] for n in range(groups)], axis=1)
        mid = xs_ref[...].astype(F32) + dot(att, w_out_ref[...])
        mid_ref[...] = mid
        unit, unused = norm_parts(mid)
        ein_ref[...] = (unit * gain_ref[1:2] + bias_ref[1:2]).astype(BF16)
        made_ref[...] = jnp.zeros_like(made_ref)
        down_ref[...] = jnp.zeros_like(down_ref)

    w1 = w1_ref[0]
    w2 = w2_ref[0]
    pre = dot(ein_ref[...], w1)
    d_active = dot(g_ref[...], w2, 1, 1)
    active, slope = gelu_both(pre)
    d_pre = (d_active * slope).astype(BF16)
    down_ref[...] += dot(d_pre, w1, 1, 1)
    made_ref[...] += dot(active.astype(BF16), w2)

    @pl.when(step == pl.num_programs(0) - 1)
    def finish():
        mid = mid_ref[...]
        unit, inv_std = norm_parts(mid)
        d_in = down_ref[...].astype(BF16).astype(F32)
        d_mid = g_ref[...].astype(F32) + norm_back(d_in * gain_ref[1:2], unit, inv_std)
        branch = d_mid.astype(BF16)
        branch_ref[...] = branch
        d_att = dot(branch, w_out_ref[...], 1, 1).astype(BF16)
        for n in range(groups):
            datt_ref[n] = d_att[:, n * width : (n + 1) * width]
        made = (mid + made_ref[...].astype(BF16).astype(F32)).astype(BF16)
        for t in range(back_ref.shape[0]):
            back_ref[t, :cap] = made[t * cap : (t + 1) * cap]
            back_ref[t, cap:] = branch[t * cap : (t + 1) * cap]
        sums_ref[...] = jnp.zeros_like(sums_ref)
        sums_ref[0:1] = jnp.sum(d_in * unit, axis=0, keepdims=True)
        sums_ref[1:2] = jnp.sum(d_in, axis=0, keepdims=True)


def expert(att, xs, grads, w_out, gains, biases, w_in, w_exp_out, seq_count):
    groups, rows, width = att.shape
    wide = xs.shape[1]
    hidden = w_in.shape[2]
    part = 512
    outs = [
        shape((seq_count, 2 * rows // seq_count, wide), BF16),
        shape(att.shape, BF16),
        shape((rows, wide), BF16),
        shape((rows, wide), BF16),
        shape((8, wide), F32),
    ]
    return pl.pallas_call(
        expert_kernel,
        out_shape=outs,
        grid=(hidden // part,),
        in_specs=[whole(a) for a in (att, xs, grads, w_out, gains, biases)]
        + [
            pl.BlockSpec((1, wide, part), lambda i: (0, 0, i)),
            pl.BlockSpec((1, part, wide), lambda i: (0, i, 0)),
        ],
        out_specs=[whole(a) for a in outs],
        scratch_shapes=[pltpu.VMEM((rows, wide), F32)] * 3,
        compiler_params=params(),
        name="expert",
    )(att, xs, grads, w_out, gains, biases, w_in, w_exp_out)


def weights_kernel(place, x_ref, g_ref, w1_ref, w2_ref, d1_ref, d2_ref, turned_ref):
    @pl.when(pl.program_id(0) == 0)
    def begin():
        turned_ref[...] = x_ref[...].T

    x = x_ref[...]
    g = g_ref[...]
    pre = dot(x, w1_ref[0])
    d_active = dot(g, w2_ref[0], 1, 1)
    active, slope = gelu_both(pre)
    d_pre = (d_active * slope).astype(BF16)
    d1_ref[0] = dot(turned_ref[...], d_pre)
    d2_ref[0] = dot(active.astype(BF16), g, 0, 0)


def expert_weights(rows, grads, w_in, w_exp_out, place, parts):
    count, wide = rows.shape
    hidden = w_in.shape[2] // parts
    part = 256
    steps = hidden // part
    spec = pltpu.PrefetchScalarGridSpec(
        num_scalar_prefetch=1,
        grid=(steps,),
        in_specs=[
            whole(rows),
            whole(grads),
            pl.BlockSpec((1, wide, part), lambda i, at: (0, 0, at[0] * steps + i)),
            pl.BlockSpec((1, part, wide), lambda i, at: (0, at[0] * steps + i, 0)),
        ],
        out_specs=[
            pl.BlockSpec((1, wide, part), lambda i, at: (0, 0, i)),
            pl.BlockSpec((1, part, wide), lambda i, at: (0, i, 0)),
        ],
        scratch_shapes=[pltpu.VMEM((wide, count), BF16)],
    )
    return pl.pallas_call(
        weights_kernel,
        out_shape=[shape((1, wide, hidden), F32), shape((1, hidden, wide), F32)],
        grid_spec=spec,
        compiler_params=params(),
        name="expert_weights",
    )(place[None].astype(jnp.int32), rows, grads, w_in, w_exp_out)


def out_weights_kernel(att_ref, branch_ref, out_ref):
    for n in range(att_ref.shape[0]):
        width = att_ref.shape[2]
        out_ref[n * width : (n + 1) * width] = dot(att_ref[n], branch_ref[...], 0, 0).astype(BF16)


def out_weights(att, branch):
    wide = branch.shape[1]
    return pl.pallas_call(
        out_weights_kernel,
        out_shape=shape((wide, wide), BF16),
        compiler_params=params(),
        name="out_weights",
    )(att, branch)


def qkv_weights_kernel(unit_ref, grad_ref, w_ref, gain_ref, bias_ref, out_ref, sums_ref):
    blocks = unit_ref.shape[0]
    parts, wide, width = out_ref.shape
    moment = jnp.zeros((wide, parts * width), F32)
    total = jnp.zeros((1, parts * width), F32)
    for t in range(blocks):
        grad = grad_ref[t]
        moment = moment + dot(unit_ref[t], grad)
        total = total + jnp.sum(grad.astype(F32), axis=0, keepdims=True)
    made = moment * gain_ref[:, 0:1] + bias_ref[:, 0:1] * total
    for p in range(parts):
        out_ref[p] = made[:, p * width : (p + 1) * width].astype(BF16)
    w = w_ref[...].astype(F32)
    d_gain = jnp.sum(w * moment, axis=1, keepdims=True)
    d_bias = jnp.sum(w * total, axis=1, keepdims=True)
    lane = lax.broadcasted_iota(jnp.int32, (wide, 128), 1)
    sums_ref[...] = jnp.where(lane == 0, d_gain, jnp.where(lane == 1, d_bias, 0.0)).T[:8]


def qkv_weights(unit, grad, w_own, gains, biases):
    blocks, wide, tok = unit.shape
    width = w_own.shape[1] // 3
    if width % 128 != 0:
        moment = jnp.einsum("tdk,tkf->df", unit, grad, preferred_element_type=F32)
        total = jnp.sum(grad.astype(F32), axis=(0, 1))
        made = moment * gains[0][:, None] + biases[0][:, None] * total[None, :]
        made = made.astype(BF16).reshape(wide, 3, width).transpose(1, 0, 2)
        w = w_own.astype(F32)
        sums = jnp.stack([jnp.sum(w * moment, axis=1), jnp.sum(w * total[None, :], axis=1)])
        return made, jnp.pad(sums, ((0, 6), (0, 0)))
    return pl.pallas_call(
        qkv_weights_kernel,
        out_shape=[shape((3, wide, width), BF16), shape((8, wide), F32)],
        compiler_params=params(),
        name="qkv_weights",
    )(unit, grad, w_own, gains.T, biases.T)


def finish_kernel(
    x_ref, grad_ref, w_ref, gain_ref, slot_ref, back_ref, out_ref, dx_ref, sum_ref
):
    step = pl.program_id(0)
    groups, tok, wide = grad_ref.shape
    width = wide // 3
    cap = back_ref.shape[1] // 2
    own = jnp.concatenate([grad_ref[n, :, :width] for n in range(groups)], axis=1)
    for p in (1, 2):
        at = p * width
        other = jnp.concatenate([grad_ref[n, :, at : at + width] for n in range(groups)], axis=1)
        own = jnp.where(step == p, other, own)
    term = dot(own, w_ref[...], 1, 1)

    @pl.when(step == 0)
    def first():
        sum_ref[...] = term
        place = place_rows(slot_ref[0:1], groups_of(back_ref) * cap)
        made = jnp.concatenate([back_ref[e, :cap] for e in range(groups_of(back_ref))], axis=0)
        out_ref[0] = dot(place, made).astype(BF16)
        branch = jnp.concatenate([back_ref[e, cap:] for e in range(groups_of(back_ref))], axis=0)
        dx_ref[0] = dot(place, branch)

    @pl.when(step > 0)
    def later():
        sum_ref[...] += term

    @pl.when(step == 2)
    def last():
        unit, inv_std = norm_parts(x_ref[...].astype(F32))
        dx_ref[0] = dx_ref[0] + norm_back(sum_ref[...] * gain_ref[0:1], unit, inv_std)


def groups_of(ref):
    return ref.shape[0]


def finish(x, grad, w_qkv, gains, slots, back):
    tok, wide = x.shape
    outs = [shape((1, tok, wide), BF16), shape((1, tok, wide), F32)]
    return pl.pallas_call(
        finish_kernel,
        out_shape=outs,
        grid=(3,),
        in_specs=[
            whole(x),
            whole(grad),
            pl.BlockSpec((wide, wide), lambda i: (0, i)),
            whole(gains),
            whole(slots),
            whole(back),
        ],
        out_specs=[whole(a) for a in outs],
        scratch_shapes=[pltpu.VMEM((tok, wide), F32)],
        compiler_params=params(),
        name="finish",
    )(x, grad, w_qkv, gains, slots, back)


WALK = (0, 2, 4, 6, 7, 5, 3, 1)


def walk_pairs(way):
    return [(WALK[n], WALK[(n + way) % len(WALK)]) for n in range(len(WALK))]


def walk_place(at, hops):
    table = [0] * len(WALK)
    for n, device in enumerate(WALK):
        table[device] = WALK[(n - hops) % len(WALK)]
    return jnp.asarray(table, jnp.int32)[at]


def gather_steps(own, at, seq_count):
    if seq_count != len(WALK):
        yield lax.all_gather(own, "seq"), jnp.arange(seq_count, dtype=jnp.int32)
        return
    yield own[None], at[None]
    ahead = behind = own
    half = own.shape[0] // 2
    for hops in range(1, 4):
        ahead = lax.ppermute(ahead, "seq", walk_pairs(1))
        behind = lax.ppermute(behind, "seq", walk_pairs(-1))
        yield ahead[None], walk_place(at, hops)[None]
        yield behind[None], walk_place(at, -hops)[None]
    top = lax.ppermute(ahead[:half], "seq", walk_pairs(1))
    low = lax.ppermute(behind[half:], "seq", walk_pairs(-1))
    yield jnp.concatenate([top, low], axis=0)[None], walk_place(at, 4)[None]


def swap(x):
    return lax.all_to_all(x, "seq", split_axis=0, concat_axis=0, tiled=True)


def swap_direct(x, at):
    count = x.shape[0]
    got = []
    for hops in range(1, count):
        piece = lax.dynamic_index_in_dim(x, (at + hops) % count, 0, keepdims=False)
        pairs = [(n, (n + hops) % count) for n in range(count)]
        got.append(lax.ppermute(piece, "seq", pairs))
    out = x
    for hops, piece in enumerate(got, 1):
        out = lax.dynamic_update_index_in_dim(out, piece, (at - hops) % count, 0)
    return out


def flip_pairs(count, bit):
    return [(n, n ^ bit) for n in range(count)]


def gather_batch(own, at, count):
    far = lax.ppermute(own, "batch", flip_pairs(count, 2))
    both = jnp.concatenate([own, far], axis=0)
    near = lax.ppermute(both, "batch", flip_pairs(count, 1))
    return jnp.concatenate([both, near], axis=0)


def sum_batch(part_of, at, count):
    send = jnp.stack([part_of(at ^ 1), part_of(at ^ 3)])
    got = lax.ppermute(send, "batch", flip_pairs(count, 1)).astype(F32)
    mine = part_of(at).astype(F32) + got[0]
    theirs = part_of(at ^ 2).astype(F32) + got[1]
    return mine + lax.ppermute(theirs.astype(BF16), "batch", flip_pairs(count, 2)).astype(F32)


def on_device(tokens, w_qkv, w_out, w_in, w_exp_out, gains, biases, lengths, hash_ids, cotangent):
    tok, width = tokens.shape[1:]
    seq_count = lax.axis_size("seq")
    batch_count = lax.axis_size("batch")
    at = lax.axis_index("seq")
    row = lax.axis_index("batch")
    groups = min(HEADS, seq_count)
    copies = seq_count // groups
    group = at // copies
    own = width // groups
    experts = seq_count
    slot_cap = max(2, 3 * tok // (2 * experts))
    cap = -(-slot_cap // 16) * 16
    x = tokens[0]
    ends = jnp.cumsum(lengths[0]).astype(jnp.int32)
    ids_row = hash_ids[0, :, 0][None, :]

    ids_rows = jnp.broadcast_to(jnp.pad(ids_row.astype(BF16), ((0, 0), (0, width - tok))), (16, width))
    load = jnp.concatenate([x, ids_rows], axis=0)
    w_own = lax.dynamic_slice_in_dim(
        w_qkv.reshape(width, 3, groups, own), group, 1, 2
    ).reshape(width, 3 * own)
    held = ()
    last = None
    for shards, places in gather_steps(load, at, seq_count):
        held = qkv_step(shards, places, at, held, w_own, gains, biases, seq_count, experts, cap)
        last = shards
    qkv, unit, xs, slots = held

    cot, unused = lax.optimization_barrier((cotangent[0], last))
    grad_rows, own_slots = send_rows(ids_row, cot, experts, cap)
    grads = swap(grad_rows.reshape(experts, cap, width)).reshape(seq_count * cap, width)

    long_rows = own % 128 != 0 or seq_count > 8
    send, att_out, lse = (attend_long if long_rows else attend)(qkv, slots, ends, cap)
    share = seq_count // copies
    if copies > 1:
        send = lax.dynamic_slice_in_dim(send, (at % copies) * share, share, 1)
    got = swap(send).reshape(groups, seq_count * cap, own)
    slot_rows = seq_count * cap
    if own % 128 != 0:
        att = got.transpose(1, 0, 2).reshape(1, slot_rows, width)
    else:
        att = got
    back, d_att, expert_in, branch, sums_two = expert(
        att, xs.reshape(slot_rows, width), grads, w_out, gains, biases, w_in, w_exp_out, seq_count
    )
    if own % 128 != 0:
        d_att = d_att.reshape(slot_rows, groups, own).transpose(1, 0, 2)
    if copies > 1:
        d_att = jnp.repeat(d_att, copies, axis=0)
    d_att = swap(d_att).reshape(experts, seq_count, cap, own)

    back = swap_direct(back, at) if seq_count == len(WALK) else swap(back)

    d_qkv = (attend_back_long if long_rows else attend_back)(qkv, slots, d_att, att_out, lse, ends, cap)
    own_grad = swap(d_qkv).reshape(groups, copies, tok, 3 * own)[:, 0]
    if own % 128 != 0:
        own_grad = own_grad.reshape(groups, tok, 3, own).transpose(1, 2, 0, 3).reshape(1, tok, 3 * width)
    output, d_tokens = finish(x, own_grad, w_qkv, gains, own_slots, back)

    all_rows = gather_batch(expert_in, row, batch_count)
    all_grads = gather_batch(grads, row, batch_count)
    d_w_in, d_w_exp_out = expert_weights(all_rows, all_grads, w_in, w_exp_out, row, batch_count)

    part = width // batch_count
    d_out = out_weights(att, branch)
    d_out = sum_batch(
        lambda n: lax.dynamic_slice_in_dim(d_out, n * part, part, 1), row, batch_count
    ).astype(BF16)
    d_out = swap(d_out.reshape(seq_count, width // seq_count, part))
    d_out = jnp.sum(d_out.astype(F32), axis=0).astype(BF16)

    d_cols, sums_one = qkv_weights(unit, d_qkv, w_own, gains, biases)
    sums = jnp.stack([sums_one[0] / copies, sums_two[0], sums_one[1] / copies, sums_two[1]])
    per_row = 3 * groups // batch_count

    def part_of(n):
        block = (n * per_row - group + groups - 1) // groups
        number = block * groups + group
        fits = (block < 3) & (number < (n + 1) * per_row)
        cols = lax.dynamic_index_in_dim(d_cols, jnp.minimum(block, 2), 0, keepdims=False)
        cols = jnp.where(fits, cols, jnp.zeros_like(cols))
        norms = lax.dynamic_slice_in_dim(sums, n * part, part, 1).astype(BF16)
        return jnp.concatenate([cols.reshape(-1), norms.reshape(-1)]).reshape(-1, 128)

    mine = sum_batch(part_of, row, batch_count).astype(BF16)
    bundle = jnp.concatenate([mine, d_out.reshape(-1, 128)], axis=0)
    cuts = (width * own // 128, (width * own + 4 * part) // 128)
    if seq_count == len(WALK):
        gathered = jnp.zeros((seq_count,) + bundle.shape, BF16)
        for blocks, places in gather_steps(bundle, at, seq_count):
            gathered = lax.dynamic_update_slice_in_dim(gathered, blocks, places[0], 0)
    else:
        gathered = lax.all_gather(bundle, "seq")
    order = (row * per_row + jnp.arange(per_row, dtype=jnp.int32)) % groups * copies
    cols = jnp.take(gathered[:, : cuts[0]], order, axis=0).reshape(per_row, width, own)
    d_w_qkv = cols.transpose(1, 0, 2).reshape(width, per_row * own).astype(F32)
    norms = jnp.sum(gathered[:, cuts[0] : cuts[1]].astype(F32), axis=0).reshape(4, part)
    d_w_out = gathered[:, cuts[1] :].reshape(width, part).astype(F32)
    return output, d_tokens, d_w_qkv, d_w_out, d_w_in, d_w_exp_out, norms[:2], norms[2:]


def solution(mesh):
    return jax.shard_map(
        on_device,
        mesh=mesh,
        in_specs=(
            P("batch", "seq", None),
            P(),
            P(),
            P("seq", None, None),
            P("seq", None, None),
            P(),
            P(),
            P("batch", None),
            P("batch", "seq", None),
            P("batch", "seq", None),
        ),
        out_specs=(
            P("batch", "seq", None),
            P("batch", "seq", None),
            P(None, "batch"),
            P(None, "batch"),
            P("seq", None, "batch"),
            P("seq", "batch", None),
            P(None, "batch"),
            P(None, "batch"),
        ),
        check_vma=False,
    )
```

```python
import functools
import math

import jax
import jax.numpy as jnp
from jax import lax
from jax.experimental import pallas as pl
from jax.experimental.pallas import tpu as pltpu
from jax.sharding import PartitionSpec as P

HEADS = 16
HEAD_DIM = 64
NORM_EPS = 1e-05
MASKED = -1e30
LOG2E = 1.4426950408889634
F32 = jnp.float32
BF16 = jnp.bfloat16
VMEM_BYTES = 56 * 1024 * 1024


def dot(a, b, ca=1, cb=0):
    return lax.dot_general(a, b, (((ca,), (cb,)), ((), ())), preferred_element_type=F32)


def cost(time_us):
    return pl.CostEstimate(flops=int(time_us * 1e9), bytes_accessed=int(time_us * 3e6), transcendentals=0)


def params():
    return pltpu.CompilerParams(vmem_limit_bytes=VMEM_BYTES)


def shape(dims, kind):
    return jax.ShapeDtypeStruct(dims, kind)


def norm_parts(rows):
    row_mean = jnp.mean(rows, axis=-1, keepdims=True)
    centred = rows - row_mean
    row_var = jnp.mean(centred * centred, axis=-1, keepdims=True)
    inv_std = lax.rsqrt(row_var + NORM_EPS)
    return centred * inv_std, inv_std


def norm_back(scaled, unit_rows, inv_std):
    centred = scaled - jnp.mean(scaled, axis=-1, keepdims=True)
    centred = centred - unit_rows * jnp.mean(scaled * unit_rows, axis=-1, keepdims=True)
    return centred * inv_std


def gelu_both(pre):
    cdf = 0.5 + 0.5 * lax.erf(pre * 0.7071067811865476)
    density = jnp.exp(-0.5 * pre * pre) * 0.3989422804014327
    return pre * cdf, cdf + pre * density


def whole(array):
    rank = len(array.shape)
    return pl.BlockSpec(array.shape, lambda *unused: (0,) * rank)


def slots_of(ids_row, experts, cap):
    count = ids_row.shape[1]
    members = (lax.broadcasted_iota(jnp.int32, (experts, count), 0) == ids_row).astype(F32)
    order = lax.broadcasted_iota(jnp.int32, (count, count), 0) <= lax.broadcasted_iota(
        jnp.int32, (count, count), 1
    )
    ranks = dot(members.astype(BF16), order.astype(BF16))
    rank = jnp.sum(members * ranks, axis=0, keepdims=True).astype(jnp.int32) - 1
    return ids_row * cap + rank


def pick_rows(slot_row, count, first=0):
    rows = lax.broadcasted_iota(jnp.int32, (count, slot_row.shape[1]), 0) + first
    return (rows == slot_row).astype(BF16)


def place_rows(slot_row, count):
    tokens = slot_row.shape[1]
    column = jnp.broadcast_to(slot_row.astype(F32), (128, tokens)).T[:, :1]
    return (lax.broadcasted_iota(jnp.int32, (tokens, count), 1).astype(F32) == column).astype(BF16)


def qkv_kernel(experts, cap, tok, first, place, x_ref, w_ref, gain_ref, bias_ref, *refs):
    qkv_ref, unit_ref, xs_ref, slot_ref = refs[-4:]
    own_expert = place[0]
    x = x_ref[0, :tok]
    unit, unused = norm_parts(x.astype(F32))
    normed = (unit * gain_ref[0:1] + bias_ref[0:1]).astype(BF16)
    qkv_ref[0] = dot(normed, w_ref[...]).astype(BF16)
    unit_ref[0] = unit.T.astype(BF16)
    ids = x_ref[0, tok:][:1, :tok].astype(F32).astype(jnp.int32)
    slot = slots_of(ids, experts, cap)
    slot_ref[0] = jnp.broadcast_to(slot, (8, tok))
    xs_ref[0] = dot(pick_rows(slot, cap, own_expert * cap), x).astype(BF16)


def qkv_step(shards, first, places, held, w_own, gains, biases, seq_count, experts, cap):
    count, rows, width = shards.shape
    tok = rows - 16
    wide = w_own.shape[1]
    outs = [
        shape((seq_count, tok, wide), BF16),
        shape((seq_count, width, tok), BF16),
        shape((seq_count, cap, width), BF16),
        shape((seq_count, 8, tok), jnp.int32),
    ]
    spec = pltpu.PrefetchScalarGridSpec(
        num_scalar_prefetch=1,
        grid=(count,),
        in_specs=[
            pl.BlockSpec((1, rows, width), lambda i, at: (i, 0, 0)),
            whole(w_own),
            whole(gains),
            whole(biases),
        ]
        + [pl.BlockSpec(memory_space=pl.ANY)] * len(held),
        out_specs=[
            pl.BlockSpec((1,) + out.shape[1:], lambda i, at: (at[first + i], 0, 0)) for out in outs
        ],
    )
    return pl.pallas_call(
        functools.partial(qkv_kernel, experts, cap, tok, first),
        out_shape=outs,
        grid_spec=spec,
        input_output_aliases={5 + n: n for n in range(len(held))},
        compiler_params=params(),
        name="qkv_step",
        cost_estimate=cost(4),
    )(places, shards, w_own, gains, biases, *held)


def send_kernel(experts, cap, ids_ref, rows_ref, out_ref, slot_ref):
    slot = slots_of(ids_ref[0:1], experts, cap)
    slot_ref[...] = jnp.broadcast_to(slot, slot_ref.shape)
    out_ref[...] = dot(pick_rows(slot, experts * cap), rows_ref[...]).astype(BF16)


def send_rows(ids_row, rows, experts, cap):
    tok, width = rows.shape
    return pl.pallas_call(
        functools.partial(send_kernel, experts, cap),
        out_shape=[shape((experts * cap, width), BF16), shape((8, tok), jnp.int32)],
        compiler_params=params(),
        name="send_rows",
        cost_estimate=cost(3),
    )(jnp.broadcast_to(ids_row, (8, tok)), rows)


def doc_start(ends_ref, positions, docs):
    start = jnp.zeros_like(positions)
    for k in range(docs):
        start = jnp.where(ends_ref[k] <= positions, ends_ref[k], start)
    return start


def head_lanes(array, head):
    lane = lax.broadcasted_iota(jnp.int32, (1, array.shape[1]), 1)
    return jnp.where(lane // HEAD_DIM == head, array, jnp.zeros_like(array))


def attend_kernel(docs, cap, ends_ref, qkv_ref, slot_ref, send_ref, out_ref, lse_ref):
    blocks, tok, wide = qkv_ref.shape
    width = wide // 3
    heads = width // HEAD_DIM
    experts = send_ref.shape[0]
    scale = LOG2E / math.sqrt(HEAD_DIM)
    lane = lax.broadcasted_iota(jnp.int32, (tok, width), 1)

    def run(block):
        q = qkv_ref[block, :, :width]
        local = lax.broadcasted_iota(jnp.int32, (tok, 1), 0)
        start = doc_start(ends_ref, block * tok + local, docs)
        ones = jnp.ones((tok, width), BF16)
        merged = jnp.zeros((tok, width), F32)
        lse = jnp.zeros((tok, width), F32)
        for head in range(heads):
            q_head = head_lanes(q, head)
            parts = []
            for other in range(block + 1):
                s = dot(q_head, qkv_ref[other, :, width : 2 * width], 1, 1)
                column = lax.broadcasted_iota(jnp.int32, (tok, tok), 1)
                if other == block:
                    mask = (column <= local) & (column + other * tok >= start)
                    s = jnp.where(mask, s, MASKED)
                elif other == 0 or block == blocks - 1:
                    s = jnp.where(column + other * tok >= start, s, MASKED)
                parts.append(s)
            top = parts[0]
            for s in parts[1:]:
                top = jnp.maximum(top, s)
            top = jnp.max(top, axis=1, keepdims=True)
            shift = top * scale
            total = jnp.zeros((tok, 2 * width), F32)
            for other in range(block + 1):
                p = jnp.exp2(parts[other] * scale - shift).astype(BF16)
                v = jnp.concatenate([qkv_ref[other, :, 2 * width :], ones], axis=1)
                total = total + dot(p, v)
            weight = total[:, width:]
            mine = lane // HEAD_DIM == head
            merged = jnp.where(mine, total[:, :width] / weight, merged)
            lse = jnp.where(lane == head, shift + jnp.log2(weight), lse)
        out_ref[block] = merged
        lse_ref[block] = lse.T[:8]
        pick = pick_rows(slot_ref[block, 0:1], experts * cap)
        rows = dot(pick, merged.astype(BF16)).astype(BF16)
        for e in range(experts):
            send_ref[e, block] = rows[e * cap : (e + 1) * cap]

    for block in range(blocks):
        run(block)


def attend(qkv, slots, ends, cap):
    blocks, tok, wide = qkv.shape
    width = wide // 3
    return pl.pallas_call(
        functools.partial(attend_kernel, ends.shape[0], cap),
        out_shape=[
            shape((blocks, blocks, cap, width), BF16),
            shape((blocks, tok, width), F32),
            shape((blocks, 8, tok), F32),
        ],
        in_specs=[pl.BlockSpec(memory_space=pltpu.SMEM)]
        + [pl.BlockSpec(memory_space=pltpu.VMEM)] * 2,
        compiler_params=params(),
        name="attend",
        cost_estimate=cost(6),
    )(ends, qkv, slots)


def attend_back_kernel(
    docs, cap, ends_ref, qkv_ref, slot_ref, back_ref, out_ref, lse_ref, upper_ref, lower_ref, do_ref, dq_ref, delta_ref
):
    blocks, tok, wide = qkv_ref.shape
    width = wide // 3
    heads = width // HEAD_DIM
    experts = back_ref.shape[0]
    scale = LOG2E / math.sqrt(HEAD_DIM)

    for t in range(blocks):
        rows = jnp.concatenate([back_ref[e, t] for e in range(experts)], axis=0)
        do = dot(place_rows(slot_ref[t, 0:1], experts * cap), rows)
        do_ref[t] = do.astype(BF16)
        product = (do * out_ref[t]).T
        delta = jnp.zeros((8, tok), F32)
        row = lax.broadcasted_iota(jnp.int32, (8, tok), 0)
        for head in range(heads):
            part = product[head * HEAD_DIM : (head + 1) * HEAD_DIM]
            delta = jnp.where(row == head, jnp.sum(part, axis=0, keepdims=True), delta)
        delta_ref[t] = delta
        dq_ref[t] = jnp.zeros((tok, width), F32)

    def run(block):
        k = qkv_ref[block, :, width : 2 * width]
        v = qkv_ref[block, :, 2 * width :]
        k_pos = lax.broadcasted_iota(jnp.int32, (tok, tok), 0) + block * tok
        dk = jnp.zeros((tok, width), F32)
        dv = jnp.zeros((tok, width), F32)
        for other in range(block, blocks):
            q_pos = lax.broadcasted_iota(jnp.int32, (1, tok), 1) + other * tok
            start = doc_start(ends_ref, q_pos, docs)
            q = qkv_ref[other, :, :width]
            do = do_ref[other]
            dq = dq_ref[other]
            for head in range(heads):
                q_head = head_lanes(q, head)
                do_head = head_lanes(do, head)
                s = dot(k, q_head, 1, 1)
                p = jnp.exp2(s * scale - lse_ref[other, head : head + 1])
                if other == block:
                    p = jnp.where((k_pos <= q_pos) & (k_pos >= start), p, 0.0)
                elif block == 0 or other == blocks - 1:
                    p = jnp.where(k_pos >= start, p, 0.0)
                dp = dot(v, do_head, 1, 1)
                ds = (p * (dp - delta_ref[other, head : head + 1])).astype(BF16)
                dv = dv + dot(p.astype(BF16), do_head)
                dk = dk + dot(ds, q_head)
                dq = dq + dot(ds, head_lanes(k, head), 0, 0)
            dq_ref[other] = dq
        factor = 1.0 / math.sqrt(HEAD_DIM)
        for n, part in enumerate((dq_ref[block] * factor, dk * factor, dv)):
            columns = slice(n * width, (n + 1) * width)
            upper_ref[block, : tok // 2, columns] = part[: tok // 2].astype(BF16)
            lower_ref[block, :, columns] = part[tok // 2 :].astype(BF16)

    for block in range(blocks):
        run(block)


def attend_back(qkv, slots, back, out, lse, ends, cap):
    blocks, tok, wide = qkv.shape
    width = wide // 3
    return pl.pallas_call(
        functools.partial(attend_back_kernel, ends.shape[0], cap),
        out_shape=[
            shape((blocks, tok // 2 + 3 * tok // 8, wide), BF16),
            shape((blocks, tok // 2, wide), BF16),
        ],
        in_specs=[pl.BlockSpec(memory_space=pltpu.SMEM)]
        + [pl.BlockSpec(memory_space=pltpu.VMEM)] * 5,
        scratch_shapes=[
            pltpu.VMEM((blocks, tok, width), BF16),
            pltpu.VMEM((blocks, tok, width), F32),
            pltpu.VMEM((blocks, 8, tok), F32),
        ],
        compiler_params=params(),
        name="attend_back",
        cost_estimate=cost(20),
    )(ends, qkv, slots, back, out, lse)


def pick_all(slots, count):
    return (slots[:, :1, :] == jnp.arange(count, dtype=jnp.int32)[None, :, None]).astype(BF16)


def long_masks(ends, first, tok, length):
    q_pos = first + jnp.arange(tok, dtype=jnp.int32)
    k_pos = jnp.arange(length, dtype=jnp.int32)
    start = jnp.max(jnp.where(ends[None, :] <= q_pos[:, None], ends[None, :], 0), axis=1)
    return (k_pos[None, :] <= q_pos[:, None]) & (k_pos[None, :] >= start[:, None])


def long_heads(rows, width):
    return rows.reshape(rows.shape[0], width // HEAD_DIM, HEAD_DIM).transpose(1, 0, 2)


def attend_long(qkv, slots, ends, cap):
    blocks, tok, wide = qkv.shape
    width = wide // 3
    length = blocks * tok
    flat = qkv.reshape(length, wide)
    keys = long_heads(flat[:, width : 2 * width], width)
    values = long_heads(flat[:, 2 * width :], width)

    def one(block):
        query = long_heads(qkv[block, :, :width], width)
        mask = long_masks(ends, block * tok, tok, length)
        s = jnp.einsum("hqd,hkd->hqk", query, keys, preferred_element_type=F32)
        s = jnp.where(mask, s / math.sqrt(HEAD_DIM), MASKED)
        top = jnp.max(s, axis=-1, keepdims=True)
        weights = jnp.where(mask, jnp.exp(s - top), 0.0)
        total = jnp.sum(weights, axis=-1, keepdims=True)
        out = jnp.einsum("hqk,hkd->hqd", (weights / total).astype(BF16), values, preferred_element_type=F32)
        return out.transpose(1, 0, 2).reshape(tok, width), (top + jnp.log(total))[:, :, 0]

    out, lse = lax.map(one, jnp.arange(blocks, dtype=jnp.int32))
    pick = pick_all(slots, blocks * cap)
    rows = jnp.einsum("tsk,tkd->tsd", pick, out.astype(BF16), preferred_element_type=F32)
    send = rows.astype(BF16).reshape(blocks, blocks, cap, width).transpose(1, 0, 2, 3)
    return send, out, lse


def attend_back_long(qkv, slots, back, out, lse, ends, cap):
    blocks, tok, wide = qkv.shape
    width = wide // 3
    length = blocks * tok
    heads = width // HEAD_DIM
    flat = qkv.reshape(length, wide)
    keys = long_heads(flat[:, width : 2 * width], width)
    values = long_heads(flat[:, 2 * width :], width)
    pick = pick_all(slots, blocks * cap)
    rows = back.transpose(1, 0, 2, 3).reshape(blocks, blocks * cap, width)
    do_all = jnp.einsum("tsk,tsd->tkd", pick, rows, preferred_element_type=F32)

    def one(sums, block):
        query = long_heads(qkv[block, :, :width], width)
        mask = long_masks(ends, block * tok, tok, length)
        do = do_all[block]
        delta = jnp.sum((do * out[block]).reshape(tok, heads, HEAD_DIM), axis=-1).T
        do = long_heads(do.astype(BF16), width)
        s = jnp.einsum("hqd,hkd->hqk", query, keys, preferred_element_type=F32)
        p = jnp.where(mask, jnp.exp(s / math.sqrt(HEAD_DIM) - lse[block][:, :, None]), 0.0)
        dp = jnp.einsum("hqd,hkd->hqk", do, values, preferred_element_type=F32)
        ds = (p * (dp - delta[:, :, None]) / math.sqrt(HEAD_DIM)).astype(BF16)
        dq = jnp.einsum("hqk,hkd->qhd", ds, keys, preferred_element_type=F32)
        dk = jnp.einsum("hqk,hqd->khd", ds, query, preferred_element_type=F32)
        dv = jnp.einsum("hqk,hqd->khd", p.astype(BF16), do, preferred_element_type=F32)
        sums = (sums[0] + dk.reshape(length, width), sums[1] + dv.reshape(length, width))
        return sums, dq.reshape(tok, width)

    start = jnp.zeros((length, width), F32)
    (dk, dv), dq = lax.scan(one, (start, start), jnp.arange(blocks, dtype=jnp.int32))
    grad = jnp.concatenate([dq.reshape(length, width), dk, dv], axis=1).astype(BF16)
    grad = grad.reshape(blocks, 2, tok // 2, wide)
    return grad[:, 0], grad[:, 1]


EXPERT_PART = 512


def expert_kernel(
    att_ref, xs_ref, g_ref, w_out_ref, gain_ref, bias_ref, w1_any, w2_any,
    datt_ref, branch_ref, sums_ref, ein_any, mid_any, active_any,
    w1_ref, w2_ref, ein_ref, mid_ref, active_ref, dpre_ref, in_sems, out_sems,
):
    groups, rows, width = att_ref.shape
    parts = [pl.ds(n, EXPERT_PART) for n in range(0, w1_ref.shape[1], EXPERT_PART)]
    loads = []
    for n, part in enumerate(parts):
        loads.append(
            (
                pltpu.make_async_copy(w1_any.at[0, :, part], w1_ref.at[:, part], in_sems.at[0, n]),
                pltpu.make_async_copy(w2_any.at[0, part], w2_ref.at[part], in_sems.at[1, n]),
            )
        )
        for load in loads[n]:
            load.start()
    stores = []

    def store(source, target):
        copy = pltpu.make_async_copy(source, target, out_sems.at[len(stores)])
        copy.start()
        stores.append(copy)

    att = jnp.concatenate([att_ref[n] for n in range(groups)], axis=1)
    mid = xs_ref[...].astype(F32) + dot(att, w_out_ref[...])
    mid_ref[...] = mid
    store(mid_ref, mid_any)
    unit, inv_std = norm_parts(mid)
    ein = (unit * gain_ref[1:2] + bias_ref[1:2]).astype(BF16)
    ein_ref[...] = ein
    store(ein_ref, ein_any)
    g = g_ref[...]
    for n, part in enumerate(parts):
        for load in loads[n]:
            load.wait()
        pre = dot(ein, w1_ref[:, part])
        d_active = dot(g, w2_ref[part], 1, 1)
        active, slope = gelu_both(pre)
        active_ref[:, part] = active.astype(BF16)
        store(active_ref.at[:, part], active_any.at[:, part])
        dpre_ref[:, part] = (d_active * slope).astype(BF16)
    d_in = dot(dpre_ref[...], w1_ref[...], 1, 1).astype(BF16).astype(F32)
    d_mid = g.astype(F32) + norm_back(d_in * gain_ref[1:2], unit, inv_std)
    branch = d_mid.astype(BF16)
    branch_ref[...] = branch
    d_att = dot(branch, w_out_ref[...], 1, 1).astype(BF16)
    for n in range(groups):
        datt_ref[n] = d_att[:, n * width : (n + 1) * width]
    sums_ref[...] = jnp.zeros_like(sums_ref)
    sums_ref[0:1] = jnp.sum(d_in * unit, axis=0, keepdims=True)
    sums_ref[1:2] = jnp.sum(d_in, axis=0, keepdims=True)
    for copy in stores:
        copy.wait()


def expert(att, xs, grads, w_out, gains, biases, w_in, w_exp_out):
    groups, rows, width = att.shape
    wide = xs.shape[1]
    hidden = w_in.shape[2]
    count = hidden // EXPERT_PART
    vmem = pl.BlockSpec(memory_space=pltpu.VMEM)
    hbm = pl.BlockSpec(memory_space=pl.ANY)
    return pl.pallas_call(
        expert_kernel,
        out_shape=[
            shape(att.shape, BF16),
            shape((rows, wide), BF16),
            shape((8, wide), F32),
            shape((rows, wide), BF16),
            shape((rows, wide), F32),
            shape((rows, hidden), BF16),
        ],
        in_specs=[vmem] * 6 + [hbm] * 2,
        out_specs=[vmem] * 3 + [hbm] * 3,
        scratch_shapes=[
            pltpu.VMEM((wide, hidden), BF16),
            pltpu.VMEM((hidden, wide), BF16),
            pltpu.VMEM((rows, wide), BF16),
            pltpu.VMEM((rows, wide), F32),
            pltpu.VMEM((rows, hidden), BF16),
            pltpu.VMEM((rows, hidden), BF16),
            pltpu.SemaphoreType.DMA((2, count)),
            pltpu.SemaphoreType.DMA((count + 2,)),
        ],
        compiler_params=params(),
        name="expert",
        cost_estimate=cost(18),
    )(att, xs, grads, w_out, gains, biases, w_in, w_exp_out)


def made_kernel(active_ref, w2_ref, mid_ref, branch_ref, back_ref, sum_ref):
    step = pl.program_id(0)
    term = dot(active_ref[...], w2_ref[0])

    @pl.when(step == 0)
    def first():
        sum_ref[...] = term

    @pl.when(step > 0)
    def later():
        sum_ref[...] += term

    @pl.when(step == pl.num_programs(0) - 1)
    def last():
        made = (mid_ref[...] + sum_ref[...].astype(BF16).astype(F32)).astype(BF16)
        seq_count = back_ref.shape[0]
        cap = made.shape[0] // seq_count
        for t in range(seq_count):
            back_ref[t, :cap] = made[t * cap : (t + 1) * cap]
            back_ref[t, cap : 2 * cap] = branch_ref[t * cap : (t + 1) * cap]


def expert_made(active, w_exp_out, mid, branch, seq_count):
    rows, hidden = active.shape
    wide = mid.shape[1]
    part = 1024
    out = shape((seq_count, 2 * rows // seq_count, wide), BF16)
    return pl.pallas_call(
        made_kernel,
        out_shape=out,
        grid=(hidden // part,),
        in_specs=[
            pl.BlockSpec((rows, part), lambda i: (0, i)),
            pl.BlockSpec((1, part, wide), lambda i: (0, i, 0)),
            whole(mid),
            whole(branch),
        ],
        out_specs=whole(out),
        scratch_shapes=[pltpu.VMEM((rows, wide), F32)],
        compiler_params=params(),
        name="expert_made",
        cost_estimate=cost(0.2),
    )(active, w_exp_out, mid, branch)


def weights_kernel(count, place, *refs):
    xs, gs = refs[:count], refs[count : 2 * count]
    w1_ref, w2_ref = refs[2 * count : 2 * count + 2]
    d1_ref, d2_ref, turned_ref = refs[-3:]

    @pl.when(pl.program_id(0) == 0)
    def begin():
        for n in range(count):
            turned_ref[n] = xs[n][...].T

    w1 = w1_ref[0]
    w2 = w2_ref[0]
    d1 = jnp.zeros(d1_ref.shape[1:], F32)
    d2 = jnp.zeros(d2_ref.shape[1:], F32)
    for n in range(count):
        g = gs[n][...]
        pre = dot(xs[n][...], w1)
        d_active = dot(g, w2, 1, 1)
        active, slope = gelu_both(pre)
        d1 = d1 + dot(turned_ref[n], (d_active * slope).astype(BF16))
        d2 = d2 + dot(active.astype(BF16), g, 0, 0)
    d1_ref[0] = d1
    d2_ref[0] = d2


def expert_weights(rows, grads, w_in, w_exp_out, place, half, held):
    parts = len(rows)
    count, wide = rows[0].shape
    hidden = w_in.shape[2] // parts
    part = 256
    steps = hidden // part
    first = half * steps // 2
    spec = pltpu.PrefetchScalarGridSpec(
        num_scalar_prefetch=1,
        grid=(steps // 2,),
        in_specs=[whole(a) for a in (*rows, *grads)]
        + [
            pl.BlockSpec((1, wide, part), lambda i, at: (0, 0, at[0] * steps + first + i)),
            pl.BlockSpec((1, part, wide), lambda i, at: (0, at[0] * steps + first + i, 0)),
        ]
        + [pl.BlockSpec(memory_space=pl.ANY)] * len(held),
        out_specs=[
            pl.BlockSpec((1, wide, part), lambda i, at: (0, 0, first + i)),
            pl.BlockSpec((1, part, wide), lambda i, at: (0, first + i, 0)),
        ],
        scratch_shapes=[pltpu.VMEM((parts, wide, count), BF16)],
    )
    return pl.pallas_call(
        functools.partial(weights_kernel, parts),
        out_shape=[shape((1, wide, hidden), F32), shape((1, hidden, wide), F32)],
        grid_spec=spec,
        input_output_aliases={3 + 2 * parts + n: n for n in range(len(held))},
        compiler_params=params(),
        name="expert_weights",
        cost_estimate=cost(3),
    )(place[None].astype(jnp.int32), *rows, *grads, w_in, w_exp_out, *held)


def out_weights_kernel(ranks_ref, att_ref, branch_ref, send_ref, keep_ref, made_ref):
    groups, unused, width = att_ref.shape
    parts, wide, part = made_ref.shape
    for n in range(groups):
        lines = slice(n * width, (n + 1) * width)
        term = dot(att_ref[n], branch_ref[...], 0, 0).astype(BF16)
        for p in range(parts):
            made_ref[p, lines] = term[:, p * part : (p + 1) * part]
    for n, (ref, slot) in enumerate(((send_ref, 0), (send_ref, 1), (keep_ref, 0), (keep_ref, 1))):
        ref[slot] = made_ref[ranks_ref[n]]


def out_weights(ranks, att, branch):
    wide = branch.shape[1]
    part = wide // 4
    return pl.pallas_call(
        out_weights_kernel,
        out_shape=[shape((2, wide, part), BF16)] * 2,
        in_specs=[pl.BlockSpec(memory_space=pltpu.SMEM)]
        + [pl.BlockSpec(memory_space=pltpu.VMEM)] * 2,
        scratch_shapes=[pltpu.VMEM((4, wide, part), BF16)],
        compiler_params=params(),
        name="out_weights",
        cost_estimate=cost(1),
    )(ranks, att, branch)


def add_kernel(keep_ref, got_ref, out_ref):
    out_ref[...] = (keep_ref[1].astype(F32) + got_ref[1].astype(F32)).astype(BF16)


def add_theirs(keep, got):
    return pl.pallas_call(
        add_kernel,
        out_shape=shape(keep.shape[1:], BF16),
        in_specs=[pl.BlockSpec(memory_space=pltpu.VMEM)] * 2,
        compiler_params=params(),
        name="add_theirs",
        cost_estimate=cost(0.2),
    )(keep, got)


def sum_of(keep_ref, got_ref, far_ref):
    return keep_ref[0].astype(F32) + got_ref[0].astype(F32) + far_ref[...].astype(F32)


def spare_rows(rows, part, wide):
    spare = 3 * rows // 4
    return spare, rows - spare, wide - part, part // (wide - part)


def join_kernel(keep_ref, got_ref, far_ref, *refs):
    total = sum_of(keep_ref, got_ref, far_ref).astype(BF16)
    outs = refs[1:]
    count, lines, wide = outs[0].shape
    rows, part = total.shape[0] // count, total.shape[1]
    spare, rest, side, folds = spare_rows(rows, part, wide)
    for t in range(count):
        piece = total[t * rows : (t + 1) * rows]
        full = jnp.concatenate(
            [piece[spare:, n * side : (n + 1) * side] for n in range(folds)]
            + [jnp.zeros((spare - folds * rest, side), BF16)],
            axis=0,
        )
        outs[0][t] = jnp.concatenate([piece[:spare], full], axis=1)


def join_sum(keep, got, far, held):
    count, rows, wide = held.shape
    spare = spare_rows(far.shape[0] // count, far.shape[1], wide)[0]
    return pl.pallas_call(
        join_kernel,
        out_shape=shape(held.shape, BF16),
        grid=(1,),
        in_specs=[whole(a) for a in (keep, got, far)] + [pl.BlockSpec(memory_space=pl.ANY)],
        out_specs=pl.BlockSpec(
            (pl.Element(count), pl.Element(spare), pl.Element(wide)), lambda i: (0, rows - spare, 0)
        ),
        input_output_aliases={3: 0},
        compiler_params=params(),
        name="join_sum",
        cost_estimate=cost(1),
    )(keep, got, far, held)


def qkv_weights_kernel(
    pick_ref, unit_ref, upper_ref, lower_ref, w_ref, gain_ref, bias_ref, two_ref, send_ref, keep_ref, cols_ref, sums_ref
):
    blocks = unit_ref.shape[0]
    parts, wide, width = cols_ref.shape
    moment = jnp.zeros((wide, parts * width), F32)
    total = jnp.zeros((1, parts * width), F32)
    for t in range(blocks):
        grad = jnp.concatenate([upper_ref[t, : lower_ref.shape[1]], lower_ref[t]], axis=0)
        moment = moment + dot(unit_ref[t], grad)
        total = total + jnp.sum(grad.astype(F32), axis=0, keepdims=True)
    gain = jnp.broadcast_to(gain_ref[0:1], (128, wide)).T[:, :1]
    bias = jnp.broadcast_to(bias_ref[0:1], (128, wide)).T[:, :1]
    made = moment * gain + bias * total
    for p in range(parts):
        cols_ref[p] = made[:, p * width : (p + 1) * width].astype(BF16)
    w = w_ref[...].astype(F32)
    d_gain = jnp.sum(w * moment, axis=1, keepdims=True)
    d_bias = jnp.sum(w * total, axis=1, keepdims=True)
    lane = lax.broadcasted_iota(jnp.int32, (wide, 128), 1)
    one = jnp.where(lane == 0, d_gain, jnp.where(lane == 1, d_bias, 0.0)).T[:8]
    row = lax.broadcasted_iota(jnp.int32, one.shape, 0)
    two = two_ref[...]
    all_sums = jnp.where(row == 0, one[0:1], jnp.where(row == 1, two[0:1], jnp.where(row == 2, one[1:2], two[1:2])))
    part = wide // 4
    for n in range(4):
        for line in range(part // 128):
            at = n * part + line * 128
            sums_ref[n, line] = all_sums[:, at : at + 128]
    for n, (ref, slot) in enumerate(((send_ref, 0), (send_ref, 1), (keep_ref, 0), (keep_ref, 1))):
        cols = cols_ref[pick_ref[4 + n]]
        ref[slot, :wide] = cols * pick_ref[8 + n].astype(F32).astype(BF16)
        lines = [sums_ref[pick_ref[n], line] for line in range(part // 128)]
        ref[slot, wide:] = jnp.concatenate(lines, axis=0).astype(BF16)


def qkv_weights(pick, unit, grads, w_own, gains, biases, sums_two):
    blocks, wide, tok = unit.shape
    width = w_own.shape[1] // 3
    lines = 8 * (wide // 4 // 128)
    outs = [shape((2, wide + lines, width), BF16)] * 2
    if width % 128 != 0:
        grad = jnp.concatenate(grads, axis=1)
        moment = jnp.einsum("tdk,tkf->df", unit, grad, preferred_element_type=F32)
        total = jnp.sum(grad.astype(F32), axis=(0, 1))
        made = moment * gains[0][:, None] + biases[0][:, None] * total[None, :]
        made = made.astype(BF16).reshape(wide, 3, width).transpose(1, 0, 2)
        w = w_own.astype(F32)
        copies = lax.axis_size("seq") * width // wide
        sums = jnp.stack(
            [
                jnp.sum(w * moment, axis=1) / copies,
                sums_two[0],
                jnp.sum(w * total[None, :], axis=1) / copies,
                sums_two[1],
            ]
        ).astype(BF16)
        terms = []
        for n in range(4):
            cols = made[pick[4 + n]] * pick[8 + n].astype(BF16)
            norms = lax.dynamic_slice_in_dim(sums, pick[n] * (wide // 4), wide // 4, 1)
            norms = norms.reshape(4, -1, 128).transpose(1, 0, 2)
            norms = jnp.pad(norms, ((0, 0), (0, 4), (0, 0))).reshape(-1, width)
            terms.append(jnp.concatenate([cols, norms], axis=0))
        return jnp.stack(terms[:2]), jnp.stack(terms[2:])
    return pl.pallas_call(
        qkv_weights_kernel,
        out_shape=outs,
        in_specs=[pl.BlockSpec(memory_space=pltpu.SMEM)]
        + [pl.BlockSpec(memory_space=pltpu.VMEM)] * 7,
        scratch_shapes=[
            pltpu.VMEM((3, wide, width), BF16),
            pltpu.VMEM((4, wide // 4 // 128, 8, 128), F32),
        ],
        compiler_params=params(),
        name="qkv_weights",
        cost_estimate=cost(4),
    )(pick, unit, *grads, w_own, gains, biases, sums_two)


def bundle_kernel(keep_ref, got_ref, far_ref, joined_ref, out_ref):
    rows, width = far_ref.shape
    out_ref[:rows] = sum_of(keep_ref, got_ref, far_ref).astype(BF16)
    total = joined_ref[0].astype(F32)
    for n in range(1, joined_ref.shape[0]):
        total = total + joined_ref[n].astype(F32)
    total = total.astype(BF16)
    spare, wide = total.shape
    lines = spare * 4 // 3
    spare, rest, side, folds = spare_rows(lines, folds_of(wide), wide)
    for half in range(folds):
        first = rows + half * lines
        out_ref[first : first + spare] = total[:, half * width : (half + 1) * width]
        out_ref[first + spare : first + lines] = total[half * rest : (half + 1) * rest, wide - side :]


def folds_of(wide):
    return 2 * wide // 3


def bundle(keep, got, far, joined):
    rows, width = far.shape
    count, held, wide = joined.shape
    spare = held - held * 4 // 7
    lines = spare * 4 // 3
    out = shape((rows + lines * folds_of(wide) // width, width), BF16)
    return pl.pallas_call(
        bundle_kernel,
        out_shape=out,
        grid=(1,),
        in_specs=[whole(a) for a in (keep, got, far)]
        + [
            pl.BlockSpec(
                (pl.Element(count), pl.Element(spare), pl.Element(wide)), lambda i: (0, held - spare, 0)
            )
        ],
        out_specs=whole(out),
        compiler_params=params(),
        name="bundle",
        cost_estimate=cost(1),
    )(keep, got, far, joined)


def columns_kernel(rows, place, *refs):
    out_ref, d_out_ref, sums_ref = refs[-3:]
    froms = refs[:-3]
    wide = out_ref.shape[0]
    width = froms[0].shape[1]
    lines = wide // len(froms)
    total = jnp.zeros(sums_ref.shape, F32)
    for n, from_ref in enumerate(froms):

        @pl.when(place[n] < out_ref.shape[1] // width)
        def columns_of(n=n, from_ref=from_ref):
            first = pl.multiple_of(place[n] * width, width)
            out_ref[:, pl.ds(first, width)] = from_ref[:wide].astype(F32)

        total = total + from_ref[wide:rows].astype(F32)
        at = pl.ds(pl.multiple_of(place[len(froms) + n] * lines, lines), lines)
        for half in range(d_out_ref.shape[1] // width):
            first = rows + half * lines
            d_out_ref[at, half * width : (half + 1) * width] = from_ref[first : first + lines].astype(F32)
    sums_ref[...] = total


def columns(froms, place, rows, wide, part):
    width = froms[0].shape[1]
    return pl.pallas_call(
        functools.partial(columns_kernel, rows),
        out_shape=[
            shape((wide, 3 * part), F32),
            shape((wide, part), F32),
            shape((rows - wide, width), F32),
        ],
        in_specs=[pl.BlockSpec(memory_space=pltpu.SMEM)]
        + [pl.BlockSpec(memory_space=pltpu.VMEM)] * len(froms),
        compiler_params=params(),
        name="columns",
        cost_estimate=cost(0.2),
    )(place.astype(jnp.int32), *froms)


def place_kernel(cap, slot_ref, back_ref, out_ref, mid_ref):
    experts = back_ref.shape[0]
    place = place_rows(slot_ref[0:1], experts * cap)
    made = jnp.concatenate([back_ref[e, :cap] for e in range(experts)], axis=0)
    out_ref[0] = dot(place, made).astype(BF16)
    branch = jnp.concatenate([back_ref[e, cap : 2 * cap] for e in range(experts)], axis=0)
    mid_ref[...] = dot(place, branch).astype(BF16)


def place_back(slots, back, cap):
    tok, wide = slots.shape[1], back.shape[2]
    return pl.pallas_call(
        functools.partial(place_kernel, cap),
        out_shape=[shape((1, tok, wide), BF16), shape((tok, wide), BF16)],
        compiler_params=params(),
        name="place_back",
        cost_estimate=cost(0.5),
    )(slots, back)


def finish_kernel(x_ref, grad_ref, w_ref, gain_ref, mid_ref, *refs):
    dx_ref, sum_ref = refs[-2:]
    step = pl.program_id(0)
    groups, tok, wide = grad_ref.shape
    width = wide // 3

    def part(p):
        at = p * width
        return jnp.concatenate([grad_ref[n, :, at : at + width] for n in range(groups)], axis=1)

    @pl.when(step == 0)
    def first():
        sum_ref[...] = dot(part(0), w_ref[...], 1, 1)

    @pl.when(step == 1)
    def second():
        sum_ref[...] += dot(part(1), w_ref[...], 1, 1)

    @pl.when(step == 2)
    def last():
        d_normed = sum_ref[...] + dot(part(2), w_ref[...], 1, 1)
        unit, inv_std = norm_parts(x_ref[...].astype(F32))
        dx_ref[0] = mid_ref[...].astype(F32) + norm_back(d_normed * gain_ref[0:1], unit, inv_std)


def finish(x, grad, w_qkv, gains, d_mid, half, held):
    tok, wide = x.shape
    rows = pl.BlockSpec((tok // 2, wide), lambda i: (half, 0))
    return pl.pallas_call(
        finish_kernel,
        out_shape=[shape((1, tok, wide), F32)],
        grid=(3,),
        in_specs=[
            rows,
            pl.BlockSpec((grad.shape[0], tok // 2, grad.shape[2]), lambda i: (0, 0, 0)),
            pl.BlockSpec((wide, wide), lambda i: (0, i)),
            whole(gains),
            rows,
        ]
        + [pl.BlockSpec(memory_space=pl.ANY)] * len(held),
        out_specs=[pl.BlockSpec((1, tok // 2, wide), lambda i: (0, half, 0))],
        scratch_shapes=[pltpu.VMEM((tok // 2, wide), F32)],
        input_output_aliases={5 + n: n for n in range(len(held))},
        compiler_params=params(),
        name="finish",
        cost_estimate=cost(4),
    )(x, grad, w_qkv, gains, d_mid, *held)


WALK = (0, 2, 4, 6, 7, 5, 3, 1)


def walk_pairs(way):
    return [(WALK[n], WALK[(n + way) % len(WALK)]) for n in range(len(WALK))]


def walk_places(at):
    hops = (0, 1, -1, 2, -2, 3, -3, 4)
    table = [[0] * len(hops) for unused in WALK]
    for n, device in enumerate(WALK):
        table[device] = [WALK[(n - hop) % len(WALK)] for hop in hops]
    return jnp.asarray(table, jnp.int32)[at]


def gather_steps(own, seq_count, done=lambda: ()):
    if seq_count != len(WALK):
        yield lax.all_gather(own, "seq")
        return
    yield own[None]
    ahead = behind = own
    half = own.shape[0] // 2
    for unused in range(3):
        before = done()
        ahead = lax.ppermute(after(ahead, *before), "seq", walk_pairs(1))
        behind = lax.ppermute(after(behind, *before), "seq", walk_pairs(-1))
        yield ahead[None]
        yield behind[None]
    before = done()
    top = lax.ppermute(after(ahead[:half], *before), "seq", walk_pairs(1))
    low = lax.ppermute(after(behind[half:], *before), "seq", walk_pairs(-1))
    yield jnp.concatenate([top, low], axis=0)[None]


def after(value, *others):
    return lax.optimization_barrier((value,) + others)[0]


def swap(x):
    return lax.all_to_all(x, "seq", split_axis=0, concat_axis=0, tiled=True)


def flip_pairs(count, bit):
    return [(n, n ^ bit) for n in range(count)]


def gather_batch(own, count):
    far = lax.ppermute(own, "batch", flip_pairs(count, 2))
    near = lax.ppermute(own, "batch", flip_pairs(count, 1))
    return own, far, near, lax.ppermute(far, "batch", flip_pairs(count, 1))


def sum_batch(send, keep, count):
    got = lax.ppermute(send, "batch", flip_pairs(count, 1))
    far = lax.ppermute(add_theirs(keep, got), "batch", flip_pairs(count, 2))
    return keep, got, far


def on_device(tokens, w_qkv, w_out, w_in, w_exp_out, gains, biases, lengths, hash_ids, cotangent):
    tok, width = tokens.shape[1:]
    seq_count = lax.axis_size("seq")
    batch_count = lax.axis_size("batch")
    at = lax.axis_index("seq")
    row = lax.axis_index("batch")
    groups = min(HEADS, seq_count)
    copies = seq_count // groups
    group = at // copies
    own = width // groups
    experts = seq_count
    slot_cap = max(2, 3 * tok // (2 * experts))
    cap = -(-slot_cap // 16) * 16
    x = tokens[0]
    ends = jnp.cumsum(lengths[0]).astype(jnp.int32)
    ids_row = hash_ids[0, :, 0][None, :]

    ids_rows = jnp.broadcast_to(jnp.pad(ids_row.astype(BF16), ((0, 0), (0, width - tok))), (16, width))
    load = jnp.concatenate([x, ids_rows], axis=0)
    w_own = jnp.concatenate(
        [lax.dynamic_slice_in_dim(w_qkv, n * width + group * own, own, 1) for n in range(3)], axis=1
    )
    if seq_count == len(WALK):
        order = walk_places(at)
    else:
        order = jnp.concatenate([at[None], jnp.arange(seq_count, dtype=jnp.int32)])
    held = ()
    older = ()
    arrived = []
    for shards in gather_steps(load, seq_count, lambda: older):
        first = len(arrived) if seq_count == len(WALK) else 1
        if len(arrived) % 2 == 1:
            older = held[3:]
        held = qkv_step(shards, first, order, held, w_own, gains, biases, seq_count, experts, cap)
        arrived.append(shards)
    qkv, unit, xs, slots = held

    cot = after(cotangent[0], arrived[-1])
    grad_rows, own_slots = send_rows(ids_row, cot, experts, cap)
    grads = swap(grad_rows.reshape(experts, cap, width)).reshape(seq_count * cap, width)

    long_rows = own % 128 != 0 or seq_count > 8
    send, att_out, lse = (attend_long if long_rows else attend)(qkv, slots, ends, cap)
    share = seq_count // copies
    if copies > 1:
        send = lax.dynamic_slice_in_dim(send, (at % copies) * share, share, 1)
    got = swap(send).reshape(groups, seq_count * cap, own)
    slot_rows = seq_count * cap
    if own % 128 != 0:
        att = got.transpose(1, 0, 2).reshape(1, slot_rows, width)
    else:
        att = got
    all_grads = gather_batch(grads, batch_count)
    part = width // batch_count
    d_att, branch, sums_two, expert_in, mid, active = expert(
        after(att, *all_grads), xs.reshape(slot_rows, width), grads, w_out, gains, biases, w_in, w_exp_out
    )
    back = expert_made(active, w_exp_out, mid, branch, seq_count)
    if own % 128 != 0:
        d_att = d_att.reshape(slot_rows, groups, own).transpose(1, 0, 2)
    if copies > 1:
        d_att = jnp.repeat(d_att, copies, axis=0)
    d_att = swap(d_att).reshape(experts, seq_count, cap, own)


    ranks = row ^ jnp.asarray((1, 3, 0, 2), jnp.int32)
    out_terms = sum_batch(*out_weights(ranks, att, branch), batch_count)
    out_far = after(out_terms[2], back)
    all_rows = gather_batch(after(expert_in, out_far), batch_count)
    back = swap(after(back, d_att))

    d_att = after(d_att, out_far)
    d_qkv = (attend_back_long if long_rows else attend_back)(qkv, slots, d_att, att_out, lse, ends, cap)
    d_qkv = [after(grad, all_rows[1]) for grad in d_qkv]

    per_row = 3 * groups // batch_count
    blocks = (ranks * per_row - group + groups - 1) // groups
    fits = (blocks < 3) & (blocks * groups + group < (ranks + 1) * per_row)
    pick = jnp.concatenate([ranks, jnp.minimum(blocks, 2), fits.astype(jnp.int32)]).astype(jnp.int32)
    send, keep = qkv_weights(pick, unit, d_qkv, w_own, gains, biases, sums_two)
    terms = sum_batch(send, keep, batch_count)
    d_weights = expert_weights(all_rows, all_grads, w_in, w_exp_out, row, 0, ())
    output, d_mid = place_back(own_slots, back, cap)

    def own_rows(grad):
        grad = swap(grad).reshape(groups, copies, -1, 3 * own)[:, 0]
        if own % 128 != 0:
            grad = grad.reshape(groups, tok // 2, 3, own).transpose(1, 2, 0, 3)
            grad = grad.reshape(1, tok // 2, 3 * width)
        return grad

    upper = d_qkv[0]
    if seq_count == len(WALK):
        upper = join_sum(*out_terms[:2], out_far, upper)
    else:
        d_out = lax.psum(sum_of(*out_terms).astype(BF16), "seq").astype(F32)
    upper = own_rows(after(upper, back, keep))
    lower = own_rows(after(d_qkv[1], upper, d_weights[0], d_mid))
    d_weights = [after(part, upper) for part in d_weights]
    d_w_in, d_w_exp_out = expert_weights(all_rows, all_grads, w_in, w_exp_out, row, 1, d_weights)
    held = finish(x, upper, w_qkv, gains, d_mid, 0, ())
    (d_tokens,) = finish(x, lower, w_qkv, gains, d_mid, 1, held)

    rows = send.shape[1]
    if seq_count == len(WALK):
        waits = iter([(), (d_w_in,), (), (lower,)])
        froms = [a[0] for a in gather_steps(bundle(*terms, upper), seq_count, lambda: next(waits))]
        place = jnp.concatenate([(order - row * per_row) % groups, order])
        d_w_qkv, d_w_out, norms = columns(froms, place, rows, width, part)
    else:
        mine = sum_of(*terms).astype(BF16)
        gathered = lax.all_gather(mine, "seq")
        d_w_out = d_out
        picked = (row * per_row + jnp.arange(per_row, dtype=jnp.int32)) % groups * copies
        cols = jnp.take(gathered[:, :width], picked, axis=0)
        d_w_qkv = cols.transpose(1, 0, 2).reshape(width, per_row * own).astype(F32)
        norms = jnp.sum(gathered[:, width:].astype(F32), axis=0)
    norms = norms.reshape(-1, 8, 128)[:, :4].transpose(1, 0, 2).reshape(4, part)
    return output, d_tokens, d_w_qkv, d_w_out, d_w_in, d_w_exp_out, norms[:2], norms[2:]


def solution(mesh):
    return jax.shard_map(
        on_device,
        mesh=mesh,
        in_specs=(
            P("batch", "seq", None),
            P(),
            P(),
            P("seq", None, None),
            P("seq", None, None),
            P(),
            P(),
            P("batch", None),
            P("batch", "seq", None),
            P("batch", "seq", None),
        ),
        out_specs=(
            P("batch", "seq", None),
            P("batch", "seq", None),
            P(None, "batch"),
            P(None, "batch"),
            P("seq", None, "batch"),
            P("seq", "batch", None),
            P(None, "batch"),
            P(None, "batch"),
        ),
        check_vma=False,
    )
```

```python
import functools
import math

import jax
import jax.numpy as jnp
from jax import lax
from jax.experimental import pallas as pl
from jax.experimental.pallas import tpu as pltpu
from jax.sharding import PartitionSpec as P

HEADS = 16
HEAD_DIM = 64
NORM_EPS = 1e-05
MASKED = -1e30
LOG2E = 1.4426950408889634
F32 = jnp.float32
BF16 = jnp.bfloat16
VMEM_BYTES = 56 * 1024 * 1024


def dot(a, b, ca=1, cb=0):
    return lax.dot_general(a, b, (((ca,), (cb,)), ((), ())), preferred_element_type=F32)


def cost(time_us):
    return pl.CostEstimate(flops=int(time_us * 1e9), bytes_accessed=int(time_us * 3e6), transcendentals=0)


def params():
    return pltpu.CompilerParams(vmem_limit_bytes=VMEM_BYTES)


def shape(dims, kind):
    return jax.ShapeDtypeStruct(dims, kind)


def norm_parts(rows):
    row_mean = jnp.mean(rows, axis=-1, keepdims=True)
    centred = rows - row_mean
    row_var = jnp.mean(centred * centred, axis=-1, keepdims=True)
    inv_std = lax.rsqrt(row_var + NORM_EPS)
    return centred * inv_std, inv_std


def norm_back(scaled, unit_rows, inv_std):
    centred = scaled - jnp.mean(scaled, axis=-1, keepdims=True)
    centred = centred - unit_rows * jnp.mean(scaled * unit_rows, axis=-1, keepdims=True)
    return centred * inv_std


def gelu_both(pre):
    cdf = 0.5 + 0.5 * lax.erf(pre * 0.7071067811865476)
    density = jnp.exp(-0.5 * pre * pre) * 0.3989422804014327
    return pre * cdf, cdf + pre * density


def whole(array):
    rank = len(array.shape)
    return pl.BlockSpec(array.shape, lambda *unused: (0,) * rank)


def slots_of(ids_row, experts, cap):
    count = ids_row.shape[1]
    members = (lax.broadcasted_iota(jnp.int32, (experts, count), 0) == ids_row).astype(F32)
    order = lax.broadcasted_iota(jnp.int32, (count, count), 0) <= lax.broadcasted_iota(
        jnp.int32, (count, count), 1
    )
    ranks = dot(members.astype(BF16), order.astype(BF16))
    rank = jnp.sum(members * ranks, axis=0, keepdims=True).astype(jnp.int32) - 1
    return ids_row * cap + rank


def pick_rows(slot_row, count, first=0):
    rows = lax.broadcasted_iota(jnp.int32, (count, slot_row.shape[1]), 0) + first
    return (rows == slot_row).astype(BF16)


def place_rows(slot_row, count):
    tokens = slot_row.shape[1]
    column = jnp.broadcast_to(slot_row.astype(F32), (128, tokens)).T[:, :1]
    return (lax.broadcasted_iota(jnp.int32, (tokens, count), 1).astype(F32) == column).astype(BF16)


def qkv_kernel(experts, cap, tok, first, place, x_ref, w_ref, gain_ref, bias_ref, *refs):
    qkv_ref, unit_ref, xs_ref, slot_ref = refs[-4:]
    own_expert = place[0]
    x = x_ref[0, :tok]
    unit, unused = norm_parts(x.astype(F32))
    normed = (unit * gain_ref[0:1] + bias_ref[0:1]).astype(BF16)
    qkv_ref[0] = dot(normed, w_ref[...]).astype(BF16)
    unit_ref[0] = unit.T.astype(BF16)
    ids = x_ref[0, tok:][:1, :tok].astype(F32).astype(jnp.int32)
    slot = slots_of(ids, experts, cap)
    slot_ref[0] = jnp.broadcast_to(slot, (8, tok))
    xs_ref[0] = dot(pick_rows(slot, cap, own_expert * cap), x).astype(BF16)


def qkv_step(shards, first, places, held, w_own, gains, biases, seq_count, experts, cap):
    count, rows, width = shards.shape
    tok = rows - 16
    wide = w_own.shape[1]
    outs = [
        shape((seq_count, tok, wide), BF16),
        shape((seq_count, width, tok), BF16),
        shape((seq_count, cap, width), BF16),
        shape((seq_count, 8, tok), jnp.int32),
    ]
    spec = pltpu.PrefetchScalarGridSpec(
        num_scalar_prefetch=1,
        grid=(count,),
        in_specs=[
            pl.BlockSpec((1, rows, width), lambda i, at: (i, 0, 0)),
            whole(w_own),
            whole(gains),
            whole(biases),
        ]
        + [pl.BlockSpec(memory_space=pl.ANY)] * len(held),
        out_specs=[
            pl.BlockSpec((1,) + out.shape[1:], lambda i, at: (at[first + i], 0, 0)) for out in outs
        ],
    )
    return pl.pallas_call(
        functools.partial(qkv_kernel, experts, cap, tok, first),
        out_shape=outs,
        grid_spec=spec,
        input_output_aliases={5 + n: n for n in range(len(held))},
        compiler_params=params(),
        name="qkv_step",
        cost_estimate=cost(4),
    )(places, shards, w_own, gains, biases, *held)


def send_kernel(experts, cap, ids_ref, rows_ref, out_ref, slot_ref):
    slot = slots_of(ids_ref[0:1], experts, cap)
    slot_ref[...] = jnp.broadcast_to(slot, slot_ref.shape)
    out_ref[...] = dot(pick_rows(slot, experts * cap), rows_ref[...]).astype(BF16)


def send_rows(ids_row, rows, experts, cap):
    tok, width = rows.shape
    return pl.pallas_call(
        functools.partial(send_kernel, experts, cap),
        out_shape=[shape((experts * cap, width), BF16), shape((8, tok), jnp.int32)],
        compiler_params=params(),
        name="send_rows",
        cost_estimate=cost(3),
    )(jnp.broadcast_to(ids_row, (8, tok)), rows)


def doc_start(ends_ref, positions, docs):
    start = jnp.zeros_like(positions)
    for k in range(docs):
        start = jnp.where(ends_ref[k] <= positions, ends_ref[k], start)
    return start


def head_lanes(array, head):
    lane = lax.broadcasted_iota(jnp.int32, (1, array.shape[1]), 1)
    return jnp.where(lane // HEAD_DIM == head, array, jnp.zeros_like(array))


def attend_kernel(docs, cap, ends_ref, qkv_ref, slot_ref, send_ref, out_ref, lse_ref):
    blocks, tok, wide = qkv_ref.shape
    width = wide // 3
    heads = width // HEAD_DIM
    experts = send_ref.shape[0]
    scale = LOG2E / math.sqrt(HEAD_DIM)
    lane = lax.broadcasted_iota(jnp.int32, (tok, width), 1)

    def run(block):
        q = qkv_ref[block, :, :width]
        local = lax.broadcasted_iota(jnp.int32, (tok, 1), 0)
        start = doc_start(ends_ref, block * tok + local, docs)
        ones = jnp.ones((tok, width), BF16)
        merged = jnp.zeros((tok, width), F32)
        lse = jnp.zeros((tok, width), F32)
        for head in range(heads):
            q_head = head_lanes(q, head)
            parts = []
            for other in range(block + 1):
                s = dot(q_head, qkv_ref[other, :, width : 2 * width], 1, 1)
                column = lax.broadcasted_iota(jnp.int32, (tok, tok), 1)
                if other == block:
                    mask = (column <= local) & (column + other * tok >= start)
                    s = jnp.where(mask, s, MASKED)
                elif other == 0 or block == blocks - 1:
                    s = jnp.where(column + other * tok >= start, s, MASKED)
                parts.append(s)
            top = parts[0]
            for s in parts[1:]:
                top = jnp.maximum(top, s)
            top = jnp.max(top, axis=1, keepdims=True)
            shift = top * scale
            total = jnp.zeros((tok, 2 * width), F32)
            for other in range(block + 1):
                p = jnp.exp2(parts[other] * scale - shift).astype(BF16)
                v = jnp.concatenate([qkv_ref[other, :, 2 * width :], ones], axis=1)
                total = total + dot(p, v)
            weight = total[:, width:]
            mine = lane // HEAD_DIM == head
            merged = jnp.where(mine, total[:, :width] / weight, merged)
            lse = jnp.where(lane == head, shift + jnp.log2(weight), lse)
        out_ref[block] = merged
        lse_ref[block] = lse.T[:8]
        pick = pick_rows(slot_ref[block, 0:1], experts * cap)
        rows = dot(pick, merged.astype(BF16)).astype(BF16)
        for e in range(experts):
            send_ref[e, block] = rows[e * cap : (e + 1) * cap]

    for block in range(blocks):
        run(block)


def attend(qkv, slots, ends, cap):
    blocks, tok, wide = qkv.shape
    width = wide // 3
    return pl.pallas_call(
        functools.partial(attend_kernel, ends.shape[0], cap),
        out_shape=[
            shape((blocks, blocks, cap, width), BF16),
            shape((blocks, tok, width), F32),
            shape((blocks, 8, tok), F32),
        ],
        in_specs=[pl.BlockSpec(memory_space=pltpu.SMEM)]
        + [pl.BlockSpec(memory_space=pltpu.VMEM)] * 2,
        compiler_params=params(),
        name="attend",
        cost_estimate=cost(12),
    )(ends, qkv, slots)


def attend_back_kernel(
    docs, cap, ends_ref, qkv_ref, slot_ref, back_ref, out_ref, lse_ref, grad_ref, do_ref, dq_ref, delta_ref
):
    blocks, tok, wide = qkv_ref.shape
    width = wide // 3
    heads = width // HEAD_DIM
    experts = back_ref.shape[0]
    scale = LOG2E / math.sqrt(HEAD_DIM)

    for t in range(blocks):
        rows = jnp.concatenate([back_ref[e, t] for e in range(experts)], axis=0)
        do = dot(place_rows(slot_ref[t, 0:1], experts * cap), rows)
        do_ref[t] = do.astype(BF16)
        product = (do * out_ref[t]).T
        delta = jnp.zeros((8, tok), F32)
        row = lax.broadcasted_iota(jnp.int32, (8, tok), 0)
        for head in range(heads):
            part = product[head * HEAD_DIM : (head + 1) * HEAD_DIM]
            delta = jnp.where(row == head, jnp.sum(part, axis=0, keepdims=True), delta)
        delta_ref[t] = delta
        dq_ref[t] = jnp.zeros((tok, width), F32)

    def run(block):
        k = qkv_ref[block, :, width : 2 * width]
        v = qkv_ref[block, :, 2 * width :]
        k_pos = lax.broadcasted_iota(jnp.int32, (tok, tok), 0) + block * tok
        dk = jnp.zeros((tok, width), F32)
        dv = jnp.zeros((tok, width), F32)
        for other in range(block, blocks):
            q_pos = lax.broadcasted_iota(jnp.int32, (1, tok), 1) + other * tok
            start = doc_start(ends_ref, q_pos, docs)
            q = qkv_ref[other, :, :width]
            do = do_ref[other]
            dq = dq_ref[other]
            for head in range(heads):
                q_head = head_lanes(q, head)
                do_head = head_lanes(do, head)
                s = dot(k, q_head, 1, 1)
                p = jnp.exp2(s * scale - lse_ref[other, head : head + 1])
                if other == block:
                    p = jnp.where((k_pos <= q_pos) & (k_pos >= start), p, 0.0)
                elif block == 0 or other == blocks - 1:
                    p = jnp.where(k_pos >= start, p, 0.0)
                dp = dot(v, do_head, 1, 1)
                ds = (p * (dp - delta_ref[other, head : head + 1])).astype(BF16)
                dv = dv + dot(p.astype(BF16), do_head)
                dk = dk + dot(ds, q_head)
                dq = dq + dot(ds, head_lanes(k, head), 0, 0)
            dq_ref[other] = dq
        factor = 1.0 / math.sqrt(HEAD_DIM)
        for n, part in enumerate((dq_ref[block] * factor, dk * factor, dv)):
            columns = slice(n * width, (n + 1) * width)
            grad_ref[block, :, columns] = part.astype(BF16)

    for block in range(blocks):
        run(block)


def attend_back(qkv, slots, back, out, lse, ends, cap):
    blocks, tok, wide = qkv.shape
    width = wide // 3
    return pl.pallas_call(
        functools.partial(attend_back_kernel, ends.shape[0], cap),
        out_shape=shape((blocks, tok, wide), BF16),
        in_specs=[pl.BlockSpec(memory_space=pltpu.SMEM)]
        + [pl.BlockSpec(memory_space=pltpu.VMEM)] * 5,
        scratch_shapes=[
            pltpu.VMEM((blocks, tok, width), BF16),
            pltpu.VMEM((blocks, tok, width), F32),
            pltpu.VMEM((blocks, 8, tok), F32),
        ],
        compiler_params=params(),
        name="attend_back",
        cost_estimate=cost(20),
    )(ends, qkv, slots, back, out, lse)


def pick_all(slots, count):
    return (slots[:, :1, :] == jnp.arange(count, dtype=jnp.int32)[None, :, None]).astype(BF16)


def long_masks(ends, first, tok, length):
    q_pos = first + jnp.arange(tok, dtype=jnp.int32)
    k_pos = jnp.arange(length, dtype=jnp.int32)
    start = jnp.max(jnp.where(ends[None, :] <= q_pos[:, None], ends[None, :], 0), axis=1)
    return (k_pos[None, :] <= q_pos[:, None]) & (k_pos[None, :] >= start[:, None])


def long_heads(rows, width):
    return rows.reshape(rows.shape[0], width // HEAD_DIM, HEAD_DIM).transpose(1, 0, 2)


def attend_long(qkv, slots, ends, cap):
    blocks, tok, wide = qkv.shape
    width = wide // 3
    length = blocks * tok
    flat = qkv.reshape(length, wide)
    keys = long_heads(flat[:, width : 2 * width], width)
    values = long_heads(flat[:, 2 * width :], width)

    def one(block):
        query = long_heads(qkv[block, :, :width], width)
        mask = long_masks(ends, block * tok, tok, length)
        s = jnp.einsum("hqd,hkd->hqk", query, keys, preferred_element_type=F32)
        s = jnp.where(mask, s / math.sqrt(HEAD_DIM), MASKED)
        top = jnp.max(s, axis=-1, keepdims=True)
        weights = jnp.where(mask, jnp.exp(s - top), 0.0)
        total = jnp.sum(weights, axis=-1, keepdims=True)
        out = jnp.einsum("hqk,hkd->hqd", (weights / total).astype(BF16), values, preferred_element_type=F32)
        return out.transpose(1, 0, 2).reshape(tok, width), (top + jnp.log(total))[:, :, 0]

    out, lse = lax.map(one, jnp.arange(blocks, dtype=jnp.int32))
    pick = pick_all(slots, blocks * cap)
    rows = jnp.einsum("tsk,tkd->tsd", pick, out.astype(BF16), preferred_element_type=F32)
    send = rows.astype(BF16).reshape(blocks, blocks, cap, width).transpose(1, 0, 2, 3)
    return send, out, lse


def attend_back_long(qkv, slots, back, out, lse, ends, cap):
    blocks, tok, wide = qkv.shape
    width = wide // 3
    length = blocks * tok
    heads = width // HEAD_DIM
    flat = qkv.reshape(length, wide)
    keys = long_heads(flat[:, width : 2 * width], width)
    values = long_heads(flat[:, 2 * width :], width)
    pick = pick_all(slots, blocks * cap)
    rows = back.transpose(1, 0, 2, 3).reshape(blocks, blocks * cap, width)
    do_all = jnp.einsum("tsk,tsd->tkd", pick, rows, preferred_element_type=F32)

    def one(sums, block):
        query = long_heads(qkv[block, :, :width], width)
        mask = long_masks(ends, block * tok, tok, length)
        do = do_all[block]
        delta = jnp.sum((do * out[block]).reshape(tok, heads, HEAD_DIM), axis=-1).T
        do = long_heads(do.astype(BF16), width)
        s = jnp.einsum("hqd,hkd->hqk", query, keys, preferred_element_type=F32)
        p = jnp.where(mask, jnp.exp(s / math.sqrt(HEAD_DIM) - lse[block][:, :, None]), 0.0)
        dp = jnp.einsum("hqd,hkd->hqk", do, values, preferred_element_type=F32)
        ds = (p * (dp - delta[:, :, None]) / math.sqrt(HEAD_DIM)).astype(BF16)
        dq = jnp.einsum("hqk,hkd->qhd", ds, keys, preferred_element_type=F32)
        dk = jnp.einsum("hqk,hqd->khd", ds, query, preferred_element_type=F32)
        dv = jnp.einsum("hqk,hqd->khd", p.astype(BF16), do, preferred_element_type=F32)
        sums = (sums[0] + dk.reshape(length, width), sums[1] + dv.reshape(length, width))
        return sums, dq.reshape(tok, width)

    start = jnp.zeros((length, width), F32)
    (dk, dv), dq = lax.scan(one, (start, start), jnp.arange(blocks, dtype=jnp.int32))
    grad = jnp.concatenate([dq.reshape(length, width), dk, dv], axis=1).astype(BF16)
    return grad.reshape(blocks, tok, wide)


EXPERT_PART = 512


def expert_kernel(
    att_ref, xs_ref, g_ref, w_out_ref, gain_ref, bias_ref, w1_any, w2_any,
    datt_ref, branch_ref, sums_ref, ein_any, mid_any, active_any,
    w1_ref, w2_ref, ein_ref, mid_ref, active_ref, dpre_ref, in_sems, out_sems,
):
    groups, rows, width = att_ref.shape
    parts = [pl.ds(n, EXPERT_PART) for n in range(0, w1_ref.shape[1], EXPERT_PART)]
    loads = []
    for n, part in enumerate(parts):
        loads.append(
            (
                pltpu.make_async_copy(w1_any.at[0, :, part], w1_ref.at[:, part], in_sems.at[0, n]),
                pltpu.make_async_copy(w2_any.at[0, part], w2_ref.at[part], in_sems.at[1, n]),
            )
        )
        for load in loads[n]:
            load.start()
    stores = []

    def store(source, target):
        copy = pltpu.make_async_copy(source, target, out_sems.at[len(stores)])
        copy.start()
        stores.append(copy)

    att = jnp.concatenate([att_ref[n] for n in range(groups)], axis=1)
    mid = xs_ref[...].astype(F32) + dot(att, w_out_ref[...])
    mid_ref[...] = mid
    store(mid_ref, mid_any)
    unit, inv_std = norm_parts(mid)
    ein = (unit * gain_ref[1:2] + bias_ref[1:2]).astype(BF16)
    ein_ref[...] = ein
    store(ein_ref, ein_any)
    g = g_ref[...]
    for n, part in enumerate(parts):
        for load in loads[n]:
            load.wait()
        pre = dot(ein, w1_ref[:, part])
        d_active = dot(g, w2_ref[part], 1, 1)
        active, slope = gelu_both(pre)
        active_ref[:, part] = active.astype(BF16)
        store(active_ref.at[:, part], active_any.at[:, part])
        dpre_ref[:, part] = (d_active * slope).astype(BF16)
    d_in = dot(dpre_ref[...], w1_ref[...], 1, 1).astype(BF16).astype(F32)
    d_mid = g.astype(F32) + norm_back(d_in * gain_ref[1:2], unit, inv_std)
    branch = d_mid.astype(BF16)
    branch_ref[...] = branch
    d_att = dot(branch, w_out_ref[...], 1, 1).astype(BF16)
    for n in range(groups):
        datt_ref[n] = d_att[:, n * width : (n + 1) * width]
    sums_ref[...] = jnp.zeros_like(sums_ref)
    sums_ref[0:1] = jnp.sum(d_in * unit, axis=0, keepdims=True)
    sums_ref[1:2] = jnp.sum(d_in, axis=0, keepdims=True)
    for copy in stores:
        copy.wait()


def expert(att, xs, grads, w_out, gains, biases, w_in, w_exp_out):
    groups, rows, width = att.shape
    wide = xs.shape[1]
    hidden = w_in.shape[2]
    count = hidden // EXPERT_PART
    vmem = pl.BlockSpec(memory_space=pltpu.VMEM)
    hbm = pl.BlockSpec(memory_space=pl.ANY)
    return pl.pallas_call(
        expert_kernel,
        out_shape=[
            shape(att.shape, BF16),
            shape((rows, wide), BF16),
            shape((8, wide), F32),
            shape((rows, wide), BF16),
            shape((rows, wide), F32),
            shape((rows, hidden), BF16),
        ],
        in_specs=[vmem] * 6 + [hbm] * 2,
        out_specs=[vmem] * 3 + [hbm] * 3,
        scratch_shapes=[
            pltpu.VMEM((wide, hidden), BF16),
            pltpu.VMEM((hidden, wide), BF16),
            pltpu.VMEM((rows, wide), BF16),
            pltpu.VMEM((rows, wide), F32),
            pltpu.VMEM((rows, hidden), BF16),
            pltpu.VMEM((rows, hidden), BF16),
            pltpu.SemaphoreType.DMA((2, count)),
            pltpu.SemaphoreType.DMA((count + 2,)),
        ],
        compiler_params=params(),
        name="expert",
        cost_estimate=cost(18),
    )(att, xs, grads, w_out, gains, biases, w_in, w_exp_out)


def made_kernel(active_ref, w2_ref, mid_ref, branch_ref, back_ref, sum_ref):
    step = pl.program_id(0)
    term = dot(active_ref[...], w2_ref[0])

    @pl.when(step == 0)
    def first():
        sum_ref[...] = term

    @pl.when(step > 0)
    def later():
        sum_ref[...] += term

    @pl.when(step == pl.num_programs(0) - 1)
    def last():
        made = (mid_ref[...] + sum_ref[...].astype(BF16).astype(F32)).astype(BF16)
        seq_count = back_ref.shape[0]
        cap = made.shape[0] // seq_count
        for t in range(seq_count):
            back_ref[t, :cap] = made[t * cap : (t + 1) * cap]
            back_ref[t, cap : 2 * cap] = branch_ref[t * cap : (t + 1) * cap]


def expert_made(active, w_exp_out, mid, branch, seq_count, free):
    rows, hidden = active.shape
    wide = mid.shape[1]
    part = 1024
    out = shape((seq_count, 2 * rows // seq_count + free, wide), BF16)
    return pl.pallas_call(
        made_kernel,
        out_shape=out,
        grid=(hidden // part,),
        in_specs=[
            pl.BlockSpec((rows, part), lambda i: (0, i)),
            pl.BlockSpec((1, part, wide), lambda i: (0, i, 0)),
            whole(mid),
            whole(branch),
        ],
        out_specs=whole(out),
        scratch_shapes=[pltpu.VMEM((rows, wide), F32)],
        compiler_params=params(),
        name="expert_made",
        cost_estimate=cost(0.2),
    )(active, w_exp_out, mid, branch)


def weights_kernel(count, place, *refs):
    xs, gs = refs[:count], refs[count : 2 * count]
    w1_ref, w2_ref = refs[2 * count : 2 * count + 2]
    d1_ref, d2_ref, turned_ref = refs[-3:]

    @pl.when(pl.program_id(0) == 0)
    def begin():
        for n in range(count):
            turned_ref[n] = xs[n][...].T

    w1 = w1_ref[0]
    w2 = w2_ref[0]
    d1 = jnp.zeros(d1_ref.shape[1:], F32)
    d2 = jnp.zeros(d2_ref.shape[1:], F32)
    for n in range(count):
        g = gs[n][...]
        pre = dot(xs[n][...], w1)
        d_active = dot(g, w2, 1, 1)
        active, slope = gelu_both(pre)
        d1 = d1 + dot(turned_ref[n], (d_active * slope).astype(BF16))
        d2 = d2 + dot(active.astype(BF16), g, 0, 0)
    d1_ref[0] = d1
    d2_ref[0] = d2


WEIGHT_CALLS = 4


def expert_weights(rows, grads, w_in, w_exp_out, place, call, held):
    parts = len(rows)
    count, wide = rows[0].shape
    hidden = w_in.shape[2] // parts
    part = 256
    steps = hidden // part
    share = steps // WEIGHT_CALLS
    first = call * share
    spec = pltpu.PrefetchScalarGridSpec(
        num_scalar_prefetch=1,
        grid=(share,),
        in_specs=[whole(a) for a in (*rows, *grads)]
        + [
            pl.BlockSpec((1, wide, part), lambda i, at: (0, 0, at[0] * steps + first + i)),
            pl.BlockSpec((1, part, wide), lambda i, at: (0, at[0] * steps + first + i, 0)),
        ]
        + [pl.BlockSpec(memory_space=pl.ANY)] * len(held),
        out_specs=[
            pl.BlockSpec((1, wide, part), lambda i, at: (0, 0, first + i)),
            pl.BlockSpec((1, part, wide), lambda i, at: (0, first + i, 0)),
        ],
        scratch_shapes=[pltpu.VMEM((parts, wide, count), BF16)],
    )
    return pl.pallas_call(
        functools.partial(weights_kernel, parts),
        out_shape=[shape((1, wide, hidden), F32), shape((1, hidden, wide), F32)],
        grid_spec=spec,
        input_output_aliases={3 + 2 * parts + n: n for n in range(len(held))},
        compiler_params=params(),
        name="expert_weights",
        cost_estimate=cost(0.5),
    )(place[None].astype(jnp.int32), *rows, *grads, w_in, w_exp_out, *held)


def out_weights_kernel(ranks_ref, att_ref, branch_ref, send_ref, keep_ref, made_ref):
    groups, unused, width = att_ref.shape
    parts, wide, part = made_ref.shape
    for n in range(groups):
        lines = slice(n * width, (n + 1) * width)
        term = dot(att_ref[n], branch_ref[...], 0, 0).astype(BF16)
        for p in range(parts):
            made_ref[p, lines] = term[:, p * part : (p + 1) * part]
    for n, (ref, slot) in enumerate(((send_ref, 0), (send_ref, 1), (keep_ref, 0), (keep_ref, 1))):
        ref[slot] = made_ref[ranks_ref[n]]


def out_weights(ranks, att, branch):
    wide = branch.shape[1]
    part = wide // 4
    return pl.pallas_call(
        out_weights_kernel,
        out_shape=[shape((2, wide, part), BF16)] * 2,
        in_specs=[pl.BlockSpec(memory_space=pltpu.SMEM)]
        + [pl.BlockSpec(memory_space=pltpu.VMEM)] * 2,
        scratch_shapes=[pltpu.VMEM((4, wide, part), BF16)],
        compiler_params=params(),
        name="out_weights",
        cost_estimate=cost(1),
    )(ranks, att, branch)


def add_kernel(keep_ref, got_ref, out_ref):
    out_ref[...] = (keep_ref[1].astype(F32) + got_ref[1].astype(F32)).astype(BF16)


def add_theirs(keep, got):
    return pl.pallas_call(
        add_kernel,
        out_shape=shape(keep.shape[1:], BF16),
        in_specs=[pl.BlockSpec(memory_space=pltpu.VMEM)] * 2,
        compiler_params=params(),
        name="add_theirs",
        cost_estimate=cost(0.2),
    )(keep, got)


def sum_of(keep_ref, got_ref, far_ref):
    return keep_ref[0].astype(F32) + got_ref[0].astype(F32) + far_ref[...].astype(F32)


def join_kernel(keep_ref, got_ref, far_ref, back_ref, out_ref):
    total = sum_of(keep_ref, got_ref, far_ref).astype(BF16)
    count, lines, wide = out_ref.shape
    part = total.shape[1]
    folds = wide // part
    for t in range(count):
        for n in range(folds):
            at = (t * folds + n) * lines
            out_ref[t, :, n * part : (n + 1) * part] = total[at : at + lines]


def join_sum(keep, got, far, back):
    count, rows, wide = back.shape
    lines = far.shape[0] * far.shape[1] // (count * wide)
    return pl.pallas_call(
        join_kernel,
        out_shape=shape(back.shape, BF16),
        grid=(1,),
        in_specs=[whole(a) for a in (keep, got, far)] + [pl.BlockSpec(memory_space=pl.ANY)],
        out_specs=pl.BlockSpec((count, lines, wide), lambda i: (0, rows // lines - 1, 0)),
        input_output_aliases={3: 0},
        compiler_params=params(),
        name="join_sum",
        cost_estimate=cost(1),
    )(keep, got, far, back)


def qkv_weights_kernel(
    pick_ref, unit_ref, grad_ref, w_ref, gain_ref, bias_ref, two_ref, send_ref, keep_ref, cols_ref, sums_ref
):
    blocks = unit_ref.shape[0]
    parts, wide, width = cols_ref.shape
    moment = jnp.zeros((wide, parts * width), F32)
    total = jnp.zeros((1, parts * width), F32)
    for t in range(blocks):
        grad = grad_ref[t]
        moment = moment + dot(unit_ref[t], grad)
        total = total + jnp.sum(grad.astype(F32), axis=0, keepdims=True)
    gain = jnp.broadcast_to(gain_ref[0:1], (128, wide)).T[:, :1]
    bias = jnp.broadcast_to(bias_ref[0:1], (128, wide)).T[:, :1]
    made = moment * gain + bias * total
    for p in range(parts):
        cols_ref[p] = made[:, p * width : (p + 1) * width].astype(BF16)
    w = w_ref[...].astype(F32)
    d_gain = jnp.sum(w * moment, axis=1, keepdims=True)
    d_bias = jnp.sum(w * total, axis=1, keepdims=True)
    lane = lax.broadcasted_iota(jnp.int32, (wide, 128), 1)
    one = jnp.where(lane == 0, d_gain, jnp.where(lane == 1, d_bias, 0.0)).T[:8]
    row = lax.broadcasted_iota(jnp.int32, one.shape, 0)
    two = two_ref[...]
    all_sums = jnp.where(row == 0, one[0:1], jnp.where(row == 1, two[0:1], jnp.where(row == 2, one[1:2], two[1:2])))
    part = wide // 4
    for n in range(4):
        for line in range(part // 128):
            at = n * part + line * 128
            sums_ref[n, line] = all_sums[:, at : at + 128]
    for n, (ref, slot) in enumerate(((send_ref, 0), (send_ref, 1), (keep_ref, 0), (keep_ref, 1))):
        cols = cols_ref[pick_ref[4 + n]]
        ref[slot, :wide] = cols * pick_ref[8 + n].astype(F32).astype(BF16)
        lines = [sums_ref[pick_ref[n], line] for line in range(part // 128)]
        ref[slot, wide:] = jnp.concatenate(lines, axis=0).astype(BF16)


def qkv_weights(pick, unit, grad, w_own, gains, biases, sums_two):
    blocks, wide, tok = unit.shape
    width = w_own.shape[1] // 3
    lines = 8 * (wide // 4 // 128)
    outs = [shape((2, wide + lines, width), BF16)] * 2
    if width % 128 != 0:
        moment = jnp.einsum("tdk,tkf->df", unit, grad, preferred_element_type=F32)
        total = jnp.sum(grad.astype(F32), axis=(0, 1))
        made = moment * gains[0][:, None] + biases[0][:, None] * total[None, :]
        made = made.astype(BF16).reshape(wide, 3, width).transpose(1, 0, 2)
        w = w_own.astype(F32)
        copies = lax.axis_size("seq") * width // wide
        sums = jnp.stack(
            [
                jnp.sum(w * moment, axis=1) / copies,
                sums_two[0],
                jnp.sum(w * total[None, :], axis=1) / copies,
                sums_two[1],
            ]
        ).astype(BF16)
        terms = []
        for n in range(4):
            cols = made[pick[4 + n]] * pick[8 + n].astype(BF16)
            norms = lax.dynamic_slice_in_dim(sums, pick[n] * (wide // 4), wide // 4, 1)
            norms = norms.reshape(4, -1, 128).transpose(1, 0, 2)
            norms = jnp.pad(norms, ((0, 0), (0, 4), (0, 0))).reshape(-1, width)
            terms.append(jnp.concatenate([cols, norms], axis=0))
        return jnp.stack(terms[:2]), jnp.stack(terms[2:])
    return pl.pallas_call(
        qkv_weights_kernel,
        out_shape=outs,
        in_specs=[pl.BlockSpec(memory_space=pltpu.SMEM)]
        + [pl.BlockSpec(memory_space=pltpu.VMEM)] * 6,
        scratch_shapes=[
            pltpu.VMEM((3, wide, width), BF16),
            pltpu.VMEM((4, wide // 4 // 128, 8, 128), F32),
        ],
        compiler_params=params(),
        name="qkv_weights",
        cost_estimate=cost(4),
    )(pick, unit, grad, w_own, gains, biases, sums_two)


def bundle_kernel(keep_ref, got_ref, far_ref, back_ref, out_ref):
    rows, width = far_ref.shape
    out_ref[:rows] = sum_of(keep_ref, got_ref, far_ref).astype(BF16)
    count, lines, wide = back_ref.shape
    total = back_ref[0].astype(F32)
    for t in range(1, count):
        total = total + back_ref[t].astype(F32)
    total = total.astype(BF16)
    part = wide // 4
    for half in range(part // width):
        for n in range(4):
            at = rows + half * 4 * lines + n * lines
            first = n * part + half * width
            out_ref[at : at + lines] = total[:, first : first + width]


def bundle(keep, got, far, back):
    count, rows, wide = back.shape
    width = far.shape[1]
    lines = wide // 4 // count
    out = shape((far.shape[0] + lines * wide // width, width), BF16)
    return pl.pallas_call(
        bundle_kernel,
        out_shape=out,
        grid=(1,),
        in_specs=[whole(a) for a in (keep, got, far)]
        + [pl.BlockSpec((count, lines, wide), lambda i: (0, rows // lines - 1, 0))],
        out_specs=whole(out),
        compiler_params=params(),
        name="bundle",
        cost_estimate=cost(1),
    )(keep, got, far, back)


def columns_kernel(rows, place, *refs):
    out_ref, d_out_ref, gain_ref, bias_ref = refs[-4:]
    froms = refs[:-4]
    wide = out_ref.shape[0]
    width = froms[0].shape[1]
    lines = wide // len(froms)
    total = jnp.zeros((rows - wide, width), F32)
    for n, from_ref in enumerate(froms):

        @pl.when(place[n] < out_ref.shape[1] // width)
        def columns_of(n=n, from_ref=from_ref):
            first = pl.multiple_of(place[n] * width, width)
            out_ref[:, pl.ds(first, width)] = from_ref[:wide].astype(F32)

        total = total + from_ref[wide:rows].astype(F32)
        at = pl.ds(pl.multiple_of(place[len(froms) + n] * lines, lines), lines)
        for half in range(d_out_ref.shape[1] // width):
            first = rows + half * lines
            d_out_ref[at, half * width : (half + 1) * width] = from_ref[first : first + lines].astype(F32)
    for line in range(gain_ref.shape[1] // width):
        gain_ref[:, line * width : (line + 1) * width] = total[line * 8 : line * 8 + 2]
        bias_ref[:, line * width : (line + 1) * width] = total[line * 8 + 2 : line * 8 + 4]


def columns(froms, place, rows, wide, part):
    width = froms[0].shape[1]
    return pl.pallas_call(
        functools.partial(columns_kernel, rows),
        out_shape=[
            shape((wide, 3 * part), F32),
            shape((wide, part), F32),
            shape((2, part), F32),
            shape((2, part), F32),
        ],
        in_specs=[pl.BlockSpec(memory_space=pltpu.SMEM)]
        + [pl.BlockSpec(memory_space=pltpu.VMEM)] * len(froms),
        compiler_params=params(),
        name="columns",
        cost_estimate=cost(0.2),
    )(place.astype(jnp.int32), *froms)


def place_kernel(cap, slot_ref, back_ref, out_ref, mid_ref):
    experts = back_ref.shape[0]
    place = place_rows(slot_ref[0:1], experts * cap)
    made = jnp.concatenate([back_ref[e, :cap] for e in range(experts)], axis=0)
    out_ref[0] = dot(place, made).astype(BF16)
    branch = jnp.concatenate([back_ref[e, cap : 2 * cap] for e in range(experts)], axis=0)
    mid_ref[...] = dot(place, branch).astype(BF16)


def place_back(slots, back, cap):
    tok, wide = slots.shape[1], back.shape[2]
    return pl.pallas_call(
        functools.partial(place_kernel, cap),
        out_shape=[shape((1, tok, wide), BF16), shape((tok, wide), BF16)],
        compiler_params=params(),
        name="place_back",
        cost_estimate=cost(0.5),
    )(slots, back)


def finish_kernel(x_ref, grad_ref, w_ref, gain_ref, mid_ref, dx_ref, sum_ref):
    step = pl.program_id(0)
    groups, tok, wide = grad_ref.shape
    width = wide // 3

    def part(p):
        at = p * width
        return jnp.concatenate([grad_ref[n, :, at : at + width] for n in range(groups)], axis=1)

    @pl.when(step == 0)
    def first():
        sum_ref[...] = dot(part(0), w_ref[...], 1, 1)

    @pl.when(step == 1)
    def second():
        sum_ref[...] += dot(part(1), w_ref[...], 1, 1)

    @pl.when(step == 2)
    def last():
        d_normed = sum_ref[...] + dot(part(2), w_ref[...], 1, 1)
        unit, inv_std = norm_parts(x_ref[...].astype(F32))
        dx_ref[0] = mid_ref[...].astype(F32) + norm_back(d_normed * gain_ref[0:1], unit, inv_std)


def finish(x, grad, w_qkv, gains, d_mid):
    tok, wide = x.shape
    out = shape((1, tok, wide), F32)
    return pl.pallas_call(
        finish_kernel,
        out_shape=out,
        grid=(3,),
        in_specs=[
            whole(x),
            whole(grad),
            pl.BlockSpec((wide, wide), lambda i: (0, i)),
            whole(gains),
            whole(d_mid),
        ],
        out_specs=whole(out),
        scratch_shapes=[pltpu.VMEM((tok, wide), F32)],
        compiler_params=params(),
        name="finish",
        cost_estimate=cost(0.5),
    )(x, grad, w_qkv, gains, d_mid)


WALK = (0, 2, 4, 6, 7, 5, 3, 1)


def walk_pairs(way):
    return [(WALK[n], WALK[(n + way) % len(WALK)]) for n in range(len(WALK))]


def walk_places(at):
    hops = (0, 1, -1, 2, -2, 3, -3, 4)
    table = [[0] * len(hops) for unused in WALK]
    for n, device in enumerate(WALK):
        table[device] = [WALK[(n - hop) % len(WALK)] for hop in hops]
    return jnp.asarray(table, jnp.int32)[at]


def gather_steps(own, seq_count, done=lambda: ()):
    if seq_count != len(WALK):
        yield lax.all_gather(own, "seq")
        return
    yield own[None]
    ahead = behind = own
    half = own.shape[0] // 2
    for unused in range(3):
        before = done()
        ahead = lax.ppermute(after(ahead, *before), "seq", walk_pairs(1))
        behind = lax.ppermute(after(behind, *before), "seq", walk_pairs(-1))
        yield ahead[None]
        yield behind[None]
    before = done()
    top = lax.ppermute(after(ahead[:half], *before), "seq", walk_pairs(1))
    low = lax.ppermute(after(behind[half:], *before), "seq", walk_pairs(-1))
    yield jnp.concatenate([top, low], axis=0)[None]


def after(value, *others):
    return lax.optimization_barrier((value,) + others)[0]


def swap(x):
    return lax.all_to_all(x, "seq", split_axis=0, concat_axis=0, tiled=True)


def flip_pairs(count, bit):
    return [(n, n ^ bit) for n in range(count)]


def gather_batch(own, count):
    far = lax.ppermute(own, "batch", flip_pairs(count, 2))
    near = lax.ppermute(own, "batch", flip_pairs(count, 1))
    return own, far, near, lax.ppermute(far, "batch", flip_pairs(count, 1))


def sum_batch(send, keep, count):
    got = lax.ppermute(send, "batch", flip_pairs(count, 1))
    far = lax.ppermute(add_theirs(keep, got), "batch", flip_pairs(count, 2))
    return keep, got, far


def on_device(tokens, w_qkv, w_out, w_in, w_exp_out, gains, biases, lengths, hash_ids, cotangent):
    tok, width = tokens.shape[1:]
    seq_count = lax.axis_size("seq")
    batch_count = lax.axis_size("batch")
    at = lax.axis_index("seq")
    row = lax.axis_index("batch")
    groups = min(HEADS, seq_count)
    copies = seq_count // groups
    group = at // copies
    own = width // groups
    experts = seq_count
    slot_cap = max(2, 3 * tok // (2 * experts))
    cap = -(-slot_cap // 16) * 16
    x = tokens[0]
    ends = jnp.cumsum(lengths[0]).astype(jnp.int32)
    ids_row = hash_ids[0, :, 0][None, :]

    ids_rows = jnp.broadcast_to(jnp.pad(ids_row.astype(BF16), ((0, 0), (0, width - tok))), (16, width))
    load = jnp.concatenate([x, ids_rows], axis=0)
    w_own = jnp.concatenate(
        [lax.dynamic_slice_in_dim(w_qkv, n * width + group * own, own, 1) for n in range(3)], axis=1
    )
    if seq_count == len(WALK):
        order = walk_places(at)
    else:
        order = jnp.concatenate([at[None], jnp.arange(seq_count, dtype=jnp.int32)])
    grad_rows, own_slots = send_rows(ids_row, cotangent[0], experts, cap)
    held = ()
    older = ()
    arrived = []
    for shards in gather_steps(load, seq_count, lambda: older):
        first = len(arrived) if seq_count == len(WALK) else 1
        if len(arrived) % 2 == 1:
            older = held[3:]
        ready = held[3:]
        held = qkv_step(shards, first, order, held, w_own, gains, biases, seq_count, experts, cap)
        arrived.append(shards)
    qkv, unit, xs, slots = held

    grad_rows = after(grad_rows, arrived[-1], *ready)
    grads = swap(grad_rows.reshape(experts, cap, width)).reshape(seq_count * cap, width)

    long_rows = own % 128 != 0 or seq_count > 8
    send, att_out, lse = (attend_long if long_rows else attend)(qkv, slots, ends, cap)
    send = after(send, grads)
    share = seq_count // copies
    if copies > 1:
        send = lax.dynamic_slice_in_dim(send, (at % copies) * share, share, 1)
    got = swap(send).reshape(groups, seq_count * cap, own)
    slot_rows = seq_count * cap
    if own % 128 != 0:
        att = got.transpose(1, 0, 2).reshape(1, slot_rows, width)
    else:
        att = got
    part = width // batch_count
    d_att, branch, sums_two, expert_in, mid, active = expert(
        att, xs.reshape(slot_rows, width), grads, w_out, gains, biases, w_in, w_exp_out
    )
    free = part // seq_count if seq_count == len(WALK) else 0
    back = expert_made(active, w_exp_out, mid, branch, seq_count, free)
    if own % 128 != 0:
        d_att = d_att.reshape(slot_rows, groups, own).transpose(1, 0, 2)
    if copies > 1:
        d_att = jnp.repeat(d_att, copies, axis=0)
    d_att = swap(d_att).reshape(experts, seq_count, cap, own)


    all_grads = gather_batch(after(grads, att), batch_count)
    ranks = row ^ jnp.asarray((1, 3, 0, 2), jnp.int32)
    out_terms = sum_batch(*out_weights(ranks, after(att, all_grads[1]), branch), batch_count)
    out_far = after(out_terms[2], back)
    all_rows = gather_batch(after(expert_in, out_far), batch_count)
    if seq_count == len(WALK):
        back = join_sum(*out_terms[:2], out_far, back)
    else:
        d_out = lax.psum(sum_of(*out_terms).astype(BF16), "seq").astype(F32)
    back = swap(after(back, d_att))

    d_att = after(d_att, out_far)
    d_qkv = (attend_back_long if long_rows else attend_back)(qkv, slots, d_att, att_out, lse, ends, cap)
    d_qkv = after(d_qkv, all_rows[1])

    per_row = 3 * groups // batch_count
    blocks = (ranks * per_row - group + groups - 1) // groups
    fits = (blocks < 3) & (blocks * groups + group < (ranks + 1) * per_row)
    pick = jnp.concatenate([ranks, jnp.minimum(blocks, 2), fits.astype(jnp.int32)]).astype(jnp.int32)
    send, keep = qkv_weights(pick, unit, d_qkv, w_own, gains, biases, sums_two)
    got = lax.ppermute(send, "batch", flip_pairs(batch_count, 1))
    output, d_mid = place_back(own_slots, back, cap)

    d_weights = ()

    def weights_call(call, *others):
        nonlocal d_weights
        first = after(all_rows[0], *others)
        d_weights = expert_weights(
            (first, *all_rows[1:]), all_grads, w_in, w_exp_out, row, call, tuple(d_weights)
        )
        return d_weights[:1]

    theirs = add_theirs(keep, after(got, *weights_call(0)))
    terms = keep, got, lax.ppermute(theirs, "batch", flip_pairs(batch_count, 2))
    own_grad = swap(after(d_qkv, back, theirs))
    own_grad = own_grad.reshape(groups, copies, tok, 3 * own)[:, 0]
    if own % 128 != 0:
        own_grad = own_grad.reshape(groups, tok, 3, own).transpose(1, 2, 0, 3).reshape(1, tok, 3 * width)
    d_tokens = finish(x, own_grad, w_qkv, gains, d_mid)

    if seq_count == len(WALK):
        load = bundle(*terms, back)
        calls = iter(range(WEIGHT_CALLS))

        def weights_between():
            call = next(calls)
            if call == 0:
                return ()
            if call == 1:
                weights_call(1, load)
                return (*weights_call(2), d_mid)
            return (d_tokens,) if call == 2 else tuple(weights_call(3))

        froms = [a[0] for a in gather_steps(load, seq_count, weights_between)]
        place = jnp.concatenate([(order - row * per_row) % groups, order])
        d_w_qkv, d_w_out, d_gains, d_biases = columns(froms, place, send.shape[1], width, part)
    else:
        mine = sum_of(*terms).astype(BF16)
        gathered = lax.all_gather(mine, "seq")
        d_w_out = d_out
        for call in range(1, WEIGHT_CALLS):
            weights_call(call)
        picked = (row * per_row + jnp.arange(per_row, dtype=jnp.int32)) % groups * copies
        cols = jnp.take(gathered[:, :width], picked, axis=0)
        d_w_qkv = cols.transpose(1, 0, 2).reshape(width, per_row * own).astype(F32)
        norms = jnp.sum(gathered[:, width:].astype(F32), axis=0)
        norms = norms.reshape(-1, 8, 128)[:, :4].transpose(1, 0, 2).reshape(4, part)
        d_gains, d_biases = norms[:2], norms[2:]
    return output, d_tokens, d_w_qkv, d_w_out, *d_weights, d_gains, d_biases


def solution(mesh):
    return jax.shard_map(
        on_device,
        mesh=mesh,
        in_specs=(
            P("batch", "seq", None),
            P(),
            P(),
            P("seq", None, None),
            P("seq", None, None),
            P(),
            P(),
            P("batch", None),
            P("batch", "seq", None),
            P("batch", "seq", None),
        ),
        out_specs=(
            P("batch", "seq", None),
            P("batch", "seq", None),
            P(None, "batch"),
            P(None, "batch"),
            P("seq", None, "batch"),
            P("seq", "batch", None),
            P(None, "batch"),
            P(None, "batch"),
        ),
        check_vma=False,
    )
```

```python
import functools
import math

import jax
import jax.numpy as jnp
from jax import lax
from jax.experimental import pallas as pl
from jax.experimental.pallas import tpu as pltpu
from jax.sharding import PartitionSpec as P

HEADS = 16
HEAD_DIM = 64
NORM_EPS = 1e-05
MASKED = -1e30
LOG2E = 1.4426950408889634
F32 = jnp.float32
BF16 = jnp.bfloat16
VMEM_BYTES = 56 * 1024 * 1024


def dot(a, b, ca=1, cb=0):
    return lax.dot_general(a, b, (((ca,), (cb,)), ((), ())), preferred_element_type=F32)


def cost(time_us):
    return pl.CostEstimate(flops=int(time_us * 1e9), bytes_accessed=int(time_us * 3e6), transcendentals=0)


def params():
    return pltpu.CompilerParams(vmem_limit_bytes=VMEM_BYTES)


def shape(dims, kind):
    return jax.ShapeDtypeStruct(dims, kind)


def norm_parts(rows):
    row_mean = jnp.mean(rows, axis=-1, keepdims=True)
    centred = rows - row_mean
    row_var = jnp.mean(centred * centred, axis=-1, keepdims=True)
    inv_std = lax.rsqrt(row_var + NORM_EPS)
    return centred * inv_std, inv_std


def norm_back(scaled, unit_rows, inv_std):
    centred = scaled - jnp.mean(scaled, axis=-1, keepdims=True)
    centred = centred - unit_rows * jnp.mean(scaled * unit_rows, axis=-1, keepdims=True)
    return centred * inv_std


def gelu_both(pre):
    cdf = 0.5 + 0.5 * lax.erf(pre * 0.7071067811865476)
    density = jnp.exp(-0.5 * pre * pre) * 0.3989422804014327
    return pre * cdf, cdf + pre * density


def whole(array):
    rank = len(array.shape)
    return pl.BlockSpec(array.shape, lambda *unused: (0,) * rank)


def slots_of(ids_row, experts, cap):
    count = ids_row.shape[1]
    members = (lax.broadcasted_iota(jnp.int32, (experts, count), 0) == ids_row).astype(F32)
    order = lax.broadcasted_iota(jnp.int32, (count, count), 0) <= lax.broadcasted_iota(
        jnp.int32, (count, count), 1
    )
    ranks = dot(members.astype(BF16), order.astype(BF16))
    rank = jnp.sum(members * ranks, axis=0, keepdims=True).astype(jnp.int32) - 1
    return ids_row * cap + rank


def pick_rows(slot_row, count, first=0):
    rows = lax.broadcasted_iota(jnp.int32, (count, slot_row.shape[1]), 0) + first
    return (rows == slot_row).astype(BF16)


def place_rows(slot_row, count):
    tokens = slot_row.shape[1]
    column = jnp.broadcast_to(slot_row.astype(F32), (128, tokens)).T[:, :1]
    return (lax.broadcasted_iota(jnp.int32, (tokens, count), 1).astype(F32) == column).astype(BF16)


def qkv_kernel(experts, cap, first, count, place, *refs):
    w_ref, gain_ref, bias_ref = refs[2 * count : 2 * count + 3]
    qkv_ref, unit_ref, xs_ref, slot_ref = refs[-4:]
    own_expert = place[0]

    def run(x_ref, y_ref):
        x = jnp.concatenate([x_ref[...], y_ref[:-16]], axis=0)
        tok = x.shape[0]
        unit, unused = norm_parts(x.astype(F32))
        normed = (unit * gain_ref[0:1] + bias_ref[0:1]).astype(BF16)
        qkv_ref[0] = dot(normed, w_ref[...]).astype(BF16)
        unit_ref[0] = unit.T.astype(BF16)
        ids = y_ref[-16:][:1, :tok].astype(F32).astype(jnp.int32)
        slot = slots_of(ids, experts, cap)
        slot_ref[0] = jnp.broadcast_to(slot, (8, tok))
        xs_ref[0] = dot(pick_rows(slot, cap, own_expert * cap), x).astype(BF16)

    for n in range(count):
        pl.when(pl.program_id(0) == n)(functools.partial(run, refs[2 * n], refs[2 * n + 1]))


def qkv_step(shards, first, places, held, w_own, gains, biases, seq_count, experts, cap):
    count = len(shards)
    width = shards[0][0].shape[1]
    tok = shards[0][0].shape[0] + shards[0][1].shape[0] - 16
    wide = w_own.shape[1]
    outs = [
        shape((seq_count, tok, wide), BF16),
        shape((seq_count, width, tok), BF16),
        shape((seq_count, cap, width), BF16),
        shape((seq_count, 8, tok), jnp.int32),
    ]
    parts = [part for shard in shards for part in shard]
    spec = pltpu.PrefetchScalarGridSpec(
        num_scalar_prefetch=1,
        grid=(count,),
        in_specs=[whole(a) for a in (*parts, w_own, gains, biases)]
        + [pl.BlockSpec(memory_space=pl.ANY)] * len(held),
        out_specs=[
            pl.BlockSpec((1,) + out.shape[1:], lambda i, at: (at[first + i], 0, 0)) for out in outs
        ],
    )
    return pl.pallas_call(
        functools.partial(qkv_kernel, experts, cap, first, count),
        out_shape=outs,
        grid_spec=spec,
        input_output_aliases={4 + len(parts) + n: n for n in range(len(held))},
        compiler_params=params(),
        name="qkv_step",
        cost_estimate=cost(4 * count),
    )(places, *parts, w_own, gains, biases, *held)


def send_kernel(experts, cap, ids_ref, rows_ref, out_ref, slot_ref):
    slot = slots_of(ids_ref[0:1], experts, cap)
    slot_ref[...] = jnp.broadcast_to(slot, slot_ref.shape)
    out_ref[...] = dot(pick_rows(slot, experts * cap), rows_ref[...]).astype(BF16)


def send_rows(ids_row, rows, experts, cap):
    tok, width = rows.shape
    return pl.pallas_call(
        functools.partial(send_kernel, experts, cap),
        out_shape=[shape((experts * cap, width), BF16), shape((8, tok), jnp.int32)],
        compiler_params=params(),
        name="send_rows",
        cost_estimate=cost(3),
    )(jnp.broadcast_to(ids_row, (8, tok)), rows)


def doc_start(ends_ref, positions, docs):
    start = jnp.zeros_like(positions)
    for k in range(docs):
        start = jnp.where(ends_ref[k] <= positions, ends_ref[k], start)
    return start


def head_lanes(array, head):
    lane = lax.broadcasted_iota(jnp.int32, (1, array.shape[1]), 1)
    return jnp.where(lane // HEAD_DIM == head, array, jnp.zeros_like(array))


def attend_kernel(docs, cap, ends_ref, qkv_ref, slot_ref, send_ref, out_ref, lse_ref):
    blocks, tok, wide = qkv_ref.shape
    width = wide // 3
    heads = width // HEAD_DIM
    experts = send_ref.shape[0]
    scale = LOG2E / math.sqrt(HEAD_DIM)
    lane = lax.broadcasted_iota(jnp.int32, (tok, width), 1)

    def run(block):
        q = qkv_ref[block, :, :width]
        local = lax.broadcasted_iota(jnp.int32, (tok, 1), 0)
        start = doc_start(ends_ref, block * tok + local, docs)
        ones = jnp.ones((tok, width), BF16)
        merged = jnp.zeros((tok, width), F32)
        lse = jnp.zeros((tok, width), F32)
        for head in range(heads):
            q_head = head_lanes(q, head)
            parts = []
            for other in range(block + 1):
                s = dot(q_head, qkv_ref[other, :, width : 2 * width], 1, 1)
                column = lax.broadcasted_iota(jnp.int32, (tok, tok), 1)
                if other == block:
                    mask = (column <= local) & (column + other * tok >= start)
                    s = jnp.where(mask, s, MASKED)
                elif other == 0 or block == blocks - 1:
                    s = jnp.where(column + other * tok >= start, s, MASKED)
                parts.append(s)
            top = parts[0]
            for s in parts[1:]:
                top = jnp.maximum(top, s)
            top = jnp.max(top, axis=1, keepdims=True)
            shift = top * scale
            total = jnp.zeros((tok, 2 * width), F32)
            for other in range(block + 1):
                p = jnp.exp2(parts[other] * scale - shift).astype(BF16)
                v = jnp.concatenate([qkv_ref[other, :, 2 * width :], ones], axis=1)
                total = total + dot(p, v)
            weight = total[:, width:]
            mine = lane // HEAD_DIM == head
            merged = jnp.where(mine, total[:, :width] / weight, merged)
            lse = jnp.where(lane == head, shift + jnp.log2(weight), lse)
        out_ref[block] = merged
        lse_ref[block] = lse.T[:8]
        pick = pick_rows(slot_ref[block, 0:1], experts * cap)
        rows = dot(pick, merged.astype(BF16)).astype(BF16)
        for e in range(experts):
            send_ref[e, block] = rows[e * cap : (e + 1) * cap]

    for block in range(blocks):
        run(block)


def attend(qkv, slots, ends, cap):
    blocks, tok, wide = qkv.shape
    width = wide // 3
    return pl.pallas_call(
        functools.partial(attend_kernel, ends.shape[0], cap),
        out_shape=[
            shape((blocks, blocks, cap, width), BF16),
            shape((blocks, tok, width), F32),
            shape((blocks, 8, tok), F32),
        ],
        in_specs=[pl.BlockSpec(memory_space=pltpu.SMEM)]
        + [pl.BlockSpec(memory_space=pltpu.VMEM)] * 2,
        compiler_params=params(),
        name="attend",
        cost_estimate=cost(12),
    )(ends, qkv, slots)


def attend_back_kernel(
    docs, cap, ends_ref, qkv_ref, slot_ref, back_ref, out_ref, lse_ref, grad_ref, do_ref, dq_ref, delta_ref
):
    blocks, tok, wide = qkv_ref.shape
    width = wide // 3
    heads = width // HEAD_DIM
    experts = back_ref.shape[0]
    scale = LOG2E / math.sqrt(HEAD_DIM)

    for t in range(blocks):
        rows = jnp.concatenate([back_ref[e, t] for e in range(experts)], axis=0)
        do = dot(place_rows(slot_ref[t, 0:1], experts * cap), rows)
        do_ref[t] = do.astype(BF16)
        product = (do * out_ref[t]).T
        delta = jnp.zeros((8, tok), F32)
        row = lax.broadcasted_iota(jnp.int32, (8, tok), 0)
        for head in range(heads):
            part = product[head * HEAD_DIM : (head + 1) * HEAD_DIM]
            delta = jnp.where(row == head, jnp.sum(part, axis=0, keepdims=True), delta)
        delta_ref[t] = delta
        dq_ref[t] = jnp.zeros((tok, width), F32)

    def run(block):
        k = qkv_ref[block, :, width : 2 * width]
        v = qkv_ref[block, :, 2 * width :]
        k_pos = lax.broadcasted_iota(jnp.int32, (tok, tok), 0) + block * tok
        dk = jnp.zeros((tok, width), F32)
        dv = jnp.zeros((tok, width), F32)
        for other in range(block, blocks):
            q_pos = lax.broadcasted_iota(jnp.int32, (1, tok), 1) + other * tok
            start = doc_start(ends_ref, q_pos, docs)
            q = qkv_ref[other, :, :width]
            do = do_ref[other]
            dq = dq_ref[other]
            for head in range(heads):
                q_head = head_lanes(q, head)
                do_head = head_lanes(do, head)
                s = dot(k, q_head, 1, 1)
                p = jnp.exp2(s * scale - lse_ref[other, head : head + 1])
                if other == block:
                    p = jnp.where((k_pos <= q_pos) & (k_pos >= start), p, 0.0)
                elif block == 0 or other == blocks - 1:
                    p = jnp.where(k_pos >= start, p, 0.0)
                dp = dot(v, do_head, 1, 1)
                ds = (p * (dp - delta_ref[other, head : head + 1])).astype(BF16)
                dv = dv + dot(p.astype(BF16), do_head)
                dk = dk + dot(ds, q_head)
                dq = dq + dot(ds, head_lanes(k, head), 0, 0)
            dq_ref[other] = dq
        factor = 1.0 / math.sqrt(HEAD_DIM)
        for n, part in enumerate((dq_ref[block] * factor, dk * factor, dv)):
            columns = slice(n * width, (n + 1) * width)
            grad_ref[block, :, columns] = part.astype(BF16)

    for block in range(blocks):
        run(block)


def attend_back(qkv, slots, back, out, lse, ends, cap):
    blocks, tok, wide = qkv.shape
    width = wide // 3
    return pl.pallas_call(
        functools.partial(attend_back_kernel, ends.shape[0], cap),
        out_shape=shape((blocks, tok, wide), BF16),
        in_specs=[pl.BlockSpec(memory_space=pltpu.SMEM)]
        + [pl.BlockSpec(memory_space=pltpu.VMEM)] * 5,
        scratch_shapes=[
            pltpu.VMEM((blocks, tok, width), BF16),
            pltpu.VMEM((blocks, tok, width), F32),
            pltpu.VMEM((blocks, 8, tok), F32),
        ],
        compiler_params=params(),
        name="attend_back",
        cost_estimate=cost(20),
    )(ends, qkv, slots, back, out, lse)


def pick_all(slots, count):
    return (slots[:, :1, :] == jnp.arange(count, dtype=jnp.int32)[None, :, None]).astype(BF16)


def long_masks(ends, first, tok, length):
    q_pos = first + jnp.arange(tok, dtype=jnp.int32)
    k_pos = jnp.arange(length, dtype=jnp.int32)
    start = jnp.max(jnp.where(ends[None, :] <= q_pos[:, None], ends[None, :], 0), axis=1)
    return (k_pos[None, :] <= q_pos[:, None]) & (k_pos[None, :] >= start[:, None])


def long_heads(rows, width):
    return rows.reshape(rows.shape[0], width // HEAD_DIM, HEAD_DIM).transpose(1, 0, 2)


def attend_long(qkv, slots, ends, cap):
    blocks, tok, wide = qkv.shape
    width = wide // 3
    length = blocks * tok
    flat = qkv.reshape(length, wide)
    keys = long_heads(flat[:, width : 2 * width], width)
    values = long_heads(flat[:, 2 * width :], width)

    def one(block):
        query = long_heads(qkv[block, :, :width], width)
        mask = long_masks(ends, block * tok, tok, length)
        s = jnp.einsum("hqd,hkd->hqk", query, keys, preferred_element_type=F32)
        s = jnp.where(mask, s / math.sqrt(HEAD_DIM), MASKED)
        top = jnp.max(s, axis=-1, keepdims=True)
        weights = jnp.where(mask, jnp.exp(s - top), 0.0)
        total = jnp.sum(weights, axis=-1, keepdims=True)
        out = jnp.einsum("hqk,hkd->hqd", (weights / total).astype(BF16), values, preferred_element_type=F32)
        return out.transpose(1, 0, 2).reshape(tok, width), (top + jnp.log(total))[:, :, 0]

    out, lse = lax.map(one, jnp.arange(blocks, dtype=jnp.int32))
    pick = pick_all(slots, blocks * cap)
    rows = jnp.einsum("tsk,tkd->tsd", pick, out.astype(BF16), preferred_element_type=F32)
    send = rows.astype(BF16).reshape(blocks, blocks, cap, width).transpose(1, 0, 2, 3)
    return send, out, lse


def attend_back_long(qkv, slots, back, out, lse, ends, cap):
    blocks, tok, wide = qkv.shape
    width = wide // 3
    length = blocks * tok
    heads = width // HEAD_DIM
    flat = qkv.reshape(length, wide)
    keys = long_heads(flat[:, width : 2 * width], width)
    values = long_heads(flat[:, 2 * width :], width)
    pick = pick_all(slots, blocks * cap)
    rows = back.transpose(1, 0, 2, 3).reshape(blocks, blocks * cap, width)
    do_all = jnp.einsum("tsk,tsd->tkd", pick, rows, preferred_element_type=F32)

    def one(sums, block):
        query = long_heads(qkv[block, :, :width], width)
        mask = long_masks(ends, block * tok, tok, length)
        do = do_all[block]
        delta = jnp.sum((do * out[block]).reshape(tok, heads, HEAD_DIM), axis=-1).T
        do = long_heads(do.astype(BF16), width)
        s = jnp.einsum("hqd,hkd->hqk", query, keys, preferred_element_type=F32)
        p = jnp.where(mask, jnp.exp(s / math.sqrt(HEAD_DIM) - lse[block][:, :, None]), 0.0)
        dp = jnp.einsum("hqd,hkd->hqk", do, values, preferred_element_type=F32)
        ds = (p * (dp - delta[:, :, None]) / math.sqrt(HEAD_DIM)).astype(BF16)
        dq = jnp.einsum("hqk,hkd->qhd", ds, keys, preferred_element_type=F32)
        dk = jnp.einsum("hqk,hqd->khd", ds, query, preferred_element_type=F32)
        dv = jnp.einsum("hqk,hqd->khd", p.astype(BF16), do, preferred_element_type=F32)
        sums = (sums[0] + dk.reshape(length, width), sums[1] + dv.reshape(length, width))
        return sums, dq.reshape(tok, width)

    start = jnp.zeros((length, width), F32)
    (dk, dv), dq = lax.scan(one, (start, start), jnp.arange(blocks, dtype=jnp.int32))
    grad = jnp.concatenate([dq.reshape(length, width), dk, dv], axis=1).astype(BF16)
    return grad.reshape(blocks, tok, wide)


EXPERT_PART = 512


def active_kernel(g_ref, w2_ref, out_ref):
    out_ref[...] = dot(g_ref[...], w2_ref[0], 1, 1)


def expert_active(grads, w_exp_out):
    rows, wide = grads.shape
    hidden = w_exp_out.shape[1]
    return pl.pallas_call(
        active_kernel,
        out_shape=shape((rows, hidden), F32),
        grid=(hidden // EXPERT_PART,),
        in_specs=[whole(grads), pl.BlockSpec((1, EXPERT_PART, wide), lambda i: (0, i, 0))],
        out_specs=pl.BlockSpec((rows, EXPERT_PART), lambda i: (0, i)),
        compiler_params=params(),
        name="expert_active",
        cost_estimate=cost(5),
    )(grads, w_exp_out)


def expert_kernel(
    att_ref, xs_ref, g_ref, w_out_ref, gain_ref, bias_ref, w1_any, dact_any,
    datt_ref, branch_ref, sums_ref, ein_any, mid_any, active_any,
    w1_ref, dact_ref, ein_ref, mid_ref, active_ref, dpre_ref, in_sems, out_sems,
):
    groups, rows, width = att_ref.shape
    parts = [pl.ds(n, EXPERT_PART) for n in range(0, w1_ref.shape[1], EXPERT_PART)]
    loads = []
    for n, part in enumerate(parts):
        loads.append(
            (
                pltpu.make_async_copy(w1_any.at[0, :, part], w1_ref.at[:, part], in_sems.at[0, n]),
                pltpu.make_async_copy(dact_any.at[:, part], dact_ref.at[:, part], in_sems.at[1, n]),
            )
        )
        for load in loads[n]:
            load.start()
    stores = []

    def store(source, target):
        copy = pltpu.make_async_copy(source, target, out_sems.at[len(stores)])
        copy.start()
        stores.append(copy)

    att = jnp.concatenate([att_ref[n] for n in range(groups)], axis=1)
    mid = xs_ref[...].astype(F32) + dot(att, w_out_ref[...])
    mid_ref[...] = mid
    store(mid_ref, mid_any)
    unit, inv_std = norm_parts(mid)
    ein = (unit * gain_ref[1:2] + bias_ref[1:2]).astype(BF16)
    ein_ref[...] = ein
    store(ein_ref, ein_any)
    g = g_ref[...]
    for n, part in enumerate(parts):
        for load in loads[n]:
            load.wait()
        pre = dot(ein, w1_ref[:, part])
        active, slope = gelu_both(pre)
        active_ref[:, part] = active.astype(BF16)
        store(active_ref.at[:, part], active_any.at[:, part])
        dpre_ref[:, part] = (dact_ref[:, part] * slope).astype(BF16)
    d_in = dot(dpre_ref[...], w1_ref[...], 1, 1).astype(BF16).astype(F32)
    d_mid = g.astype(F32) + norm_back(d_in * gain_ref[1:2], unit, inv_std)
    branch = d_mid.astype(BF16)
    branch_ref[...] = branch
    d_att = dot(branch, w_out_ref[...], 1, 1).astype(BF16)
    for n in range(groups):
        datt_ref[n] = d_att[:, n * width : (n + 1) * width]
    sums_ref[...] = jnp.zeros_like(sums_ref)
    sums_ref[0:1] = jnp.sum(d_in * unit, axis=0, keepdims=True)
    sums_ref[1:2] = jnp.sum(d_in, axis=0, keepdims=True)
    for copy in stores:
        copy.wait()


def expert(att, xs, grads, w_out, gains, biases, w_in, d_active):
    groups, rows, width = att.shape
    wide = xs.shape[1]
    hidden = w_in.shape[2]
    count = hidden // EXPERT_PART
    vmem = pl.BlockSpec(memory_space=pltpu.VMEM)
    hbm = pl.BlockSpec(memory_space=pl.ANY)
    return pl.pallas_call(
        expert_kernel,
        out_shape=[
            shape(att.shape, BF16),
            shape((rows, wide), BF16),
            shape((8, wide), F32),
            shape((rows, wide), BF16),
            shape((rows, wide), F32),
            shape((rows, hidden), BF16),
        ],
        in_specs=[vmem] * 6 + [hbm] * 2,
        out_specs=[vmem] * 3 + [hbm] * 3,
        scratch_shapes=[
            pltpu.VMEM((wide, hidden), BF16),
            pltpu.VMEM((rows, hidden), F32),
            pltpu.VMEM((rows, wide), BF16),
            pltpu.VMEM((rows, wide), F32),
            pltpu.VMEM((rows, hidden), BF16),
            pltpu.VMEM((rows, hidden), BF16),
            pltpu.SemaphoreType.DMA((2, count)),
            pltpu.SemaphoreType.DMA((count + 2,)),
        ],
        compiler_params=params(),
        name="expert",
        cost_estimate=cost(18),
    )(att, xs, grads, w_out, gains, biases, w_in, d_active)


def made_kernel(active_ref, w2_ref, mid_ref, branch_ref, back_ref, sum_ref):
    step = pl.program_id(0)
    term = dot(active_ref[...], w2_ref[0])

    @pl.when(step == 0)
    def first():
        sum_ref[...] = term

    @pl.when(step > 0)
    def later():
        sum_ref[...] += term

    @pl.when(step == pl.num_programs(0) - 1)
    def last():
        made = (mid_ref[...] + sum_ref[...].astype(BF16).astype(F32)).astype(BF16)
        seq_count = back_ref.shape[0]
        cap = made.shape[0] // seq_count
        for t in range(seq_count):
            back_ref[t, :cap] = made[t * cap : (t + 1) * cap]
            back_ref[t, cap : 2 * cap] = branch_ref[t * cap : (t + 1) * cap]


def expert_made(active, w_exp_out, mid, branch, seq_count, free):
    rows, hidden = active.shape
    wide = mid.shape[1]
    part = 1024
    out = shape((seq_count, 2 * rows // seq_count + free, wide), BF16)
    return pl.pallas_call(
        made_kernel,
        out_shape=out,
        grid=(hidden // part,),
        in_specs=[
            pl.BlockSpec((rows, part), lambda i: (0, i)),
            pl.BlockSpec((1, part, wide), lambda i: (0, i, 0)),
            whole(mid),
            whole(branch),
        ],
        out_specs=whole(out),
        scratch_shapes=[pltpu.VMEM((rows, wide), F32)],
        compiler_params=params(),
        name="expert_made",
        cost_estimate=cost(0.2),
    )(active, w_exp_out, mid, branch)


def weights_kernel(count, place, *refs):
    xs, gs = refs[:count], refs[count : 2 * count]
    w1_ref, w2_ref = refs[2 * count : 2 * count + 2]
    d1_ref, d2_ref, turned_ref = refs[-3:]

    @pl.when(pl.program_id(0) == 0)
    def begin():
        for n in range(count):
            turned_ref[n] = xs[n][...].T

    x = jnp.concatenate([xs[n][...] for n in range(count)], axis=0)
    g = jnp.concatenate([gs[n][...] for n in range(count)], axis=0)
    pre = dot(x, w1_ref[0])
    d_active = dot(g, w2_ref[0], 1, 1)
    active, slope = gelu_both(pre)
    turned = jnp.concatenate([turned_ref[n] for n in range(count)], axis=1)
    d1_ref[0] = dot(turned, (d_active * slope).astype(BF16))
    d2_ref[0] = dot(active.astype(BF16), g, 0, 0)


WEIGHT_CALLS = 1


def expert_weights(rows, grads, w_in, w_exp_out, place, call, held):
    parts = len(rows)
    count, wide = rows[0].shape
    hidden = w_in.shape[2] // parts
    part = 256
    steps = hidden // part
    share = steps // WEIGHT_CALLS
    first = call * share
    spec = pltpu.PrefetchScalarGridSpec(
        num_scalar_prefetch=1,
        grid=(share,),
        in_specs=[whole(a) for a in (*rows, *grads)]
        + [
            pl.BlockSpec((1, wide, part), lambda i, at: (0, 0, at[0] * steps + first + i)),
            pl.BlockSpec((1, part, wide), lambda i, at: (0, at[0] * steps + first + i, 0)),
        ]
        + [pl.BlockSpec(memory_space=pl.ANY)] * len(held),
        out_specs=[
            pl.BlockSpec((1, wide, part), lambda i, at: (0, 0, first + i)),
            pl.BlockSpec((1, part, wide), lambda i, at: (0, first + i, 0)),
        ],
        scratch_shapes=[pltpu.VMEM((parts, wide, count), BF16)],
    )
    return pl.pallas_call(
        functools.partial(weights_kernel, parts),
        out_shape=[shape((1, wide, hidden), F32), shape((1, hidden, wide), F32)],
        grid_spec=spec,
        input_output_aliases={3 + 2 * parts + n: n for n in range(len(held))},
        compiler_params=params(),
        name="expert_weights",
        cost_estimate=cost(0.5),
    )(place[None].astype(jnp.int32), *rows, *grads, w_in, w_exp_out, *held)


def out_weights_kernel(ranks_ref, att_ref, branch_ref, send_ref, keep_ref):
    groups = att_ref.shape[0]
    part = send_ref.shape[2]
    att = jnp.concatenate([att_ref[n] for n in range(groups)], axis=1)
    for n, (ref, slot) in enumerate(((send_ref, 0), (send_ref, 1), (keep_ref, 0), (keep_ref, 1))):
        columns = pl.ds(pl.multiple_of(ranks_ref[n] * part, part), part)
        ref[slot] = dot(att, branch_ref[:, columns], 0, 0).astype(BF16)


def out_weights(ranks, att, branch):
    wide = branch.shape[1]
    part = wide // 4
    return pl.pallas_call(
        out_weights_kernel,
        out_shape=[shape((2, wide, part), BF16)] * 2,
        in_specs=[pl.BlockSpec(memory_space=pltpu.SMEM)]
        + [pl.BlockSpec(memory_space=pltpu.VMEM)] * 2,
        compiler_params=params(),
        name="out_weights",
        cost_estimate=cost(1),
    )(ranks, att, branch)


def add_kernel(keep_ref, got_ref, out_ref):
    out_ref[...] = (keep_ref[1].astype(F32) + got_ref[1].astype(F32)).astype(BF16)


def add_theirs(keep, got):
    return pl.pallas_call(
        add_kernel,
        out_shape=shape(keep.shape[1:], BF16),
        in_specs=[pl.BlockSpec(memory_space=pltpu.VMEM)] * 2,
        compiler_params=params(),
        name="add_theirs",
        cost_estimate=cost(0.2),
    )(keep, got)


def sum_of(keep_ref, got_ref, far_ref):
    return keep_ref[0].astype(F32) + got_ref[0].astype(F32) + far_ref[...].astype(F32)


def join_kernel(keep_ref, got_ref, far_ref, back_ref, out_ref):
    total = sum_of(keep_ref, got_ref, far_ref).astype(BF16)
    count, lines, wide = out_ref.shape
    part = total.shape[1]
    folds = wide // part
    for t in range(count):
        for n in range(folds):
            at = (t * folds + n) * lines
            out_ref[t, :, n * part : (n + 1) * part] = total[at : at + lines]


def join_sum(keep, got, far, back):
    count, rows, wide = back.shape
    lines = far.shape[0] * far.shape[1] // (count * wide)
    return pl.pallas_call(
        join_kernel,
        out_shape=shape(back.shape, BF16),
        grid=(1,),
        in_specs=[whole(a) for a in (keep, got, far)] + [pl.BlockSpec(memory_space=pl.ANY)],
        out_specs=pl.BlockSpec((count, lines, wide), lambda i: (0, rows // lines - 1, 0)),
        input_output_aliases={3: 0},
        compiler_params=params(),
        name="join_sum",
        cost_estimate=cost(1),
    )(keep, got, far, back)


def qkv_weights_kernel(
    pick_ref, unit_ref, grad_ref, w_ref, gain_ref, bias_ref, two_ref, send_ref, keep_ref, cols_ref, sums_ref
):
    blocks = unit_ref.shape[0]
    parts, wide, width = cols_ref.shape
    grad = jnp.concatenate([grad_ref[t] for t in range(blocks)], axis=0)
    moment = dot(jnp.concatenate([unit_ref[t] for t in range(blocks)], axis=1), grad)
    total = jnp.sum(grad.astype(F32), axis=0, keepdims=True)
    gain = jnp.broadcast_to(gain_ref[0:1], (128, wide)).T[:, :1]
    bias = jnp.broadcast_to(bias_ref[0:1], (128, wide)).T[:, :1]
    made = moment * gain + bias * total
    for p in range(parts):
        cols_ref[p] = made[:, p * width : (p + 1) * width].astype(BF16)
    w = w_ref[...].astype(F32)
    d_gain = jnp.sum(w * moment, axis=1, keepdims=True)
    d_bias = jnp.sum(w * total, axis=1, keepdims=True)
    lane = lax.broadcasted_iota(jnp.int32, (wide, 128), 1)
    one = jnp.where(lane == 0, d_gain, jnp.where(lane == 1, d_bias, 0.0)).T[:8]
    row = lax.broadcasted_iota(jnp.int32, one.shape, 0)
    two = two_ref[...]
    all_sums = jnp.where(row == 0, one[0:1], jnp.where(row == 1, two[0:1], jnp.where(row == 2, one[1:2], two[1:2])))
    part = wide // 4
    for n in range(4):
        for line in range(part // 128):
            at = n * part + line * 128
            sums_ref[n, line] = all_sums[:, at : at + 128]
    for n, (ref, slot) in enumerate(((send_ref, 0), (send_ref, 1), (keep_ref, 0), (keep_ref, 1))):
        cols = cols_ref[pick_ref[4 + n]]
        ref[slot, :wide] = cols * pick_ref[8 + n].astype(F32).astype(BF16)
        lines = [sums_ref[pick_ref[n], line] for line in range(part // 128)]
        ref[slot, wide:] = jnp.concatenate(lines, axis=0).astype(BF16)


def qkv_weights(pick, unit, grad, w_own, gains, biases, sums_two):
    blocks, wide, tok = unit.shape
    width = w_own.shape[1] // 3
    lines = 8 * (wide // 4 // 128)
    outs = [shape((2, wide + lines, width), BF16)] * 2
    if width % 128 != 0:
        moment = jnp.einsum("tdk,tkf->df", unit, grad, preferred_element_type=F32)
        total = jnp.sum(grad.astype(F32), axis=(0, 1))
        made = moment * gains[0][:, None] + biases[0][:, None] * total[None, :]
        made = made.astype(BF16).reshape(wide, 3, width).transpose(1, 0, 2)
        w = w_own.astype(F32)
        copies = lax.axis_size("seq") * width // wide
        sums = jnp.stack(
            [
                jnp.sum(w * moment, axis=1) / copies,
                sums_two[0],
                jnp.sum(w * total[None, :], axis=1) / copies,
                sums_two[1],
            ]
        ).astype(BF16)
        terms = []
        for n in range(4):
            cols = made[pick[4 + n]] * pick[8 + n].astype(BF16)
            norms = lax.dynamic_slice_in_dim(sums, pick[n] * (wide // 4), wide // 4, 1)
            norms = norms.reshape(4, -1, 128).transpose(1, 0, 2)
            norms = jnp.pad(norms, ((0, 0), (0, 4), (0, 0))).reshape(-1, width)
            terms.append(jnp.concatenate([cols, norms], axis=0))
        return jnp.stack(terms[:2]), jnp.stack(terms[2:])
    return pl.pallas_call(
        qkv_weights_kernel,
        out_shape=outs,
        in_specs=[pl.BlockSpec(memory_space=pltpu.SMEM)]
        + [pl.BlockSpec(memory_space=pltpu.VMEM)] * 6,
        scratch_shapes=[
            pltpu.VMEM((3, wide, width), BF16),
            pltpu.VMEM((4, wide // 4 // 128, 8, 128), F32),
        ],
        compiler_params=params(),
        name="qkv_weights",
        cost_estimate=cost(4),
    )(pick, unit, grad, w_own, gains, biases, sums_two)


def bundle_kernel(keep_ref, got_ref, far_ref, back_ref, first_ref, out_ref):
    rows, width = far_ref.shape
    cut = first_ref.shape[0]
    made = sum_of(keep_ref, got_ref, far_ref).astype(BF16)
    first_ref[...] = made[:cut]
    rows = rows - cut
    out_ref[:rows] = made[cut:]
    count, lines, wide = back_ref.shape
    total = back_ref[0].astype(F32)
    for t in range(1, count):
        total = total + back_ref[t].astype(F32)
    total = total.astype(BF16)
    part = wide // 4
    for half in range(part // width):
        for n in range(4):
            at = rows + half * 4 * lines + n * lines
            first = n * part + half * width
            out_ref[at : at + lines] = total[:, first : first + width]


def bundle(keep, got, far, back):
    count, rows, wide = back.shape
    width = far.shape[1]
    lines = wide // 4 // count
    total = far.shape[0] + lines * wide // width
    outs = [shape((total // 32 * 16, width), BF16), shape((total - total // 32 * 16, width), BF16)]
    return pl.pallas_call(
        bundle_kernel,
        out_shape=outs,
        grid=(1,),
        in_specs=[whole(a) for a in (keep, got, far)]
        + [pl.BlockSpec((count, lines, wide), lambda i: (0, rows // lines - 1, 0))],
        out_specs=[whole(a) for a in outs],
        compiler_params=params(),
        name="bundle",
        cost_estimate=cost(1),
    )(keep, got, far, back)


def columns_kernel(rows, place, *refs):
    out_ref, d_out_ref, gain_ref, bias_ref = refs[-4:]
    froms = refs[:-4]
    count = len(froms) // 2
    wide = out_ref.shape[0]
    cut, width = froms[0].shape
    lines = wide // count
    total = jnp.zeros((rows - wide, width), F32)
    for n in range(count):
        head, tail = froms[2 * n : 2 * n + 2]

        @pl.when(place[n] < out_ref.shape[1] // width)
        def columns_of(n=n, head=head, tail=tail):
            first = pl.ds(pl.multiple_of(place[n] * width, width), width)
            out_ref[:cut, first] = head[...].astype(F32)
            out_ref[cut:, first] = tail[: wide - cut].astype(F32)

        total = total + tail[wide - cut : rows - cut].astype(F32)
        at = pl.ds(pl.multiple_of(place[count + n] * lines, lines), lines)
        for half in range(d_out_ref.shape[1] // width):
            first = rows - cut + half * lines
            d_out_ref[at, half * width : (half + 1) * width] = tail[first : first + lines].astype(F32)
    for line in range(gain_ref.shape[1] // width):
        gain_ref[:, line * width : (line + 1) * width] = total[line * 8 : line * 8 + 2]
        bias_ref[:, line * width : (line + 1) * width] = total[line * 8 + 2 : line * 8 + 4]


def columns(froms, place, rows, wide, part):
    width = froms[0].shape[1]
    return pl.pallas_call(
        functools.partial(columns_kernel, rows),
        out_shape=[
            shape((wide, 3 * part), F32),
            shape((wide, part), F32),
            shape((2, part), F32),
            shape((2, part), F32),
        ],
        in_specs=[pl.BlockSpec(memory_space=pltpu.SMEM)]
        + [pl.BlockSpec(memory_space=pltpu.VMEM)] * len(froms),
        compiler_params=params(),
        name="columns",
        cost_estimate=cost(0.2),
    )(place.astype(jnp.int32), *froms)


def place_kernel(cap, slot_ref, back_ref, out_ref, mid_ref):
    experts = back_ref.shape[0]
    place = place_rows(slot_ref[0:1], experts * cap)
    made = jnp.concatenate([back_ref[e, :cap] for e in range(experts)], axis=0)
    out_ref[0] = dot(place, made).astype(BF16)
    branch = jnp.concatenate([back_ref[e, cap : 2 * cap] for e in range(experts)], axis=0)
    mid_ref[...] = dot(place, branch).astype(BF16)


def place_back(slots, back, cap):
    tok, wide = slots.shape[1], back.shape[2]
    return pl.pallas_call(
        functools.partial(place_kernel, cap),
        out_shape=[shape((1, tok, wide), BF16), shape((tok, wide), BF16)],
        compiler_params=params(),
        name="place_back",
        cost_estimate=cost(0.5),
    )(slots, back)


def finish_kernel(x_ref, grad_ref, w_ref, gain_ref, mid_ref, dx_ref, sum_ref):
    step = pl.program_id(0)
    groups, tok, wide = grad_ref.shape
    width = wide // 3

    def part(p):
        at = p * width
        return jnp.concatenate([grad_ref[n, :, at : at + width] for n in range(groups)], axis=1)

    @pl.when(step == 0)
    def first():
        sum_ref[...] = dot(part(0), w_ref[...], 1, 1)

    @pl.when(step == 1)
    def second():
        sum_ref[...] += dot(part(1), w_ref[...], 1, 1)

    @pl.when(step == 2)
    def last():
        d_normed = sum_ref[...] + dot(part(2), w_ref[...], 1, 1)
        unit, inv_std = norm_parts(x_ref[...].astype(F32))
        dx_ref[0] = mid_ref[...].astype(F32) + norm_back(d_normed * gain_ref[0:1], unit, inv_std)


def finish(x, grad, w_qkv, gains, d_mid):
    tok, wide = x.shape
    out = shape((1, tok, wide), F32)
    return pl.pallas_call(
        finish_kernel,
        out_shape=out,
        grid=(3,),
        in_specs=[
            whole(x),
            whole(grad),
            pl.BlockSpec((wide, wide), lambda i: (0, i)),
            whole(gains),
            whole(d_mid),
        ],
        out_specs=whole(out),
        scratch_shapes=[pltpu.VMEM((tok, wide), F32)],
        compiler_params=params(),
        name="finish",
        cost_estimate=cost(0.5),
    )(x, grad, w_qkv, gains, d_mid)


WALK = (0, 2, 4, 6, 7, 5, 3, 1)


def walk_pairs(way):
    return [(WALK[n], WALK[(n + way) % len(WALK)]) for n in range(len(WALK))]


def walk_places(at):
    hops = (0, 1, -1, 2, -2, 3, -3, 4)
    table = [[0] * len(hops) for unused in WALK]
    for n, device in enumerate(WALK):
        table[device] = [WALK[(n - hop) % len(WALK)] for hop in hops]
    return jnp.asarray(table, jnp.int32)[at]


def gather_steps(own, done):
    ahead = behind = own
    yield [own]
    for unused in range(3):
        before = done()
        ahead, behind = [
            tuple(lax.ppermute(after(part, *before), "seq", walk_pairs(way)) for part in parts)
            for way, parts in ((1, ahead), (-1, behind))
        ]
        yield [ahead, behind]
    before = done()
    first = lax.ppermute(after(ahead[0], *before), "seq", walk_pairs(1))
    second = lax.ppermute(after(behind[1], *before), "seq", walk_pairs(-1))
    yield [(first, second)]


def after(value, *others):
    return lax.optimization_barrier((value,) + others)[0]


def swap(x):
    return lax.all_to_all(x, "seq", split_axis=0, concat_axis=0, tiled=True)


def flip_pairs(count, bit):
    return [(n, n ^ bit) for n in range(count)]


def gather_batch(own, count):
    far = lax.ppermute(own, "batch", flip_pairs(count, 2))
    near = lax.ppermute(own, "batch", flip_pairs(count, 1))
    return own, far, near, lax.ppermute(far, "batch", flip_pairs(count, 1))


def sum_batch(send, keep, count):
    got = lax.ppermute(send, "batch", flip_pairs(count, 1))
    far = lax.ppermute(add_theirs(keep, got), "batch", flip_pairs(count, 2))
    return keep, got, far


def on_device(tokens, w_qkv, w_out, w_in, w_exp_out, gains, biases, lengths, hash_ids, cotangent):
    tok, width = tokens.shape[1:]
    seq_count = lax.axis_size("seq")
    batch_count = lax.axis_size("batch")
    at = lax.axis_index("seq")
    row = lax.axis_index("batch")
    groups = min(HEADS, seq_count)
    copies = seq_count // groups
    group = at // copies
    own = width // groups
    experts = seq_count
    slot_cap = max(2, 3 * tok // (2 * experts))
    cap = -(-slot_cap // 16) * 16
    x = tokens[0]
    ends = jnp.cumsum(lengths[0]).astype(jnp.int32)
    ids_row = hash_ids[0, :, 0][None, :]

    ids_rows = jnp.broadcast_to(jnp.pad(ids_row.astype(BF16), ((0, 0), (0, width - tok))), (16, width))
    load = (x[: tok // 2], jnp.concatenate([x[tok // 2 :], ids_rows], axis=0))
    w_own = jnp.concatenate(
        [lax.dynamic_slice_in_dim(w_qkv, n * width + group * own, own, 1) for n in range(3)], axis=1
    )
    order = jnp.concatenate([at[None], jnp.arange(seq_count, dtype=jnp.int32)])
    grad_rows, own_slots = send_rows(ids_row, cotangent[0], experts, cap)
    held = ready = ()
    if seq_count == len(WALK):
        order = walk_places(at)
        seen = 0
        for shards in gather_steps(load, lambda: ready):
            ready = held[3:]
            held = qkv_step(shards, seen, order, held, w_own, gains, biases, seq_count, experts, cap)
            seen += len(shards)
        last = shards[0]
    else:
        last = [lax.all_gather(part, "seq") for part in load]
        for n in range(seq_count):
            shards = [(last[0][n], last[1][n])]
            held = qkv_step(shards, n + 1, order, held, w_own, gains, biases, seq_count, experts, cap)
    qkv, unit, xs, slots = held

    grad_rows = after(grad_rows, *last, *ready)
    grads = swap(grad_rows.reshape(experts, cap, width)).reshape(seq_count * cap, width)

    d_active = expert_active(grads, w_exp_out)
    long_rows = own % 128 != 0 or seq_count > 8
    send, att_out, lse = (attend_long if long_rows else attend)(qkv, slots, ends, cap)
    send = after(send, grads)
    share = seq_count // copies
    if copies > 1:
        send = lax.dynamic_slice_in_dim(send, (at % copies) * share, share, 1)
    got = swap(send).reshape(groups, seq_count * cap, own)
    slot_rows = seq_count * cap
    if own % 128 != 0:
        att = got.transpose(1, 0, 2).reshape(1, slot_rows, width)
    else:
        att = got
    part = width // batch_count
    d_att, branch, sums_two, expert_in, mid, active = expert(
        att, xs.reshape(slot_rows, width), grads, w_out, gains, biases, w_in, d_active
    )
    free = part // seq_count if seq_count == len(WALK) else 0
    back = expert_made(active, w_exp_out, mid, branch, seq_count, free)
    if own % 128 != 0:
        d_att = d_att.reshape(slot_rows, groups, own).transpose(1, 0, 2)
    if copies > 1:
        d_att = jnp.repeat(d_att, copies, axis=0)
    d_att = swap(d_att).reshape(experts, seq_count, cap, own)


    all_grads = gather_batch(after(grads, att), batch_count)
    ranks = row ^ jnp.asarray((1, 3, 0, 2), jnp.int32)
    out_terms = sum_batch(*out_weights(ranks, after(att, all_grads[1]), branch), batch_count)
    out_far = after(out_terms[2], back)
    all_rows = gather_batch(after(expert_in, out_far), batch_count)
    if seq_count == len(WALK):
        back = join_sum(*out_terms[:2], out_far, back)
    else:
        d_out = lax.psum(sum_of(*out_terms).astype(BF16), "seq").astype(F32)
    back = swap(after(back, d_att))

    d_att = after(d_att, out_far)
    d_qkv = (attend_back_long if long_rows else attend_back)(qkv, slots, d_att, att_out, lse, ends, cap)
    d_qkv = after(d_qkv, all_rows[1])

    per_row = 3 * groups // batch_count
    blocks = (ranks * per_row - group + groups - 1) // groups
    fits = (blocks < 3) & (blocks * groups + group < (ranks + 1) * per_row)
    pick = jnp.concatenate([ranks, jnp.minimum(blocks, 2), fits.astype(jnp.int32)]).astype(jnp.int32)
    send, keep = qkv_weights(pick, unit, d_qkv, w_own, gains, biases, sums_two)
    got = lax.ppermute(send, "batch", flip_pairs(batch_count, 1))
    output, d_mid = place_back(own_slots, back, cap)

    d_weights = ()

    def weights_call(call, *others):
        nonlocal d_weights
        first = after(all_rows[0], *others)
        d_weights = expert_weights(
            (first, *all_rows[1:]), all_grads, w_in, w_exp_out, row, call, tuple(d_weights)
        )
        return d_weights[:1]

    theirs = add_theirs(keep, got)
    terms = keep, got, lax.ppermute(theirs, "batch", flip_pairs(batch_count, 2))
    own_grad = swap(after(d_qkv, back, terms[2]))
    own_grad = own_grad.reshape(groups, copies, tok, 3 * own)[:, 0]
    if own % 128 != 0:
        own_grad = own_grad.reshape(groups, tok, 3, own).transpose(1, 2, 0, 3).reshape(1, tok, 3 * width)
    d_tokens = finish(x, own_grad, w_qkv, gains, d_mid)

    if seq_count == len(WALK):
        load = bundle(*terms, back)
        calls = iter(range(4))

        def weights_between():
            call = next(calls)
            if call == 0:
                return ()
            if call == 1:
                return (*weights_call(0, *load), d_mid)
            return (d_tokens,) if call == 2 else ()

        froms = [part for step in gather_steps(load, weights_between) for block in step for part in block]
        place = jnp.concatenate([(order - row * per_row) % groups, order])
        d_w_qkv, d_w_out, d_gains, d_biases = columns(froms, place, send.shape[1], width, part)
    else:
        mine = sum_of(*terms).astype(BF16)
        gathered = lax.all_gather(mine, "seq")
        d_w_out = d_out
        for call in range(WEIGHT_CALLS):
            weights_call(call)
        picked = (row * per_row + jnp.arange(per_row, dtype=jnp.int32)) % groups * copies
        cols = jnp.take(gathered[:, :width], picked, axis=0)
        d_w_qkv = cols.transpose(1, 0, 2).reshape(width, per_row * own).astype(F32)
        norms = jnp.sum(gathered[:, width:].astype(F32), axis=0)
        norms = norms.reshape(-1, 8, 128)[:, :4].transpose(1, 0, 2).reshape(4, part)
        d_gains, d_biases = norms[:2], norms[2:]
    return output, d_tokens, d_w_qkv, d_w_out, *d_weights, d_gains, d_biases


def solution(mesh):
    return jax.shard_map(
        on_device,
        mesh=mesh,
        in_specs=(
            P("batch", "seq", None),
            P(),
            P(),
            P("seq", None, None),
            P("seq", None, None),
            P(),
            P(),
            P("batch", None),
            P("batch", "seq", None),
            P("batch", "seq", None),
        ),
        out_specs=(
            P("batch", "seq", None),
            P("batch", "seq", None),
            P(None, "batch"),
            P(None, "batch"),
            P("seq", None, "batch"),
            P("seq", "batch", None),
            P(None, "batch"),
            P(None, "batch"),
        ),
        check_vma=False,
    )
```

```python
import functools
import math

import jax
import jax.numpy as jnp
from jax import lax
from jax.experimental import pallas as pl
from jax.experimental.pallas import tpu as pltpu
from jax.sharding import PartitionSpec as P

HEADS = 16
HEAD_DIM = 64
NORM_EPS = 1e-05
MASKED = -1e30
LOG2E = 1.4426950408889634
F32 = jnp.float32
BF16 = jnp.bfloat16
VMEM_BYTES = 56 * 1024 * 1024


def dot(a, b, ca=1, cb=0):
    return lax.dot_general(a, b, (((ca,), (cb,)), ((), ())), preferred_element_type=F32)


def cost(time_us):
    return pl.CostEstimate(flops=int(time_us * 1e9), bytes_accessed=int(time_us * 3e6), transcendentals=0)


def params():
    return pltpu.CompilerParams(vmem_limit_bytes=VMEM_BYTES)


def shape(dims, kind):
    return jax.ShapeDtypeStruct(dims, kind)


def norm_parts(rows):
    row_mean = jnp.mean(rows, axis=-1, keepdims=True)
    centred = rows - row_mean
    row_var = jnp.mean(centred * centred, axis=-1, keepdims=True)
    inv_std = lax.rsqrt(row_var + NORM_EPS)
    return centred * inv_std, inv_std


def norm_back(scaled, unit_rows, inv_std):
    centred = scaled - jnp.mean(scaled, axis=-1, keepdims=True)
    centred = centred - unit_rows * jnp.mean(scaled * unit_rows, axis=-1, keepdims=True)
    return centred * inv_std


def gelu_both(pre):
    cdf = 0.5 + 0.5 * lax.erf(pre * 0.7071067811865476)
    density = jnp.exp(-0.5 * pre * pre) * 0.3989422804014327
    return pre * cdf, cdf + pre * density


def whole(array):
    rank = len(array.shape)
    return pl.BlockSpec(array.shape, lambda *unused: (0,) * rank)


def slots_of(ids_row, experts, cap):
    count = ids_row.shape[1]
    members = (lax.broadcasted_iota(jnp.int32, (experts, count), 0) == ids_row).astype(F32)
    order = lax.broadcasted_iota(jnp.int32, (count, count), 0) <= lax.broadcasted_iota(
        jnp.int32, (count, count), 1
    )
    ranks = dot(members.astype(BF16), order.astype(BF16))
    rank = jnp.sum(members * ranks, axis=0, keepdims=True).astype(jnp.int32) - 1
    return ids_row * cap + rank


def pick_rows(slot_row, count, first=0):
    rows = lax.broadcasted_iota(jnp.int32, (count, slot_row.shape[1]), 0) + first
    return (rows == slot_row).astype(BF16)


def place_rows(slot_row, count):
    tokens = slot_row.shape[1]
    column = jnp.broadcast_to(slot_row.astype(F32), (128, tokens)).T[:, :1]
    return (lax.broadcasted_iota(jnp.int32, (tokens, count), 1).astype(F32) == column).astype(BF16)


def qkv_kernel(experts, cap, first, count, place, *refs):
    w_ref, gain_ref, bias_ref = refs[2 * count : 2 * count + 3]
    qkv_ref, unit_ref, xs_ref, slot_ref = refs[-4:]
    own_expert = place[0]

    def run(x_ref, y_ref):
        x = jnp.concatenate([x_ref[...], y_ref[:-16]], axis=0)
        tok = x.shape[0]
        unit, unused = norm_parts(x.astype(F32))
        normed = (unit * gain_ref[0:1] + bias_ref[0:1]).astype(BF16)
        qkv_ref[0] = dot(normed, w_ref[...]).astype(BF16)
        unit_ref[0] = unit.T.astype(BF16)
        ids = y_ref[-16:][:1, :tok].astype(F32).astype(jnp.int32)
        slot = slots_of(ids, experts, cap)
        slot_ref[0] = jnp.broadcast_to(slot, (8, tok))
        xs_ref[0] = dot(pick_rows(slot, cap, own_expert * cap), x).astype(BF16)

    for n in range(count):
        pl.when(pl.program_id(0) == n)(functools.partial(run, refs[2 * n], refs[2 * n + 1]))


def qkv_step(shards, first, places, held, w_own, gains, biases, seq_count, experts, cap):
    count = len(shards)
    width = shards[0][0].shape[1]
    tok = shards[0][0].shape[0] + shards[0][1].shape[0] - 16
    wide = w_own.shape[1]
    outs = [
        shape((seq_count, tok, wide), BF16),
        shape((seq_count, width, tok), BF16),
        shape((seq_count, cap, width), BF16),
        shape((seq_count, 8, tok), jnp.int32),
    ]
    parts = [part for shard in shards for part in shard]
    spec = pltpu.PrefetchScalarGridSpec(
        num_scalar_prefetch=1,
        grid=(count,),
        in_specs=[whole(a) for a in (*parts, w_own, gains, biases)]
        + [pl.BlockSpec(memory_space=pl.ANY)] * len(held),
        out_specs=[
            pl.BlockSpec((1,) + out.shape[1:], lambda i, at: (at[first + i], 0, 0)) for out in outs
        ],
    )
    return pl.pallas_call(
        functools.partial(qkv_kernel, experts, cap, first, count),
        out_shape=outs,
        grid_spec=spec,
        input_output_aliases={4 + len(parts) + n: n for n in range(len(held))},
        compiler_params=params(),
        name="qkv_step",
        cost_estimate=cost(4 * count),
    )(places, *parts, w_own, gains, biases, *held)


def send_kernel(experts, cap, ids_ref, rows_ref, out_ref, slot_ref):
    slot = slots_of(ids_ref[0:1], experts, cap)
    slot_ref[...] = jnp.broadcast_to(slot, slot_ref.shape)
    out_ref[...] = dot(pick_rows(slot, experts * cap), rows_ref[...]).astype(BF16)


def send_rows(ids_row, rows, experts, cap):
    tok, width = rows.shape
    return pl.pallas_call(
        functools.partial(send_kernel, experts, cap),
        out_shape=[shape((experts * cap, width), BF16), shape((8, tok), jnp.int32)],
        compiler_params=params(),
        name="send_rows",
        cost_estimate=cost(3),
    )(jnp.broadcast_to(ids_row, (8, tok)), rows)


def doc_start(ends_ref, positions, docs):
    start = jnp.zeros_like(positions)
    for k in range(docs):
        start = jnp.where(ends_ref[k] <= positions, ends_ref[k], start)
    return start


def head_lanes(array, head):
    lane = lax.broadcasted_iota(jnp.int32, (1, array.shape[1]), 1)
    return jnp.where(lane // HEAD_DIM == head, array, jnp.zeros_like(array))


def attend_kernel(docs, cap, ends_ref, qkv_ref, slot_ref, send_ref, out_ref, lse_ref):
    blocks, tok, wide = qkv_ref.shape
    width = wide // 3
    heads = width // HEAD_DIM
    experts = send_ref.shape[0]
    scale = LOG2E / math.sqrt(HEAD_DIM)
    lane = lax.broadcasted_iota(jnp.int32, (tok, width), 1)

    def run(block):
        q = qkv_ref[block, :, :width]
        local = lax.broadcasted_iota(jnp.int32, (tok, 1), 0)
        start = doc_start(ends_ref, block * tok + local, docs)
        ones = jnp.ones((tok, width), BF16)
        merged = jnp.zeros((tok, width), F32)
        lse = jnp.zeros((tok, width), F32)
        for head in range(heads):
            q_head = head_lanes(q, head)
            parts = []
            for other in range(block + 1):
                s = dot(q_head, qkv_ref[other, :, width : 2 * width], 1, 1)
                column = lax.broadcasted_iota(jnp.int32, (tok, tok), 1)
                if other == block:
                    mask = (column <= local) & (column + other * tok >= start)
                    s = jnp.where(mask, s, MASKED)
                elif other == 0 or block == blocks - 1:
                    s = jnp.where(column + other * tok >= start, s, MASKED)
                parts.append(s)
            top = parts[0]
            for s in parts[1:]:
                top = jnp.maximum(top, s)
            top = jnp.max(top, axis=1, keepdims=True)
            shift = top * scale
            total = jnp.zeros((tok, 2 * width), F32)
            for other in range(block + 1):
                p = jnp.exp2(parts[other] * scale - shift).astype(BF16)
                v = jnp.concatenate([qkv_ref[other, :, 2 * width :], ones], axis=1)
                total = total + dot(p, v)
            weight = total[:, width:]
            mine = lane // HEAD_DIM == head
            merged = jnp.where(mine, total[:, :width] / weight, merged)
            lse = jnp.where(lane == head, shift + jnp.log2(weight), lse)
        out_ref[block] = merged
        lse_ref[block] = lse.T[:8]
        pick = pick_rows(slot_ref[block, 0:1], experts * cap)
        rows = dot(pick, merged.astype(BF16)).astype(BF16)
        for e in range(experts):
            send_ref[e, block] = rows[e * cap : (e + 1) * cap]

    for block in range(blocks):
        run(block)


def attend(qkv, slots, ends, cap):
    blocks, tok, wide = qkv.shape
    width = wide // 3
    return pl.pallas_call(
        functools.partial(attend_kernel, ends.shape[0], cap),
        out_shape=[
            shape((blocks, blocks, cap, width), BF16),
            shape((blocks, tok, width), F32),
            shape((blocks, 8, tok), F32),
        ],
        in_specs=[pl.BlockSpec(memory_space=pltpu.SMEM)]
        + [pl.BlockSpec(memory_space=pltpu.VMEM)] * 2,
        compiler_params=params(),
        name="attend",
        cost_estimate=cost(12),
    )(ends, qkv, slots)


def attend_back_kernel(
    docs, cap, ends_ref, qkv_ref, slot_ref, back_ref, out_ref, lse_ref, grad_ref, do_ref, dq_ref, delta_ref
):
    blocks, tok, wide = qkv_ref.shape
    width = wide // 3
    heads = width // HEAD_DIM
    experts = back_ref.shape[0]
    scale = LOG2E / math.sqrt(HEAD_DIM)

    for t in range(blocks):
        rows = jnp.concatenate([back_ref[e, t] for e in range(experts)], axis=0)
        do = dot(place_rows(slot_ref[t, 0:1], experts * cap), rows)
        do_ref[t] = do.astype(BF16)
        product = (do * out_ref[t]).T
        delta = jnp.zeros((8, tok), F32)
        row = lax.broadcasted_iota(jnp.int32, (8, tok), 0)
        for head in range(heads):
            part = product[head * HEAD_DIM : (head + 1) * HEAD_DIM]
            delta = jnp.where(row == head, jnp.sum(part, axis=0, keepdims=True), delta)
        delta_ref[t] = delta
        dq_ref[t] = jnp.zeros((tok, width), F32)

    def run(block):
        k = qkv_ref[block, :, width : 2 * width]
        v = qkv_ref[block, :, 2 * width :]
        k_pos = lax.broadcasted_iota(jnp.int32, (tok, tok), 0) + block * tok
        dk = jnp.zeros((tok, width), F32)
        dv = jnp.zeros((tok, width), F32)
        for other in range(block, blocks):
            q_pos = lax.broadcasted_iota(jnp.int32, (1, tok), 1) + other * tok
            start = doc_start(ends_ref, q_pos, docs)
            q = qkv_ref[other, :, :width]
            do = do_ref[other]
            dq = dq_ref[other]
            for head in range(heads):
                q_head = head_lanes(q, head)
                do_head = head_lanes(do, head)
                s = dot(k, q_head, 1, 1)
                p = jnp.exp2(s * scale - lse_ref[other, head : head + 1])
                if other == block:
                    p = jnp.where((k_pos <= q_pos) & (k_pos >= start), p, 0.0)
                elif block == 0 or other == blocks - 1:
                    p = jnp.where(k_pos >= start, p, 0.0)
                dp = dot(v, do_head, 1, 1)
                ds = (p * (dp - delta_ref[other, head : head + 1])).astype(BF16)
                dv = dv + dot(p.astype(BF16), do_head)
                dk = dk + dot(ds, q_head)
                dq = dq + dot(ds, head_lanes(k, head), 0, 0)
            dq_ref[other] = dq
        factor = 1.0 / math.sqrt(HEAD_DIM)
        for n, part in enumerate((dq_ref[block] * factor, dk * factor, dv)):
            columns = slice(n * width, (n + 1) * width)
            grad_ref[block, :, columns] = part.astype(BF16)

    for block in range(blocks):
        run(block)


def attend_back(qkv, slots, back, out, lse, ends, cap):
    blocks, tok, wide = qkv.shape
    width = wide // 3
    return pl.pallas_call(
        functools.partial(attend_back_kernel, ends.shape[0], cap),
        out_shape=shape((blocks, tok, wide), BF16),
        in_specs=[pl.BlockSpec(memory_space=pltpu.SMEM)]
        + [pl.BlockSpec(memory_space=pltpu.VMEM)] * 5,
        scratch_shapes=[
            pltpu.VMEM((blocks, tok, width), BF16),
            pltpu.VMEM((blocks, tok, width), F32),
            pltpu.VMEM((blocks, 8, tok), F32),
        ],
        compiler_params=params(),
        name="attend_back",
        cost_estimate=cost(20),
    )(ends, qkv, slots, back, out, lse)


def pick_all(slots, count):
    return (slots[:, :1, :] == jnp.arange(count, dtype=jnp.int32)[None, :, None]).astype(BF16)


def long_masks(ends, first, tok, length):
    q_pos = first + jnp.arange(tok, dtype=jnp.int32)
    k_pos = jnp.arange(length, dtype=jnp.int32)
    start = jnp.max(jnp.where(ends[None, :] <= q_pos[:, None], ends[None, :], 0), axis=1)
    return (k_pos[None, :] <= q_pos[:, None]) & (k_pos[None, :] >= start[:, None])


def long_heads(rows, width):
    return rows.reshape(rows.shape[0], width // HEAD_DIM, HEAD_DIM).transpose(1, 0, 2)


def attend_long(qkv, slots, ends, cap):
    blocks, tok, wide = qkv.shape
    width = wide // 3
    length = blocks * tok
    flat = qkv.reshape(length, wide)
    keys = long_heads(flat[:, width : 2 * width], width)
    values = long_heads(flat[:, 2 * width :], width)

    def one(block):
        query = long_heads(qkv[block, :, :width], width)
        mask = long_masks(ends, block * tok, tok, length)
        s = jnp.einsum("hqd,hkd->hqk", query, keys, preferred_element_type=F32)
        s = jnp.where(mask, s / math.sqrt(HEAD_DIM), MASKED)
        top = jnp.max(s, axis=-1, keepdims=True)
        weights = jnp.where(mask, jnp.exp(s - top), 0.0)
        total = jnp.sum(weights, axis=-1, keepdims=True)
        out = jnp.einsum("hqk,hkd->hqd", (weights / total).astype(BF16), values, preferred_element_type=F32)
        return out.transpose(1, 0, 2).reshape(tok, width), (top + jnp.log(total))[:, :, 0]

    out, lse = lax.map(one, jnp.arange(blocks, dtype=jnp.int32))
    pick = pick_all(slots, blocks * cap)
    rows = jnp.einsum("tsk,tkd->tsd", pick, out.astype(BF16), preferred_element_type=F32)
    send = rows.astype(BF16).reshape(blocks, blocks, cap, width).transpose(1, 0, 2, 3)
    return send, out, lse


def attend_back_long(qkv, slots, back, out, lse, ends, cap):
    blocks, tok, wide = qkv.shape
    width = wide // 3
    length = blocks * tok
    heads = width // HEAD_DIM
    flat = qkv.reshape(length, wide)
    keys = long_heads(flat[:, width : 2 * width], width)
    values = long_heads(flat[:, 2 * width :], width)
    pick = pick_all(slots, blocks * cap)
    rows = back.transpose(1, 0, 2, 3).reshape(blocks, blocks * cap, width)
    do_all = jnp.einsum("tsk,tsd->tkd", pick, rows, preferred_element_type=F32)

    def one(sums, block):
        query = long_heads(qkv[block, :, :width], width)
        mask = long_masks(ends, block * tok, tok, length)
        do = do_all[block]
        delta = jnp.sum((do * out[block]).reshape(tok, heads, HEAD_DIM), axis=-1).T
        do = long_heads(do.astype(BF16), width)
        s = jnp.einsum("hqd,hkd->hqk", query, keys, preferred_element_type=F32)
        p = jnp.where(mask, jnp.exp(s / math.sqrt(HEAD_DIM) - lse[block][:, :, None]), 0.0)
        dp = jnp.einsum("hqd,hkd->hqk", do, values, preferred_element_type=F32)
        ds = (p * (dp - delta[:, :, None]) / math.sqrt(HEAD_DIM)).astype(BF16)
        dq = jnp.einsum("hqk,hkd->qhd", ds, keys, preferred_element_type=F32)
        dk = jnp.einsum("hqk,hqd->khd", ds, query, preferred_element_type=F32)
        dv = jnp.einsum("hqk,hqd->khd", p.astype(BF16), do, preferred_element_type=F32)
        sums = (sums[0] + dk.reshape(length, width), sums[1] + dv.reshape(length, width))
        return sums, dq.reshape(tok, width)

    start = jnp.zeros((length, width), F32)
    (dk, dv), dq = lax.scan(one, (start, start), jnp.arange(blocks, dtype=jnp.int32))
    grad = jnp.concatenate([dq.reshape(length, width), dk, dv], axis=1).astype(BF16)
    return grad.reshape(blocks, tok, wide)


EXPERT_PART = 512


def active_kernel(g_ref, w2_ref, out_ref):
    out_ref[...] = dot(g_ref[...], w2_ref[0], 1, 1)


def expert_active(grads, w_exp_out):
    rows, wide = grads.shape
    hidden = w_exp_out.shape[1]
    return pl.pallas_call(
        active_kernel,
        out_shape=shape((rows, hidden), F32),
        grid=(hidden // EXPERT_PART,),
        in_specs=[whole(grads), pl.BlockSpec((1, EXPERT_PART, wide), lambda i: (0, i, 0))],
        out_specs=pl.BlockSpec((rows, EXPERT_PART), lambda i: (0, i)),
        compiler_params=params(),
        name="expert_active",
        cost_estimate=cost(5),
    )(grads, w_exp_out)


def expert_kernel(
    att_ref, xs_ref, g_ref, w_out_ref, gain_ref, bias_ref, w1_any, dact_any,
    datt_ref, branch_ref, sums_ref, ein_any, mid_any, active_any,
    w1_ref, dact_ref, ein_ref, mid_ref, active_ref, dpre_ref, in_sems, out_sems,
):
    groups, rows, width = att_ref.shape
    parts = [pl.ds(n, EXPERT_PART) for n in range(0, w1_ref.shape[1], EXPERT_PART)]
    loads = []
    for n, part in enumerate(parts):
        loads.append(
            (
                pltpu.make_async_copy(w1_any.at[0, :, part], w1_ref.at[:, part], in_sems.at[0, n]),
                pltpu.make_async_copy(dact_any.at[:, part], dact_ref.at[:, part], in_sems.at[1, n]),
            )
        )
        for load in loads[n]:
            load.start()
    stores = []

    def store(source, target):
        copy = pltpu.make_async_copy(source, target, out_sems.at[len(stores)])
        copy.start()
        stores.append(copy)

    att = jnp.concatenate([att_ref[n] for n in range(groups)], axis=1)
    mid = xs_ref[...].astype(F32) + dot(att, w_out_ref[...])
    mid_ref[...] = mid
    store(mid_ref, mid_any)
    unit, inv_std = norm_parts(mid)
    ein = (unit * gain_ref[1:2] + bias_ref[1:2]).astype(BF16)
    ein_ref[...] = ein
    store(ein_ref, ein_any)
    g = g_ref[...]
    for n, part in enumerate(parts):
        for load in loads[n]:
            load.wait()
        pre = dot(ein, w1_ref[:, part])
        active, slope = gelu_both(pre)
        active_ref[:, part] = active.astype(BF16)
        store(active_ref.at[:, part], active_any.at[:, part])
        dpre_ref[:, part] = (dact_ref[:, part] * slope).astype(BF16)
    d_in = dot(dpre_ref[...], w1_ref[...], 1, 1).astype(BF16).astype(F32)
    d_mid = g.astype(F32) + norm_back(d_in * gain_ref[1:2], unit, inv_std)
    branch = d_mid.astype(BF16)
    branch_ref[...] = branch
    d_att = dot(branch, w_out_ref[...], 1, 1).astype(BF16)
    for n in range(groups):
        datt_ref[n] = d_att[:, n * width : (n + 1) * width]
    sums_ref[...] = jnp.zeros_like(sums_ref)
    sums_ref[0:1] = jnp.sum(d_in * unit, axis=0, keepdims=True)
    sums_ref[1:2] = jnp.sum(d_in, axis=0, keepdims=True)
    for copy in stores:
        copy.wait()


def expert(att, xs, grads, w_out, gains, biases, w_in, d_active):
    groups, rows, width = att.shape
    wide = xs.shape[1]
    hidden = w_in.shape[2]
    count = hidden // EXPERT_PART
    vmem = pl.BlockSpec(memory_space=pltpu.VMEM)
    hbm = pl.BlockSpec(memory_space=pl.ANY)
    return pl.pallas_call(
        expert_kernel,
        out_shape=[
            shape(att.shape, BF16),
            shape((rows, wide), BF16),
            shape((8, wide), F32),
            shape((rows, wide), BF16),
            shape((rows, wide), F32),
            shape((rows, hidden), BF16),
        ],
        in_specs=[vmem] * 6 + [hbm] * 2,
        out_specs=[vmem] * 3 + [hbm] * 3,
        scratch_shapes=[
            pltpu.VMEM((wide, hidden), BF16),
            pltpu.VMEM((rows, hidden), F32),
            pltpu.VMEM((rows, wide), BF16),
            pltpu.VMEM((rows, wide), F32),
            pltpu.VMEM((rows, hidden), BF16),
            pltpu.VMEM((rows, hidden), BF16),
            pltpu.SemaphoreType.DMA((2, count)),
            pltpu.SemaphoreType.DMA((count + 2,)),
        ],
        compiler_params=params(),
        name="expert",
        cost_estimate=cost(18),
    )(att, xs, grads, w_out, gains, biases, w_in, d_active)


def made_kernel(active_ref, w2_ref, mid_ref, branch_ref, back_ref, sum_ref):
    step = pl.program_id(0)
    term = dot(active_ref[...], w2_ref[0])

    @pl.when(step == 0)
    def first():
        sum_ref[...] = term

    @pl.when(step > 0)
    def later():
        sum_ref[...] += term

    @pl.when(step == pl.num_programs(0) - 1)
    def last():
        made = (mid_ref[...] + sum_ref[...].astype(BF16).astype(F32)).astype(BF16)
        seq_count = back_ref.shape[0]
        cap = made.shape[0] // seq_count
        for t in range(seq_count):
            back_ref[t, :cap] = made[t * cap : (t + 1) * cap]
            back_ref[t, cap : 2 * cap] = branch_ref[t * cap : (t + 1) * cap]


def expert_made(active, w_exp_out, mid, branch, seq_count, free):
    rows, hidden = active.shape
    wide = mid.shape[1]
    part = 1024
    out = shape((seq_count, 2 * rows // seq_count + free, wide), BF16)
    return pl.pallas_call(
        made_kernel,
        out_shape=out,
        grid=(hidden // part,),
        in_specs=[
            pl.BlockSpec((rows, part), lambda i: (0, i)),
            pl.BlockSpec((1, part, wide), lambda i: (0, i, 0)),
            whole(mid),
            whole(branch),
        ],
        out_specs=whole(out),
        scratch_shapes=[pltpu.VMEM((rows, wide), F32)],
        compiler_params=params(),
        name="expert_made",
        cost_estimate=cost(0.2),
    )(active, w_exp_out, mid, branch)


def weights_kernel(count, place, *refs):
    xs, gs = refs[:count], refs[count : 2 * count]
    w1_ref, w2_ref = refs[2 * count : 2 * count + 2]
    d1_ref, d2_ref, turned_ref = refs[-3:]

    @pl.when(pl.program_id(0) == 0)
    def begin():
        for n in range(count):
            turned_ref[n] = xs[n][...].T

    x = jnp.concatenate([xs[n][...] for n in range(count)], axis=0)
    g = jnp.concatenate([gs[n][...] for n in range(count)], axis=0)
    pre = dot(x, w1_ref[0])
    d_active = dot(g, w2_ref[0], 1, 1)
    active, slope = gelu_both(pre)
    turned = jnp.concatenate([turned_ref[n] for n in range(count)], axis=1)
    d1_ref[0] = dot(turned, (d_active * slope).astype(BF16))
    d2_ref[0] = dot(active.astype(BF16), g, 0, 0)


WEIGHT_CALLS = 1


def expert_weights(rows, grads, w_in, w_exp_out, place, call, held):
    parts = len(rows)
    count, wide = rows[0].shape
    hidden = w_in.shape[2] // parts
    part = 256
    steps = hidden // part
    share = steps // WEIGHT_CALLS
    first = call * share
    spec = pltpu.PrefetchScalarGridSpec(
        num_scalar_prefetch=1,
        grid=(share,),
        in_specs=[whole(a) for a in (*rows, *grads)]
        + [
            pl.BlockSpec((1, wide, part), lambda i, at: (0, 0, at[0] * steps + first + i)),
            pl.BlockSpec((1, part, wide), lambda i, at: (0, at[0] * steps + first + i, 0)),
        ]
        + [pl.BlockSpec(memory_space=pl.ANY)] * len(held),
        out_specs=[
            pl.BlockSpec((1, wide, part), lambda i, at: (0, 0, first + i)),
            pl.BlockSpec((1, part, wide), lambda i, at: (0, first + i, 0)),
        ],
        scratch_shapes=[pltpu.VMEM((parts, wide, count), BF16)],
    )
    return pl.pallas_call(
        functools.partial(weights_kernel, parts),
        out_shape=[shape((1, wide, hidden), F32), shape((1, hidden, wide), F32)],
        grid_spec=spec,
        input_output_aliases={3 + 2 * parts + n: n for n in range(len(held))},
        compiler_params=params(),
        name="expert_weights",
        cost_estimate=cost(0.5),
    )(place[None].astype(jnp.int32), *rows, *grads, w_in, w_exp_out, *held)


def out_weights_kernel(ranks_ref, att_ref, branch_ref, send_ref, keep_ref):
    groups = att_ref.shape[0]
    part = send_ref.shape[2]
    att = jnp.concatenate([att_ref[n] for n in range(groups)], axis=1)
    for n, (ref, slot) in enumerate(((send_ref, 0), (send_ref, 1), (keep_ref, 0), (keep_ref, 1))):
        columns = pl.ds(pl.multiple_of(ranks_ref[n] * part, part), part)
        ref[slot] = dot(att, branch_ref[:, columns], 0, 0).astype(BF16)


def out_weights(ranks, att, branch):
    wide = branch.shape[1]
    part = wide // 4
    return pl.pallas_call(
        out_weights_kernel,
        out_shape=[shape((2, wide, part), BF16)] * 2,
        in_specs=[pl.BlockSpec(memory_space=pltpu.SMEM)]
        + [pl.BlockSpec(memory_space=pltpu.VMEM)] * 2,
        compiler_params=params(),
        name="out_weights",
        cost_estimate=cost(1),
    )(ranks, att, branch)


def add_kernel(keep_ref, got_ref, out_ref):
    out_ref[...] = (keep_ref[1].astype(F32) + got_ref[1].astype(F32)).astype(BF16)


def add_theirs(keep, got):
    return pl.pallas_call(
        add_kernel,
        out_shape=shape(keep.shape[1:], BF16),
        in_specs=[pl.BlockSpec(memory_space=pltpu.VMEM)] * 2,
        compiler_params=params(),
        name="add_theirs",
        cost_estimate=cost(0.2),
    )(keep, got)


def sum_of(keep_ref, got_ref, far_ref):
    return keep_ref[0].astype(F32) + got_ref[0].astype(F32) + far_ref[...].astype(F32)


def join_kernel(keep_ref, got_ref, far_ref, back_ref, out_ref):
    total = sum_of(keep_ref, got_ref, far_ref).astype(BF16)
    count, lines, wide = out_ref.shape
    part = total.shape[1]
    folds = wide // part
    for t in range(count):
        for n in range(folds):
            at = (t * folds + n) * lines
            out_ref[t, :, n * part : (n + 1) * part] = total[at : at + lines]


def join_sum(keep, got, far, back):
    count, rows, wide = back.shape
    lines = far.shape[0] * far.shape[1] // (count * wide)
    return pl.pallas_call(
        join_kernel,
        out_shape=shape(back.shape, BF16),
        grid=(1,),
        in_specs=[whole(a) for a in (keep, got, far)] + [pl.BlockSpec(memory_space=pl.ANY)],
        out_specs=pl.BlockSpec((count, lines, wide), lambda i: (0, rows // lines - 1, 0)),
        input_output_aliases={3: 0},
        compiler_params=params(),
        name="join_sum",
        cost_estimate=cost(1),
    )(keep, got, far, back)


def qkv_weights_kernel(
    pick_ref, unit_ref, grad_ref, w_ref, gain_ref, bias_ref, two_ref, send_ref, keep_ref, cols_ref, sums_ref
):
    blocks = unit_ref.shape[0]
    parts, wide, width = cols_ref.shape
    grad = jnp.concatenate([grad_ref[t] for t in range(blocks)], axis=0)
    moment = dot(jnp.concatenate([unit_ref[t] for t in range(blocks)], axis=1), grad)
    total = jnp.sum(grad.astype(F32), axis=0, keepdims=True)
    gain = jnp.broadcast_to(gain_ref[0:1], (128, wide)).T[:, :1]
    bias = jnp.broadcast_to(bias_ref[0:1], (128, wide)).T[:, :1]
    made = moment * gain + bias * total
    for p in range(parts):
        cols_ref[p] = made[:, p * width : (p + 1) * width].astype(BF16)
    w = w_ref[...].astype(F32)
    d_gain = jnp.sum(w * moment, axis=1, keepdims=True)
    d_bias = jnp.sum(w * total, axis=1, keepdims=True)
    lane = lax.broadcasted_iota(jnp.int32, (wide, 128), 1)
    one = jnp.where(lane == 0, d_gain, jnp.where(lane == 1, d_bias, 0.0)).T[:8]
    row = lax.broadcasted_iota(jnp.int32, one.shape, 0)
    two = two_ref[...]
    all_sums = jnp.where(row == 0, one[0:1], jnp.where(row == 1, two[0:1], jnp.where(row == 2, one[1:2], two[1:2])))
    part = wide // 4
    for n in range(4):
        for line in range(part // 128):
            at = n * part + line * 128
            sums_ref[n, line] = all_sums[:, at : at + 128]
    for n, (ref, slot) in enumerate(((send_ref, 0), (send_ref, 1), (keep_ref, 0), (keep_ref, 1))):
        cols = cols_ref[pick_ref[4 + n]]
        ref[slot, :wide] = cols * pick_ref[8 + n].astype(F32).astype(BF16)
        lines = [sums_ref[pick_ref[n], line] for line in range(part // 128)]
        ref[slot, wide:] = jnp.concatenate(lines, axis=0).astype(BF16)


def qkv_weights(pick, unit, grad, w_own, gains, biases, sums_two):
    blocks, wide, tok = unit.shape
    width = w_own.shape[1] // 3
    lines = 8 * (wide // 4 // 128)
    outs = [shape((2, wide + lines, width), BF16)] * 2
    if width % 128 != 0:
        moment = jnp.einsum("tdk,tkf->df", unit, grad, preferred_element_type=F32)
        total = jnp.sum(grad.astype(F32), axis=(0, 1))
        made = moment * gains[0][:, None] + biases[0][:, None] * total[None, :]
        made = made.astype(BF16).reshape(wide, 3, width).transpose(1, 0, 2)
        w = w_own.astype(F32)
        copies = lax.axis_size("seq") * width // wide
        sums = jnp.stack(
            [
                jnp.sum(w * moment, axis=1) / copies,
                sums_two[0],
                jnp.sum(w * total[None, :], axis=1) / copies,
                sums_two[1],
            ]
        ).astype(BF16)
        terms = []
        for n in range(4):
            cols = made[pick[4 + n]] * pick[8 + n].astype(BF16)
            norms = lax.dynamic_slice_in_dim(sums, pick[n] * (wide // 4), wide // 4, 1)
            norms = norms.reshape(4, -1, 128).transpose(1, 0, 2)
            norms = jnp.pad(norms, ((0, 0), (0, 4), (0, 0))).reshape(-1, width)
            terms.append(jnp.concatenate([cols, norms], axis=0))
        return jnp.stack(terms[:2]), jnp.stack(terms[2:])
    return pl.pallas_call(
        qkv_weights_kernel,
        out_shape=outs,
        in_specs=[pl.BlockSpec(memory_space=pltpu.SMEM)]
        + [pl.BlockSpec(memory_space=pltpu.VMEM)] * 6,
        scratch_shapes=[
            pltpu.VMEM((3, wide, width), BF16),
            pltpu.VMEM((4, wide // 4 // 128, 8, 128), F32),
        ],
        compiler_params=params(),
        name="qkv_weights",
        cost_estimate=cost(4),
    )(pick, unit, grad, w_own, gains, biases, sums_two)


def bundle_kernel(keep_ref, got_ref, far_ref, back_ref, first_ref, out_ref):
    rows, width = far_ref.shape
    cut = first_ref.shape[0]
    made = sum_of(keep_ref, got_ref, far_ref).astype(BF16)
    first_ref[...] = made[:cut]
    rows = rows - cut
    out_ref[:rows] = made[cut:]
    count, lines, wide = back_ref.shape
    total = back_ref[0].astype(F32)
    for t in range(1, count):
        total = total + back_ref[t].astype(F32)
    total = total.astype(BF16)
    part = wide // 4
    for half in range(part // width):
        for n in range(4):
            at = rows + half * 4 * lines + n * lines
            first = n * part + half * width
            out_ref[at : at + lines] = total[:, first : first + width]


def bundle(keep, got, far, back):
    count, rows, wide = back.shape
    width = far.shape[1]
    lines = wide // 4 // count
    total = far.shape[0] + lines * wide // width
    outs = [shape((total // 32 * 16, width), BF16), shape((total - total // 32 * 16, width), BF16)]
    return pl.pallas_call(
        bundle_kernel,
        out_shape=outs,
        grid=(1,),
        in_specs=[whole(a) for a in (keep, got, far)]
        + [pl.BlockSpec((count, lines, wide), lambda i: (0, rows // lines - 1, 0))],
        out_specs=[whole(a) for a in outs],
        compiler_params=params(),
        name="bundle",
        cost_estimate=cost(1),
    )(keep, got, far, back)


def columns_kernel(rows, place, *refs):
    out_ref, d_out_ref, gain_ref, bias_ref = refs[-4:]
    froms = refs[:-4]
    count = len(froms) // 2
    wide = out_ref.shape[0]
    cut, width = froms[0].shape
    lines = wide // count
    total = jnp.zeros((rows - wide, width), F32)
    for n in range(count):
        head, tail = froms[2 * n : 2 * n + 2]

        @pl.when(place[n] < out_ref.shape[1] // width)
        def columns_of(n=n, head=head, tail=tail):
            first = pl.ds(pl.multiple_of(place[n] * width, width), width)
            out_ref[:cut, first] = head[...].astype(F32)
            out_ref[cut:, first] = tail[: wide - cut].astype(F32)

        total = total + tail[wide - cut : rows - cut].astype(F32)
        at = pl.ds(pl.multiple_of(place[count + n] * lines, lines), lines)
        for half in range(d_out_ref.shape[1] // width):
            first = rows - cut + half * lines
            d_out_ref[at, half * width : (half + 1) * width] = tail[first : first + lines].astype(F32)
    for line in range(gain_ref.shape[1] // width):
        gain_ref[:, line * width : (line + 1) * width] = total[line * 8 : line * 8 + 2]
        bias_ref[:, line * width : (line + 1) * width] = total[line * 8 + 2 : line * 8 + 4]


def columns(froms, place, rows, wide, part):
    width = froms[0].shape[1]
    return pl.pallas_call(
        functools.partial(columns_kernel, rows),
        out_shape=[
            shape((wide, 3 * part), F32),
            shape((wide, part), F32),
            shape((2, part), F32),
            shape((2, part), F32),
        ],
        in_specs=[pl.BlockSpec(memory_space=pltpu.SMEM)]
        + [pl.BlockSpec(memory_space=pltpu.VMEM)] * len(froms),
        compiler_params=params(),
        name="columns",
        cost_estimate=cost(0.2),
    )(place.astype(jnp.int32), *froms)


def place_kernel(cap, slot_ref, back_ref, out_ref, mid_ref):
    experts = back_ref.shape[0]
    place = place_rows(slot_ref[0:1], experts * cap)
    made = jnp.concatenate([back_ref[e, :cap] for e in range(experts)], axis=0)
    out_ref[0] = dot(place, made).astype(BF16)
    branch = jnp.concatenate([back_ref[e, cap : 2 * cap] for e in range(experts)], axis=0)
    mid_ref[...] = dot(place, branch).astype(BF16)


def place_back(slots, back, cap):
    tok, wide = slots.shape[1], back.shape[2]
    return pl.pallas_call(
        functools.partial(place_kernel, cap),
        out_shape=[shape((1, tok, wide), BF16), shape((tok, wide), BF16)],
        compiler_params=params(),
        name="place_back",
        cost_estimate=cost(0.5),
    )(slots, back)


def finish_kernel(x_ref, grad_ref, w_ref, gain_ref, mid_ref, dx_ref, sum_ref):
    step = pl.program_id(0)
    groups, tok, wide = grad_ref.shape
    width = wide // 3

    def part(p):
        at = p * width
        return jnp.concatenate([grad_ref[n, :, at : at + width] for n in range(groups)], axis=1)

    @pl.when(step == 0)
    def first():
        sum_ref[...] = dot(part(0), w_ref[...], 1, 1)

    @pl.when(step == 1)
    def second():
        sum_ref[...] += dot(part(1), w_ref[...], 1, 1)

    @pl.when(step == 2)
    def last():
        d_normed = sum_ref[...] + dot(part(2), w_ref[...], 1, 1)
        unit, inv_std = norm_parts(x_ref[...].astype(F32))
        dx_ref[0] = mid_ref[...].astype(F32) + norm_back(d_normed * gain_ref[0:1], unit, inv_std)


def finish(x, grad, w_qkv, gains, d_mid):
    tok, wide = x.shape
    out = shape((1, tok, wide), F32)
    return pl.pallas_call(
        finish_kernel,
        out_shape=out,
        grid=(3,),
        in_specs=[
            whole(x),
            whole(grad),
            pl.BlockSpec((wide, wide), lambda i: (0, i)),
            whole(gains),
            whole(d_mid),
        ],
        out_specs=whole(out),
        scratch_shapes=[pltpu.VMEM((tok, wide), F32)],
        compiler_params=params(),
        name="finish",
        cost_estimate=cost(0.5),
    )(x, grad, w_qkv, gains, d_mid)


WALK = (0, 2, 4, 6, 7, 5, 3, 1)


def walk_pairs(way):
    return [(WALK[n], WALK[(n + way) % len(WALK)]) for n in range(len(WALK))]


def walk_places(at):
    hops = (0, 1, -1, 2, -2, 3, -3, 4)
    table = [[0] * len(hops) for unused in WALK]
    for n, device in enumerate(WALK):
        table[device] = [WALK[(n - hop) % len(WALK)] for hop in hops]
    return jnp.asarray(table, jnp.int32)[at]


def gather_steps(own, done):
    ahead = behind = own
    yield [own]
    for unused in range(3):
        before = done()
        ahead, behind = [
            tuple(lax.ppermute(after(part, *before), "seq", walk_pairs(way)) for part in parts)
            for way, parts in ((1, ahead), (-1, behind))
        ]
        yield [ahead, behind]
    before = done()
    first = lax.ppermute(after(ahead[0], *before), "seq", walk_pairs(1))
    second = lax.ppermute(after(behind[1], *before), "seq", walk_pairs(-1))
    yield [(first, second)]


def after(value, *others):
    return lax.optimization_barrier((value,) + others)[0]


def swap(x):
    return lax.all_to_all(x, "seq", split_axis=0, concat_axis=0, tiled=True)


def flip_pairs(count, bit):
    return [(n, n ^ bit) for n in range(count)]


def gather_batch(own, count):
    far = lax.ppermute(own, "batch", flip_pairs(count, 2))
    near = lax.ppermute(own, "batch", flip_pairs(count, 1))
    return own, far, near, lax.ppermute(far, "batch", flip_pairs(count, 1))


def sum_batch(send, keep, count):
    got = lax.ppermute(send, "batch", flip_pairs(count, 1))
    far = lax.ppermute(add_theirs(keep, got), "batch", flip_pairs(count, 2))
    return keep, got, far


def on_device(tokens, w_qkv, w_out, w_in, w_exp_out, gains, biases, lengths, hash_ids, cotangent):
    tok, width = tokens.shape[1:]
    seq_count = lax.axis_size("seq")
    batch_count = lax.axis_size("batch")
    at = lax.axis_index("seq")
    row = lax.axis_index("batch")
    groups = min(HEADS, seq_count)
    copies = seq_count // groups
    group = at // copies
    own = width // groups
    experts = seq_count
    slot_cap = max(2, 3 * tok // (2 * experts))
    cap = -(-slot_cap // 16) * 16
    x = tokens[0]
    ends = jnp.cumsum(lengths[0]).astype(jnp.int32)
    ids_row = hash_ids[0, :, 0][None, :]

    ids_rows = jnp.broadcast_to(jnp.pad(ids_row.astype(BF16), ((0, 0), (0, width - tok))), (16, width))
    load = (x[: tok // 2], jnp.concatenate([x[tok // 2 :], ids_rows], axis=0))
    w_own = jnp.concatenate(
        [lax.dynamic_slice_in_dim(w_qkv, n * width + group * own, own, 1) for n in range(3)], axis=1
    )
    order = jnp.concatenate([at[None], jnp.arange(seq_count, dtype=jnp.int32)])
    grad_rows, own_slots = send_rows(ids_row, cotangent[0], experts, cap)
    held = ready = ()
    if seq_count == len(WALK):
        order = walk_places(at)
        seen = 0
        for shards in gather_steps(load, lambda: ready):
            ready = held[3:]
            held = qkv_step(shards, seen, order, held, w_own, gains, biases, seq_count, experts, cap)
            seen += len(shards)
        last = shards[0]
    else:
        last = [lax.all_gather(part, "seq") for part in load]
        for n in range(seq_count):
            shards = [(last[0][n], last[1][n])]
            held = qkv_step(shards, n + 1, order, held, w_own, gains, biases, seq_count, experts, cap)
    qkv, unit, xs, slots = held

    grad_rows = after(grad_rows, *last, *ready)
    grads = swap(grad_rows.reshape(experts, cap, width)).reshape(seq_count * cap, width)

    d_active = expert_active(grads, w_exp_out)
    long_rows = own % 128 != 0 or seq_count > 8
    send, att_out, lse = (attend_long if long_rows else attend)(qkv, slots, ends, cap)
    send = after(send, grads)
    share = seq_count // copies
    if copies > 1:
        send = lax.dynamic_slice_in_dim(send, (at % copies) * share, share, 1)
    got = swap(send).reshape(groups, seq_count * cap, own)
    slot_rows = seq_count * cap
    if own % 128 != 0:
        att = got.transpose(1, 0, 2).reshape(1, slot_rows, width)
    else:
        att = got
    part = width // batch_count
    d_att, branch, sums_two, expert_in, mid, active = expert(
        att, xs.reshape(slot_rows, width), grads, w_out, gains, biases, w_in, d_active
    )
    free = part // seq_count if seq_count == len(WALK) else 0
    back = expert_made(active, w_exp_out, mid, branch, seq_count, free)
    if own % 128 != 0:
        d_att = d_att.reshape(slot_rows, groups, own).transpose(1, 0, 2)
    if copies > 1:
        d_att = jnp.repeat(d_att, copies, axis=0)
    d_att = swap(d_att).reshape(experts, seq_count, cap, own)


    all_grads = gather_batch(after(grads, att), batch_count)
    ranks = row ^ jnp.asarray((1, 3, 0, 2), jnp.int32)
    out_terms = sum_batch(*out_weights(ranks, after(att, all_grads[1]), branch), batch_count)
    out_far = after(out_terms[2], back)
    all_rows = gather_batch(after(expert_in, out_far), batch_count)
    if seq_count == len(WALK):
        back = join_sum(*out_terms[:2], out_far, back)
    else:
        d_out = lax.psum(sum_of(*out_terms).astype(BF16), "seq").astype(F32)
    back = swap(after(back, d_att))

    d_att = after(d_att, out_far)
    d_qkv = (attend_back_long if long_rows else attend_back)(qkv, slots, d_att, att_out, lse, ends, cap)
    d_qkv = after(d_qkv, all_rows[1])

    per_row = 3 * groups // batch_count
    blocks = (ranks * per_row - group + groups - 1) // groups
    fits = (blocks < 3) & (blocks * groups + group < (ranks + 1) * per_row)
    pick = jnp.concatenate([ranks, jnp.minimum(blocks, 2), fits.astype(jnp.int32)]).astype(jnp.int32)
    send, keep = qkv_weights(pick, unit, d_qkv, w_own, gains, biases, sums_two)
    got = lax.ppermute(send, "batch", flip_pairs(batch_count, 1))
    output, d_mid = place_back(own_slots, back, cap)

    d_weights = ()

    def weights_call(call, *others):
        nonlocal d_weights
        first = after(all_rows[0], *others)
        d_weights = expert_weights(
            (first, *all_rows[1:]), all_grads, w_in, w_exp_out, row, call, tuple(d_weights)
        )
        return d_weights[:1]

    theirs = add_theirs(keep, got)
    terms = keep, got, lax.ppermute(theirs, "batch", flip_pairs(batch_count, 2))
    own_grad = swap(after(d_qkv, back, terms[2]))
    own_grad = own_grad.reshape(groups, copies, tok, 3 * own)[:, 0]
    if own % 128 != 0:
        own_grad = own_grad.reshape(groups, tok, 3, own).transpose(1, 2, 0, 3).reshape(1, tok, 3 * width)
    d_tokens = finish(x, own_grad, w_qkv, gains, d_mid)

    if seq_count == len(WALK):
        load = bundle(*terms, back)
        calls = iter(range(4))

        def weights_between():
            call = next(calls)
            if call == 0:
                return ()
            if call == 1:
                return (*weights_call(0, *load), d_mid)
            return (d_tokens,) if call == 3 else ()

        froms = [part for step in gather_steps(load, weights_between) for block in step for part in block]
        place = jnp.concatenate([(order - row * per_row) % groups, order])
        d_w_qkv, d_w_out, d_gains, d_biases = columns(froms, place, send.shape[1], width, part)
    else:
        mine = sum_of(*terms).astype(BF16)
        gathered = lax.all_gather(mine, "seq")
        d_w_out = d_out
        for call in range(WEIGHT_CALLS):
            weights_call(call)
        picked = (row * per_row + jnp.arange(per_row, dtype=jnp.int32)) % groups * copies
        cols = jnp.take(gathered[:, :width], picked, axis=0)
        d_w_qkv = cols.transpose(1, 0, 2).reshape(width, per_row * own).astype(F32)
        norms = jnp.sum(gathered[:, width:].astype(F32), axis=0)
        norms = norms.reshape(-1, 8, 128)[:, :4].transpose(1, 0, 2).reshape(4, part)
        d_gains, d_biases = norms[:2], norms[2:]
    return output, d_tokens, d_w_qkv, d_w_out, *d_weights, d_gains, d_biases


def solution(mesh):
    return jax.shard_map(
        on_device,
        mesh=mesh,
        in_specs=(
            P("batch", "seq", None),
            P(),
            P(),
            P("seq", None, None),
            P("seq", None, None),
            P(),
            P(),
            P("batch", None),
            P("batch", "seq", None),
            P("batch", "seq", None),
        ),
        out_specs=(
            P("batch", "seq", None),
            P("batch", "seq", None),
            P(None, "batch"),
            P(None, "batch"),
            P("seq", None, "batch"),
            P("seq", "batch", None),
            P(None, "batch"),
            P(None, "batch"),
        ),
        check_vma=False,
    )
```
